768 devices in a mesh: row: 4 (over y_lo, core), col: 192 (over y_hi, x, z).
Axes of the slice: x: 4, y: 8 (y_hi: 4, y_lo: 2; y = y_hi * 2 + y_lo), z: 12, core: 2. Of those that a mesh axis runs over, the one named last changes fastest.
Arguments:
- features: bfloat16 [98304, 128], P(('row', 'col')), may hold values from -6 to 6
- tile_rows: int32 [4, 192, 48], P('row', 'col'), may hold values from 0 to 7, as said below
- tile_cols: int32 [4, 192, 48], P('row', 'col'), may hold values from 0 to 191, as said below
- tile_counts: int32 [4, 192], P('row', 'col'), may hold values from 1 to 48, as said below
- tile_values: bfloat16 [4, 192, 48, 64, 128], P('row', 'col'), may hold values from 0 to 0.049804688
- weight: bfloat16 [128, 256], replicated, may hold values from -0.5 to 0.5
- bias: float32 [256], replicated, may hold values from -3 to 3
- cotangent: bfloat16 [98304, 256], P(('row', 'col')), may hold values from -6 to 6
Outputs:
- hidden_out: bfloat16 [98304, 256], P(('row', 'col'))
- features_grad: float32 [98304, 128], P(('row', 'col'))
- weight_grad: float32 [128, 256], replicated
- bias_grad: float32 [256], replicated
The draws below stay inside these ranges and needn't reach their ends.
Inputs may be any that keep to these rules, and one draw needn't show every extreme that they name: `tile_cols`: within each block the live slots (k < tile_counts) are ordered by tile column, then tile row; slots past the count hold 0. `tile_rows`: slots past the count hold 0. `tile_counts`: some block is full in every draw.
All inputs are finite; a program needn't handle non-finite values.
Results may differ from the reference program's by a relative error of at most 0.0075.
Values may be sent and summed in bfloat16 or wider, within the bound.
No kernel may reach another device: no remote copies, remote signals or barrier semaphores. Data moves between devices by JAX's collectives and lax.ppermute only.
A program may use at most 32 MiB of HBM per device.

```python
import math
import jax
import jax.numpy as jnp
from jax import lax

FEAT_IN = 128
HIDDEN_SIZE = 256
NODES_DEV = 128
TILE_ROWS = 64
TILE_COLS = 128
TILES = 48
NODES = 98304
ROW_TILES = 8
COL_TILES = 192
N_ROW = 4
N_COL = 192


def tile_layout(key):
    first, second, third, fourth, fifth = jax.random.split(key, 5)
    draw_a = jax.random.randint(first, (N_ROW, N_COL), 1, TILES + 1)
    draw_b = jax.random.randint(second, (N_ROW, N_COL), 1, TILES + 1)
    counts = jnp.minimum(draw_a, draw_b)
    chosen = jax.random.randint(third, (), 0, N_ROW * N_COL)
    flat_ids = jnp.arange(N_ROW * N_COL).reshape(N_ROW, N_COL)
    counts = jnp.where(flat_ids == chosen, TILES, counts).astype(jnp.int32)
    rows = jax.random.randint(fourth, (N_ROW, N_COL, TILES), 0, ROW_TILES)
    cols = jax.random.randint(fifth, (N_ROW, N_COL, TILES), 0, COL_TILES)
    slots = jnp.arange(TILES)[None, None, :]
    live = slots < counts[:, :, None]
    score = jnp.where(live, cols * ROW_TILES + rows, COL_TILES * ROW_TILES)
    ordered = jnp.sort(score, axis=-1)
    rows_out = jnp.where(live, ordered % ROW_TILES, 0).astype(jnp.int32)
    cols_out = jnp.where(live, ordered // ROW_TILES, 0).astype(jnp.int32)
    return (rows_out, cols_out, counts)


def draw_tile_rows(key, part):
    return tile_layout(key)[0]


def draw_tile_cols(key, part):
    return tile_layout(key)[1]


def draw_tile_counts(key, part):
    return tile_layout(key)[2]


def block_scale(key, dims, shards, least, top_value):
    loudness = 1.0
    for dim, blocks in shards:
        heights = jax.random.uniform(jax.random.fold_in(jax.random.fold_in(key, 6), dim), (blocks,), jnp.float32, least / len(shards), top_value / len(shards))
        loudness = loudness * jnp.repeat(jnp.exp(heights), dims[dim] // blocks).reshape((-1,) + (1,) * (len(dims) - 1 - dim))
    return loudness


def bell_draw(own_key, shape, deviation, reach, cuts=(), kind=jnp.bfloat16):
    result = deviation * jax.random.normal(own_key, shape, jnp.float32)
    if cuts:
        result = result * block_scale(own_key, shape, cuts, -0.22, 0.18)
    return jnp.clip(result, -reach, reach).astype(kind)


def setup_inputs(seed: int = 0) -> dict:
    arg_keys = jax.random.split(jax.random.key(seed), 9)
    return {
        "features": bell_draw(arg_keys[0], (NODES, FEAT_IN), 1.0, 6.0, ((0, 768),)),
        "tile_rows": draw_tile_rows(jax.random.fold_in(arg_keys[8], 71), 0),
        "tile_cols": draw_tile_cols(jax.random.fold_in(arg_keys[8], 71), 0),
        "tile_counts": draw_tile_counts(jax.random.fold_in(arg_keys[8], 71), 0),
        "tile_values": jnp.clip(0.049804688 * jax.random.uniform(arg_keys[4], (N_ROW, N_COL, TILES, TILE_ROWS, TILE_COLS), jnp.float32) ** block_scale(arg_keys[4], (N_ROW, N_COL, TILES, TILE_ROWS, TILE_COLS), ((0, 4), (1, 192)), -0.2, 0.2), 0.0, 0.049804688).astype(jnp.bfloat16),
        "weight": bell_draw(arg_keys[5], (FEAT_IN, HIDDEN_SIZE), FEAT_IN ** -0.5, 0.5),
        "bias": bell_draw(arg_keys[6], (HIDDEN_SIZE,), 0.5, 3.0, (), jnp.float32),
        "cotangent": bell_draw(arg_keys[7], (NODES, HIDDEN_SIZE), 1.0, 6.0, ((0, 768),)),
    }


def gelu_tanh(values):
    return jax.nn.gelu(values, approximate=True)

def reference(features, tile_rows, tile_cols, tile_counts, tile_values, weight, bias, cotangent):
    column_blocks = features.astype(jnp.float32).reshape(N_ROW, COL_TILES, TILE_COLS, FEAT_IN)
    slot_ids = jnp.arange(TILES, dtype=jnp.int32)

    def one_block(block_x, rows_b, cols_b, count_b, values_b):
        live = (slot_ids < count_b).astype(jnp.float32)
        slabs = block_x[cols_b]
        weighted = values_b.astype(jnp.float32) * live[:, None, None]
        products = jnp.einsum('tab,tbf->taf', weighted, slabs, precision=lax.Precision.HIGHEST)
        grouped = jnp.zeros((ROW_TILES, TILE_ROWS, FEAT_IN), jnp.float32).at[rows_b].add(products)
        return grouped.reshape(N_ROW * NODES_DEV, FEAT_IN)

    def one_group(column):
        parts = jax.vmap(one_block)(column_blocks, tile_rows[:, column], tile_cols[:, column], tile_counts[:, column], tile_values[:, column])
        return lax.optimization_barrier(jnp.sum(parts, axis=0))
    groups = lax.map(one_group, jnp.arange(N_COL, dtype=jnp.int32))
    aggregate = groups.reshape(N_COL, N_ROW, NODES_DEV, FEAT_IN).transpose(1, 0, 2, 3).reshape(NODES, FEAT_IN)
    pre = jnp.dot(aggregate, weight.astype(jnp.float32), precision=lax.Precision.HIGHEST) + bias
    activated, pullback = jax.vjp(gelu_tanh, pre)
    hidden_out = activated.astype(jnp.bfloat16)
    slope = pullback(cotangent.astype(jnp.float32))[0].astype(jnp.bfloat16)
    spread = lax.dot_general(slope, weight, (((1,), (1,)), ((), ())), preferred_element_type=jnp.float32).astype(jnp.bfloat16)
    spread_cols = spread.astype(jnp.float32).reshape(N_ROW, N_COL, NODES_DEV, FEAT_IN)

    def back_block(spread_c, rows_b, cols_b, count_b, values_b):
        live = (slot_ids < count_b).astype(jnp.float32)
        weighted = values_b.astype(jnp.float32) * live[:, None, None]
        picked = spread_c[rows_b]
        contrib = jnp.einsum('tab,taf->tbf', weighted, picked, precision=lax.Precision.HIGHEST)
        placed = jnp.zeros((COL_TILES, TILE_COLS, FEAT_IN), jnp.float32).at[cols_b].add(contrib)
        return placed.reshape(COL_TILES * TILE_COLS, FEAT_IN)

    def back_step(carry, column):
        spread_c = lax.dynamic_index_in_dim(spread_cols, column, 1, keepdims=False).reshape(ROW_TILES, TILE_ROWS, FEAT_IN)
        parts = jax.vmap(back_block, in_axes=(None, 0, 0, 0, 0))(spread_c, tile_rows[:, column], tile_cols[:, column], tile_counts[:, column], tile_values[:, column])
        return (carry + parts, None)
    start_cols = jnp.zeros((N_ROW, COL_TILES * TILE_COLS, FEAT_IN), jnp.float32)
    summed_cols, unused = lax.scan(back_step, start_cols, jnp.arange(N_COL, dtype=jnp.int32))
    features_grad = summed_cols.reshape(NODES, FEAT_IN)
    slope_wide = slope.astype(jnp.float32)
    factor = 1.0 / math.sqrt(NODES)
    weight_grad = jnp.dot(aggregate.T, slope_wide, precision=lax.Precision.HIGHEST) * factor
    bias_grad = lax.optimization_barrier(jnp.sum(slope_wide, axis=0)) * factor
    return (hidden_out, features_grad, weight_grad, bias_grad)
```

```python
import math

import jax
import jax.numpy as jnp
from jax import lax
from jax.experimental import pallas as pl
from jax.experimental.pallas import tpu as pltpu
from jax.sharding import Mesh, PartitionSpec as P

row_split = (2, 2)
col_split = (4, 4, 12)
axis_names = ("ylo", "core", "yhi", "x", "z")
row_axes = ("ylo", "core")
col_axes = ("yhi", "x", "z")
team_axes = ("ylo", "core", "x")
group = 4
lanes = 128
vmem_bytes = 32 * 1024 * 1024
root_two_over_pi = math.sqrt(2.0 / math.pi)
cubic = 0.044715


def spread_out(value, axes, count):
    copies = jnp.broadcast_to(value[None], (count,) + value.shape)
    return lax.all_to_all(copies, axes, 0, 0, tiled=True)


def pick_tiles(codes, counts, tile_refs, chosen, picked, slots, height, dummy):
    total = jnp.int32(0)
    for source, tiles in enumerate(tile_refs):

        def body(step, total, source=source, tiles=tiles):
            for sub in range(group):
                slot = step * group + sub
                code = codes[source * slots + slot]
                top = pl.multiple_of(slot * height, height)
                chosen[total] = tiles[pl.ds(top, height), :]
                picked[total] = code
                total = total + jnp.where(code >= 0, 1, 0)
            return total

        total = lax.fori_loop(0, (counts[source] + group - 1) // group, body, total)
    for sub in range(group):
        picked[total + sub] = dummy
    return total


def forward_kernel(codes, counts, slabs, *refs, slots, height, blocks):
    tile_refs = refs[: -4]
    out, chosen, totals, picked = refs[-4:]
    slab_count = slabs.shape[0]
    dummy = slab_count * 64 + blocks
    totals[...] = jnp.zeros_like(totals)
    total = pick_tiles(codes, counts, tile_refs, chosen, picked, slots, height, dummy)

    def body(step, carry):
        products = []
        for sub in range(group):
            code = picked[step * group + sub]
            slab = jnp.minimum(code >> 6, slab_count - 1)
            product = jnp.dot(
                chosen[step * group + sub], slabs[slab], preferred_element_type=jnp.float32
            )
            products.append((code & 63, product))
        for block, product in products:
            totals[block] += product
        return carry

    lax.fori_loop(0, (total + group - 1) // group, body, 0)
    halves = out.shape[1] // height
    for block in range(blocks):
        out[block // halves, pl.ds((block % halves) * height, height), :] = totals[block]


def split_wide(value):
    high = value.astype(jnp.bfloat16).astype(jnp.float32)
    return high, value - high


def bias_rows(pieces):
    rows = lax.broadcasted_iota(jnp.int32, (16, lanes), 0)
    block = jnp.zeros((16, lanes), jnp.float32)
    for index, piece in enumerate(pieces):
        block = jnp.where(rows == index, jnp.broadcast_to(piece, (16, lanes)), block)
    return block


def dense_kernel(partials, weight, bias, cotangent, hidden, message):
    members = partials.shape[0]
    nodes = partials.shape[1]
    aggregate = partials[0]
    for member in range(1, members):
        aggregate = aggregate + partials[member]
    weight_wide = weight[...].astype(jnp.float32)
    pre = (
        jnp.dot(
            aggregate,
            weight_wide,
            precision=lax.Precision.HIGHEST,
            preferred_element_type=jnp.float32,
        )
        + bias[...]
    )
    square = pre * pre
    angle = jnp.tanh(root_two_over_pi * (pre + cubic * (square * pre)))
    gate = 0.5 * (1.0 + angle)
    hidden[...] = (pre * gate).astype(jnp.bfloat16)
    inner = root_two_over_pi * (1.0 + 3.0 * cubic * square)
    gradient = gate + 0.5 * pre * (1.0 - angle * angle) * inner
    slope = (cotangent[...].astype(jnp.float32) * gradient).astype(jnp.bfloat16)
    slope_wide = slope.astype(jnp.float32)
    spread = lax.dot_general(
        slope, weight[...], (((1,), (1,)), ((), ())), preferred_element_type=jnp.float32
    ).astype(jnp.bfloat16)
    weight_part = lax.dot_general(
        aggregate,
        slope_wide,
        (((0,), (0,)), ((), ())),
        precision=lax.Precision.HIGHEST,
        preferred_element_type=jnp.float32,
    )
    bias_part = jnp.sum(slope_wide, axis=0, keepdims=True)
    high, low = split_wide(bias_part)
    bias_block = bias_rows([high[:, :lanes], high[:, lanes:], low[:, :lanes], low[:, lanes:]])
    bias_block = bias_block.astype(jnp.bfloat16)
    share = weight_part.shape[0] // members
    for member in range(members):
        message[member, pl.ds(0, nodes), :] = spread
        part = weight_part[member * share : (member + 1) * share]
        part = jnp.concatenate([part[:, :lanes], part[:, lanes:]], axis=0)
        high, low = split_wide(part)
        message[member, pl.ds(nodes, 2 * share), :] = high.astype(jnp.bfloat16)
        message[member, pl.ds(nodes + 2 * share, 2 * share), :] = low.astype(jnp.bfloat16)
        message[member, pl.ds(nodes + 4 * share, 16), :] = bias_block


def sum_rows(ref, start, size):
    value = ref[0, pl.ds(start, size), :].astype(jnp.float32)
    for index in range(1, ref.shape[0]):
        value = value + ref[index, pl.ds(start, size), :].astype(jnp.float32)
    return value


def sum_bias(ref, start):
    block = sum_rows(ref, start, 16)
    return [block[0:1] + block[2:3], block[1:2] + block[3:4]]


def pack_bias(values):
    parts = [split_wide(value) for value in values]
    return bias_rows([parts[0][0], parts[1][0], parts[0][1], parts[1][1]]).astype(jnp.bfloat16)


def backward_kernel(
    codes, counts, spreads, *refs, slots, height, blocks, nodes, share
):
    tile_refs = refs[: -4]
    out, chosen, totals, picked = refs[-4:]
    slab_count = totals.shape[0] - 1
    halves = nodes // height
    dummy = slab_count * 64 + blocks
    totals[...] = jnp.zeros_like(totals)
    total = pick_tiles(codes, counts, tile_refs, chosen, picked, slots, height, dummy)

    def body(step, carry):
        products = []
        for sub in range(group):
            code = picked[step * group + sub]
            block = jnp.minimum(code & 63, blocks - 1)
            top = pl.multiple_of((block % halves) * height, height)
            product = lax.dot_general(
                chosen[step * group + sub],
                spreads[block // halves, pl.ds(top, height), :],
                (((0,), (0,)), ((), ())),
                preferred_element_type=jnp.float32,
            )
            products.append((code >> 6, product))
        for slab, product in products:
            totals[slab] += product
        return carry

    lax.fori_loop(0, (total + group - 1) // group, body, 0)
    far = out.shape[0]
    near = slab_count // far
    width = totals.shape[1]
    for slab in range(slab_count):
        out[slab // near, pl.ds((slab % near) * width, width), :] = totals[slab].astype(
            jnp.bfloat16
        )
    weight_sum = sum_rows(spreads, nodes, 2 * share) + sum_rows(spreads, nodes + 2 * share, 2 * share)
    high, low = split_wide(weight_sum)
    bias_block = pack_bias(sum_bias(spreads, nodes + 4 * share))
    for index in range(far):
        out[index, pl.ds(near * width, 2 * share), :] = high.astype(jnp.bfloat16)
        out[index, pl.ds(near * width + 2 * share, 2 * share), :] = low.astype(jnp.bfloat16)
        out[index, pl.ds(near * width + 4 * share, 16), :] = bias_block


def middle_kernel(arrived, out, *, share):
    near = out.shape[0]
    rows = arrived.shape[1] - 4 * share - 16
    width = rows // near
    weight_sum = sum_rows(arrived, rows, 2 * share) + sum_rows(arrived, rows + 2 * share, 2 * share)
    bias_block = pack_bias(sum_bias(arrived, rows + 4 * share))
    for index in range(near):
        out[index, pl.ds(0, width), :] = sum_rows(arrived, index * width, width).astype(jnp.bfloat16)
        out[index, pl.ds(width, 2 * share), :] = weight_sum.astype(jnp.bfloat16)
        out[index, pl.ds(width + 2 * share, 16), :] = bias_block


def last_kernel(arrived, grad, weight_share, bias_grad, *, share, factor):
    width = grad.shape[0]
    grad[...] = sum_rows(arrived, 0, width)
    weight_share[...] = sum_rows(arrived, width, 2 * share) * factor
    low, high = sum_bias(arrived, width + 2 * share)
    bias_grad[:, pl.ds(0, lanes)] = low * factor
    bias_grad[:, pl.ds(lanes, lanes)] = high * factor


def in_vmem():
    return pl.BlockSpec(memory_space=pltpu.VMEM)


def in_smem():
    return pl.BlockSpec(memory_space=pltpu.SMEM)


def local(features, tile_rows, tile_cols, tile_counts, tile_values, weight, bias, cotangent):
    nodes, width = features.shape
    slots, height, tile_width = tile_values.shape[2:]
    hidden = weight.shape[1]
    far = lax.axis_size("yhi")
    across = lax.axis_size("x")
    near = lax.axis_size("z")
    members = lax.axis_size(team_axes)
    group_rows = lax.axis_size(row_axes)
    here = lax.axis_index("x")
    params = pltpu.CompilerParams(vmem_limit_bytes=vmem_bytes)

    live = jnp.arange(slots, dtype=jnp.int32) < tile_counts[0, 0]
    places = jnp.stack([tile_cols[0, 0], tile_rows[0, 0], live.astype(jnp.int32)])
    places = jnp.pad(places, ((0, 13), (0, lanes - slots))).astype(jnp.bfloat16)
    own = jnp.concatenate([tile_values[0, 0].reshape(slots * height, tile_width), places], axis=0)
    buffers = [own]
    for shift in range(1, across):
        hops = [(start, (start + shift) % across) for start in range(across)]
        buffers.append(lax.ppermute(own, "x", hops))

    line = spread_out(features, "z", near)
    slabs = spread_out(line, "yhi", far).reshape(far * near, nodes, width)

    halves = nodes // height
    blocks = members * halves
    tops = jnp.stack([buffer[slots * height :, :slots] for buffer in buffers]).astype(jnp.int32)
    columns, rows, alive = tops[:, 0], tops[:, 1], tops[:, 2]
    owner = (here - jnp.arange(across, dtype=jnp.int32)[:, None]) % across
    slab = (columns // (across * near)) * near + columns % near
    block = ((rows // halves) * across + owner) * halves + rows % halves
    mine = (alive > 0) & ((columns // near) % across == here)
    codes = jnp.where(mine, slab * 64 + block, -1).reshape(-1)
    counts = jnp.sum(alive, axis=1)

    scratch_tiles = pltpu.VMEM((across * slots + group, height, tile_width), jnp.bfloat16)
    scratch_list = pltpu.SMEM((across * slots + group,), jnp.int32)
    partial = pl.pallas_call(
        lambda *refs: forward_kernel(*refs, slots=slots, height=height, blocks=blocks),
        out_shape=jax.ShapeDtypeStruct((members, nodes, width), jnp.float32),
        in_specs=[in_smem(), in_smem(), in_vmem()] + [in_vmem()] * across,
        out_specs=in_vmem(),
        scratch_shapes=[
            scratch_tiles,
            pltpu.VMEM((blocks + 1, height, width), jnp.float32),
            scratch_list,
        ],
        compiler_params=params,
        name="forward_tiles",
    )(codes, counts, slabs, *buffers)
    partials = lax.all_to_all(partial, team_axes, 0, 0, tiled=True)

    share = width // members
    hidden_out, message = pl.pallas_call(
        dense_kernel,
        out_shape=(
            jax.ShapeDtypeStruct((nodes, hidden), jnp.bfloat16),
            jax.ShapeDtypeStruct((members, nodes + 4 * share + 16, width), jnp.bfloat16),
        ),
        in_specs=[in_vmem()] * 4,
        out_specs=(in_vmem(), in_vmem()),
        compiler_params=params,
        name="dense_layer",
    )(partials, weight, bias.reshape(1, hidden), cotangent)
    spreads = lax.all_to_all(message, team_axes, 0, 0, tiled=True)

    column_part = pl.pallas_call(
        lambda *refs: backward_kernel(
            *refs, slots=slots, height=height, blocks=blocks, nodes=nodes, share=share
        ),
        out_shape=jax.ShapeDtypeStruct((far, near * nodes + 4 * share + 16, width), jnp.bfloat16),
        in_specs=[in_smem(), in_smem(), in_vmem()] + [in_vmem()] * across,
        out_specs=in_vmem(),
        scratch_shapes=[
            scratch_tiles,
            pltpu.VMEM((far * near + 1, nodes, width), jnp.float32),
            scratch_list,
        ],
        compiler_params=params,
        name="backward_tiles",
    )(codes, counts, spreads, *buffers)
    arrived = lax.all_to_all(column_part, "yhi", 0, 0, tiled=True)
    line_part = pl.pallas_call(
        lambda *refs: middle_kernel(*refs, share=share),
        out_shape=jax.ShapeDtypeStruct((near, nodes + 2 * share + 16, width), jnp.bfloat16),
        in_specs=[in_vmem()],
        out_specs=in_vmem(),
        compiler_params=params,
        name="sum_far",
    )(arrived)
    arrived = lax.all_to_all(line_part, "z", 0, 0, tiled=True)
    factor = 1.0 / math.sqrt(nodes * group_rows * far * across * near)
    features_grad, weight_share, bias_grad = pl.pallas_call(
        lambda *refs: last_kernel(*refs, share=share, factor=factor),
        out_shape=(
            jax.ShapeDtypeStruct((nodes, width), jnp.float32),
            jax.ShapeDtypeStruct((2 * share, lanes), jnp.float32),
            jax.ShapeDtypeStruct((1, hidden), jnp.float32),
        ),
        in_specs=[in_vmem()],
        out_specs=(in_vmem(), in_vmem(), in_vmem()),
        compiler_params=params,
        name="sum_near",
    )(arrived)
    shares = spread_out(weight_share, team_axes, members)
    weight_grad = shares.reshape(members, 2, share, lanes).transpose(0, 2, 1, 3)
    weight_grad = weight_grad.reshape(width, hidden)
    return (hidden_out, features_grad, weight_grad, bias_grad.reshape(hidden))


def solution(mesh):
    fine = Mesh(mesh.devices.reshape(row_split + col_split), axis_names)
    nodes_spec = P(row_axes + col_axes, None)
    in_specs = (
        nodes_spec,
        P(row_axes, col_axes, None),
        P(row_axes, col_axes, None),
        P(row_axes, col_axes),
        P(row_axes, col_axes, None, None, None),
        P(),
        P(),
        nodes_spec,
    )
    out_specs = (nodes_spec, nodes_spec, P(), P())
    return jax.shard_map(local, mesh=fine, in_specs=in_specs, out_specs=out_specs, check_vma=False)
```

```python
import math

import jax
import jax.numpy as jnp
from jax import lax
from jax.experimental import pallas as pl
from jax.experimental.pallas import tpu as pltpu
from jax.sharding import Mesh, PartitionSpec as P

row_split = (2, 2)
col_split = (4, 4, 12)
axis_names = ("ylo", "core", "yhi", "x", "z")
row_axes = ("ylo", "core")
col_axes = ("yhi", "x", "z")
team_axes = ("ylo", "core", "x")
thirds = 3
group = 4
lanes = 128
vmem_bytes = 12 * 1024 * 1024
small_vmem_bytes = 2 * 1024 * 1024
root_two_over_pi = math.sqrt(2.0 / math.pi)
cubic = 0.044715


def spread_out(value, axes, count):
    copies = jnp.broadcast_to(value[None], (count,) + value.shape)
    return lax.all_to_all(copies, axes, 0, 0, tiled=True)


def pick_tiles(codes, tile_refs, chosen, picked, slots, height, dummy):
    total = jnp.int32(0)
    for source, tiles in enumerate(tile_refs):

        def body(step, total, source=source, tiles=tiles):
            for sub in range(group):
                slot = step * group + sub
                code = codes[source, slot]
                top = pl.multiple_of(slot * height, height)
                chosen[total] = tiles[pl.ds(top, height), :]
                picked[total] = code
                total = total + jnp.where(code >= 0, 1, 0)
            return total

        total = lax.fori_loop(0, (codes[source, slots] + group - 1) // group, body, total)
    for sub in range(group):
        picked[total + sub] = dummy
    return total


def forward_kernel(codes, slabs, *refs, slots, height, blocks):
    tile_refs = refs[: -4]
    out, chosen, totals, picked = refs[-4:]
    slab_count = slabs.shape[0]
    dummy = slab_count * 64 + blocks
    totals[...] = jnp.zeros_like(totals)
    total = pick_tiles(codes, tile_refs, chosen, picked, slots, height, dummy)

    def body(step, carry):
        products = []
        for sub in range(group):
            code = picked[step * group + sub]
            slab = jnp.minimum(code >> 6, slab_count - 1)
            product = jnp.dot(
                chosen[step * group + sub], slabs[slab], preferred_element_type=jnp.float32
            )
            products.append((code & 63, product))
        for block, product in products:
            totals[block] += product
        return carry

    lax.fori_loop(0, (total + group - 1) // group, body, 0)
    halves = out.shape[1] // height
    for block in range(blocks):
        out[block // halves, pl.ds((block % halves) * height, height), :] = totals[block].astype(
            jnp.bfloat16
        )


def split_wide(value):
    high = value.astype(jnp.bfloat16).astype(jnp.float32)
    return high, value - high


def bias_rows(pieces):
    rows = lax.broadcasted_iota(jnp.int32, (16, lanes), 0)
    block = jnp.zeros((16, lanes), jnp.float32)
    for index, piece in enumerate(pieces):
        block = jnp.where(rows == index, jnp.broadcast_to(piece, (16, lanes)), block)
    return block


def sum_rows(ref, start, size):
    value = ref[0, pl.ds(start, size), :].astype(jnp.float32)
    for index in range(1, ref.shape[0]):
        value = value + ref[index, pl.ds(start, size), :].astype(jnp.float32)
    return value


def dense_kernel(partials, weight, bias, cotangent, hidden, message):
    members = partials.shape[0]
    nodes = partials.shape[1]
    aggregate = sum_rows(partials, 0, nodes)
    weight_wide = weight[...].astype(jnp.float32)
    pre = (
        jnp.dot(
            aggregate,
            weight_wide,
            precision=lax.Precision.HIGHEST,
            preferred_element_type=jnp.float32,
        )
        + bias[...]
    )
    square = pre * pre
    angle = jnp.tanh(root_two_over_pi * (pre + cubic * (square * pre)))
    gate = 0.5 * (1.0 + angle)
    hidden[...] = (pre * gate).astype(jnp.bfloat16)
    inner = root_two_over_pi * (1.0 + 3.0 * cubic * square)
    gradient = gate + 0.5 * pre * (1.0 - angle * angle) * inner
    slope = (cotangent[...].astype(jnp.float32) * gradient).astype(jnp.bfloat16)
    slope_wide = slope.astype(jnp.float32)
    spread = lax.dot_general(
        slope, weight[...], (((1,), (1,)), ((), ())), preferred_element_type=jnp.float32
    ).astype(jnp.bfloat16)
    weight_part = lax.dot_general(
        aggregate,
        slope_wide,
        (((0,), (0,)), ((), ())),
        precision=lax.Precision.HIGHEST,
        preferred_element_type=jnp.float32,
    )
    bias_part = jnp.sum(slope_wide, axis=0, keepdims=True)
    high, low = split_wide(bias_part)
    bias_block = bias_rows([high[:, :lanes], high[:, lanes:], low[:, :lanes], low[:, lanes:]])
    bias_block = bias_block.astype(jnp.bfloat16)
    share = weight_part.shape[0] // members
    for member in range(members):
        message[member, pl.ds(0, nodes), :] = spread
        part = weight_part[member * share : (member + 1) * share]
        part = jnp.concatenate([part[:, :lanes], part[:, lanes:]], axis=0)
        high, low = split_wide(part)
        message[member, pl.ds(nodes, 2 * share), :] = high.astype(jnp.bfloat16)
        message[member, pl.ds(nodes + 2 * share, 2 * share), :] = low.astype(jnp.bfloat16)
        message[member, pl.ds(nodes + 4 * share, 16), :] = bias_block


def backward_kernel(codes, spreads, *refs, slots, height, blocks, nodes, share):
    tile_refs = refs[:-5]
    out, small, chosen, totals, picked = refs[-5:]
    slab_count = totals.shape[0] - 1
    halves = nodes // height
    dummy = slab_count * 64 + blocks
    totals[...] = jnp.zeros_like(totals)
    total = pick_tiles(codes, tile_refs, chosen, picked, slots, height, dummy)

    def body(step, carry):
        products = []
        for sub in range(group):
            code = picked[step * group + sub]
            block = jnp.minimum(code & 63, blocks - 1)
            top = pl.multiple_of((block % halves) * height, height)
            product = lax.dot_general(
                chosen[step * group + sub],
                spreads[block // halves, pl.ds(top, height), :],
                (((0,), (0,)), ((), ())),
                preferred_element_type=jnp.float32,
            )
            products.append((code >> 6, product))
        for slab, product in products:
            totals[slab] += product
        return carry

    lax.fori_loop(0, (total + group - 1) // group, body, 0)
    far = out.shape[0]
    near = slab_count // far
    width = totals.shape[1]
    for slab in range(slab_count):
        out[slab // near, pl.ds((slab % near) * width, width), :] = totals[slab].astype(
            jnp.bfloat16
        )
    small[pl.ds(0, 2 * share), :] = sum_rows(spreads, nodes, 2 * share) + sum_rows(
        spreads, nodes + 2 * share, 2 * share
    )
    block = sum_rows(spreads, nodes + 4 * share, 16)[0:8]
    small[pl.ds(2 * share, 8), :] = jnp.concatenate(
        [block[0:2] + block[2:4], jnp.zeros((6, lanes), jnp.float32)], axis=0
    )


def sum_kernel(arrived, unused, out):
    width = out.shape[1]
    for index in range(out.shape[0]):
        out[index] = sum_rows(arrived, index * width, width).astype(jnp.bfloat16)


def last_kernel(arrived, grad):
    grad[...] = sum_rows(arrived, 0, grad.shape[0])


def copies_kernel(value, *refs):
    out = refs[-1]
    for index in range(out.shape[0]):
        out[index] = value[...]


def ordered_kernel(place, *refs):
    stack, out = refs[-1], refs[-2]
    count = len(refs) - 2
    for shift in range(count):
        stack[lax.rem(place[0] - shift + count, count)] = refs[shift][...]
    total = stack[0]
    for index in range(1, count):
        total = total + stack[index]
    out[...] = total


def assemble_kernel(place, *refs, across, share, factor):
    out = refs[-1]
    for flip, shares in enumerate(refs[:-1]):
        row = place[0] ^ flip
        for shift in range(across):
            member = row * across + lax.rem(place[1] - shift + across, across)
            top = pl.multiple_of(member * share, share)
            out[pl.ds(top, share), pl.ds(0, lanes)] = shares[shift, pl.ds(0, share), :] * factor
            out[pl.ds(top, share), pl.ds(lanes, lanes)] = (
                shares[shift, pl.ds(share, share), :] * factor
            )


def in_vmem():
    return pl.BlockSpec(memory_space=pltpu.VMEM)


def in_smem():
    return pl.BlockSpec(memory_space=pltpu.SMEM)


def ordered_sum(value, axis, size, hops, place):
    pieces = [value] + [lax.ppermute(value, axis, hops(shift)) for shift in range(1, size)]
    return pl.pallas_call(
        ordered_kernel,
        out_shape=jax.ShapeDtypeStruct(value.shape, value.dtype),
        in_specs=[in_smem()] + [in_vmem()] * size,
        out_specs=in_vmem(),
        scratch_shapes=[pltpu.VMEM((size,) + value.shape, value.dtype)],
        compiler_params=pltpu.CompilerParams(vmem_limit_bytes=small_vmem_bytes),
        name="ordered_sum",
    )(place.reshape(1), *pieces)


def local(features, tile_rows, tile_cols, tile_counts, tile_values, weight, bias, cotangent):
    nodes, width = features.shape
    slots, height, tile_width = tile_values.shape[2:]
    hidden = weight.shape[1]
    far = lax.axis_size("yhi")
    across = lax.axis_size("x")
    near = lax.axis_size("z")
    members = lax.axis_size(team_axes)
    group_rows = lax.axis_size(row_axes)
    here = lax.axis_index("x")
    params = pltpu.CompilerParams(vmem_limit_bytes=vmem_bytes)
    halves = nodes // height
    blocks = members * halves

    def any_place():
        return pl.BlockSpec(memory_space=pl.ANY)

    live = jnp.arange(slots, dtype=jnp.int32) < tile_counts[0, 0]
    columns, rows = tile_cols[0, 0], tile_rows[0, 0]
    owner = jnp.where(live, (columns // near) % across, 255)
    slab = (columns // (across * near)) * near + columns % near
    block = ((rows // halves) * across + here) * halves + rows % halves
    places = jnp.stack([owner, slab, block])
    ends = jnp.stack([jnp.int32(254), jnp.int32(0), tile_counts[0, 0]])[:, None]
    places = jnp.concatenate([places, ends], axis=1)
    places = jnp.pad(places, ((0, 13), (0, lanes - slots - 1))).astype(jnp.bfloat16)
    own = jnp.concatenate([tile_values[0, 0].reshape(slots * height, tile_width), places], axis=0)

    up = [(start, (start + 1) % across) for start in range(across)]
    down = [(end, start) for start, end in up]
    buffers = [own, lax.ppermute(own, "x", up)]

    line = spread_out(features, "z", near).reshape(near * nodes, width)
    copies = pl.pallas_call(
        copies_kernel,
        out_shape=jax.ShapeDtypeStruct((far, near * nodes, width), jnp.bfloat16),
        in_specs=[in_vmem(), any_place()],
        out_specs=in_vmem(),
        compiler_params=params,
        name="line_copies",
    )(line, buffers[1])
    if across > 2:
        back = lax.ppermute(own, "x", down)
        for shift in range(2, across - 1):
            buffers.append(lax.ppermute(buffers[-1], "x", up))
        buffers.append(back)
    slabs = lax.all_to_all(copies, "yhi", 0, 0, tiled=True).reshape(far * near, nodes, width)

    tables = []
    for buffer in buffers:
        top = buffer[slots * height :].astype(jnp.int32)
        mine = (top[0] == here) | (top[0] == 254)
        tables.append(jnp.where(mine, top[1] * 64 + top[2], -1))
    codes = jnp.stack(tables)

    scratch_tiles = pltpu.VMEM((across * slots + group, height, tile_width), jnp.bfloat16)
    scratch_list = pltpu.SMEM((across * slots + group,), jnp.int32)
    partial = pl.pallas_call(
        lambda *refs: forward_kernel(*refs, slots=slots, height=height, blocks=blocks),
        out_shape=jax.ShapeDtypeStruct((members, nodes, width), jnp.bfloat16),
        in_specs=[in_smem(), in_vmem()] + [in_vmem()] * across,
        out_specs=in_vmem(),
        scratch_shapes=[
            scratch_tiles,
            pltpu.VMEM((blocks + 1, height, width), jnp.float32),
            scratch_list,
        ],
        compiler_params=params,
        name="forward_tiles",
    )(codes, slabs, *buffers)
    partials = lax.all_to_all(partial, team_axes, 0, 0, tiled=True)

    share = width // members
    hidden_out, message = pl.pallas_call(
        dense_kernel,
        out_shape=(
            jax.ShapeDtypeStruct((nodes, hidden), jnp.bfloat16),
            jax.ShapeDtypeStruct((members, nodes + 4 * share + 16, width), jnp.bfloat16),
        ),
        in_specs=[in_vmem()] * 4,
        out_specs=(in_vmem(), in_vmem()),
        compiler_params=params,
        name="dense_layer",
    )(partials, weight, bias.reshape(1, hidden), cotangent)
    spreads = lax.all_to_all(message, team_axes, 0, 0, tiled=True)

    column_part, small = pl.pallas_call(
        lambda *refs: backward_kernel(
            *refs, slots=slots, height=height, blocks=blocks, nodes=nodes, share=share
        ),
        out_shape=(
            jax.ShapeDtypeStruct((far, near * nodes, width), jnp.bfloat16),
            jax.ShapeDtypeStruct((2 * share + 8, lanes), jnp.float32),
        ),
        in_specs=[in_smem(), in_vmem()] + [in_vmem()] * across,
        out_specs=(in_vmem(), in_vmem()),
        scratch_shapes=[
            scratch_tiles,
            pltpu.VMEM((far * near + 1, nodes, width), jnp.float32),
            scratch_list,
        ],
        compiler_params=params,
        name="backward_tiles",
    )(codes, spreads, *buffers)
    def ring(size):
        return lambda shift: [(start, (start + shift) % size) for start in range(size)]

    depth = lax.axis_index("z")
    strip = near // thirds
    small = ordered_sum(small, "yhi", far, ring(far), lax.axis_index("yhi"))
    small = ordered_sum(
        small,
        "z",
        thirds,
        lambda shift: [(start, (start + shift * strip) % near) for start in range(near)],
        depth // strip,
    )
    small = ordered_sum(
        small,
        "z",
        strip,
        lambda shift: [
            (start, start // strip * strip + (start + shift) % strip) for start in range(near)
        ],
        depth % strip,
    )
    arrived = lax.all_to_all(column_part, "yhi", 0, 0, tiled=True)
    line_part = pl.pallas_call(
        sum_kernel,
        out_shape=jax.ShapeDtypeStruct((near, nodes, width), jnp.bfloat16),
        in_specs=[in_vmem(), any_place()],
        out_specs=in_vmem(),
        compiler_params=params,
        name="sum_far",
    )(arrived, small)
    arrived = lax.all_to_all(line_part, "z", 0, 0, tiled=True)
    features_grad = pl.pallas_call(
        last_kernel,
        out_shape=jax.ShapeDtypeStruct((nodes, width), jnp.float32),
        in_specs=[in_vmem()],
        out_specs=in_vmem(),
        compiler_params=params,
        name="sum_near",
    )(arrived)

    weight_share = small[: 2 * share]
    pieces = [weight_share]
    for shift in range(1, across):
        pieces.append(lax.ppermute(weight_share, "x", ring(across)(shift)))
    shares = jnp.stack(pieces)
    pieces = [shares]
    for flip in range(1, group_rows):
        pieces.append(
            lax.ppermute(shares, row_axes, [(start, start ^ flip) for start in range(group_rows)])
        )
    factor = 1.0 / math.sqrt(nodes * group_rows * far * across * near)
    place = jnp.stack([lax.axis_index(row_axes), here])
    weight_grad = pl.pallas_call(
        lambda *refs: assemble_kernel(*refs, across=across, share=share, factor=factor),
        out_shape=jax.ShapeDtypeStruct((width, hidden), jnp.float32),
        in_specs=[in_smem()] + [in_vmem()] * group_rows,
        out_specs=in_vmem(),
        compiler_params=pltpu.CompilerParams(vmem_limit_bytes=small_vmem_bytes),
        name="weight_grad",
    )(place, *pieces)
    bias_grad = small[2 * share : 2 * share + 2].reshape(hidden) * factor
    return (hidden_out, features_grad, weight_grad, bias_grad)


def solution(mesh):
    fine = Mesh(mesh.devices.reshape(row_split + col_split), axis_names)
    nodes_spec = P(row_axes + col_axes, None)
    in_specs = (
        nodes_spec,
        P(row_axes, col_axes, None),
        P(row_axes, col_axes, None),
        P(row_axes, col_axes),
        P(row_axes, col_axes, None, None, None),
        P(),
        P(),
        nodes_spec,
    )
    out_specs = (nodes_spec, nodes_spec, P(), P())
    return jax.shard_map(local, mesh=fine, in_specs=in_specs, out_specs=out_specs, check_vma=False)
```

```python
import math

import jax
import jax.numpy as jnp
from jax import lax
from jax.experimental import pallas as pl
from jax.experimental.pallas import tpu as pltpu
from jax.sharding import Mesh, PartitionSpec as P

row_split = (2, 2)
col_split = (4, 4, 12)
axis_names = ("ylo", "core", "yhi", "x", "z")
row_axes = ("ylo", "core")
col_axes = ("yhi", "x", "z")
team_axes = ("ylo", "core", "x")
ahead_rows = 80
back_rows = 96
group = 4
lanes = 128
vmem_bytes = 12 * 1024 * 1024
root_two_over_pi = math.sqrt(2.0 / math.pi)
cubic = 0.044715


def spread_out(value, axes, count):
    copies = jnp.broadcast_to(value[None], (count,) + value.shape)
    return lax.all_to_all(copies, axes, 0, 0, tiled=True)


def pick_tiles(codes, tile_refs, chosen, picked, slots, height, dummy):
    total = jnp.int32(0)
    for source, tiles in enumerate(tile_refs):

        def body(step, total, source=source, tiles=tiles):
            for sub in range(group):
                slot = step * group + sub
                code = codes[source, slot]
                top = pl.multiple_of(slot * height, height)
                chosen[total] = tiles[pl.ds(top, height), :]
                picked[total] = code
                total = total + jnp.where(code >= 0, 1, 0)
            return total

        total = lax.fori_loop(0, (codes[source, slots] + group - 1) // group, body, total)
    for sub in range(group):
        picked[total + sub] = dummy
    return total


def forward_kernel(codes, *refs, slots, height, blocks, far, across):
    lines, columns = refs[:far], refs[far]
    tile_refs = refs[far + 1 : far + 1 + across]
    out, slabs, chosen, totals, picked = refs[far + 1 + across :]
    slab_count, nodes = slabs.shape[:2]
    near = columns.shape[0]
    ahead = lines[0].shape[0] // near
    rest = nodes - ahead
    for shift in range(far):
        for index in range(near):
            slab = shift * near + index
            slabs[slab, pl.ds(0, ahead), :] = lines[shift][pl.ds(index * ahead, ahead), :]
            slabs[slab, pl.ds(ahead, rest), :] = columns[index, pl.ds(shift * rest, rest), :]
    dummy = slab_count * 64 + blocks
    totals[...] = jnp.zeros_like(totals)
    total = pick_tiles(codes, tile_refs, chosen, picked, slots, height, dummy)

    def body(step, carry):
        products = []
        for sub in range(group):
            code = picked[step * group + sub]
            slab = jnp.minimum(code >> 6, slab_count - 1)
            product = jnp.dot(
                chosen[step * group + sub], slabs[slab], preferred_element_type=jnp.float32
            )
            products.append((code & 63, product))
        for block, product in products:
            totals[block] += product
        return carry

    lax.fori_loop(0, (total + group - 1) // group, body, 0)
    halves = out.shape[1] // height
    for block in range(blocks):
        out[block // halves, pl.ds((block % halves) * height, height), :] = totals[block].astype(
            jnp.bfloat16
        )


def split_wide(value):
    high = value.astype(jnp.bfloat16).astype(jnp.float32)
    return high, value - high


def bias_rows(pieces):
    rows = lax.broadcasted_iota(jnp.int32, (16, lanes), 0)
    block = jnp.zeros((16, lanes), jnp.float32)
    for index, piece in enumerate(pieces):
        block = jnp.where(rows == index, jnp.broadcast_to(piece, (16, lanes)), block)
    return block


def sum_rows(ref, start, size):
    value = ref[0, pl.ds(start, size), :].astype(jnp.float32)
    for index in range(1, ref.shape[0]):
        value = value + ref[index, pl.ds(start, size), :].astype(jnp.float32)
    return value


def dense_kernel(partials, weight, bias, cotangent, hidden, message):
    members = partials.shape[0]
    nodes = partials.shape[1]
    aggregate = sum_rows(partials, 0, nodes)
    weight_wide = weight[...].astype(jnp.float32)
    pre = (
        jnp.dot(
            aggregate,
            weight_wide,
            precision=lax.Precision.HIGHEST,
            preferred_element_type=jnp.float32,
        )
        + bias[...]
    )
    square = pre * pre
    angle = jnp.tanh(root_two_over_pi * (pre + cubic * (square * pre)))
    gate = 0.5 * (1.0 + angle)
    hidden[...] = (pre * gate).astype(jnp.bfloat16)
    inner = root_two_over_pi * (1.0 + 3.0 * cubic * square)
    gradient = gate + 0.5 * pre * (1.0 - angle * angle) * inner
    slope = (cotangent[...].astype(jnp.float32) * gradient).astype(jnp.bfloat16)
    slope_wide = slope.astype(jnp.float32)
    spread = lax.dot_general(
        slope, weight[...], (((1,), (1,)), ((), ())), preferred_element_type=jnp.float32
    ).astype(jnp.bfloat16)
    weight_part = lax.dot_general(
        aggregate,
        slope_wide,
        (((0,), (0,)), ((), ())),
        precision=lax.Precision.HIGHEST,
        preferred_element_type=jnp.float32,
    )
    bias_part = jnp.sum(slope_wide, axis=0, keepdims=True)
    high, low = split_wide(bias_part)
    bias_block = bias_rows([high[:, :lanes], high[:, lanes:], low[:, :lanes], low[:, lanes:]])
    bias_block = bias_block.astype(jnp.bfloat16)
    share = weight_part.shape[0] // members
    for member in range(members):
        message[member, pl.ds(0, nodes), :] = spread
        part = weight_part[member * share : (member + 1) * share]
        part = jnp.concatenate([part[:, :lanes], part[:, lanes:]], axis=0)
        high, low = split_wide(part)
        message[member, pl.ds(nodes, 2 * share), :] = high.astype(jnp.bfloat16)
        message[member, pl.ds(nodes + 2 * share, 2 * share), :] = low.astype(jnp.bfloat16)
        message[member, pl.ds(nodes + 4 * share, 16), :] = bias_block


def sum_bias(ref, start):
    block = sum_rows(ref, start, 16)
    return [block[0:1] + block[2:3], block[1:2] + block[3:4]]


def pack_bias(values):
    parts = [split_wide(value) for value in values]
    return bias_rows([parts[0][0], parts[1][0], parts[0][1], parts[1][1]]).astype(jnp.bfloat16)


def backward_kernel(codes, spreads, *refs, slots, height, blocks, nodes, share, far, across):
    tile_refs, outs = refs[:across], refs[across : across + far]
    columns, chosen, totals, picked = refs[across + far :]
    slab_count = totals.shape[0] - 1
    halves = nodes // height
    dummy = slab_count * 64 + blocks
    totals[...] = jnp.zeros_like(totals)
    total = pick_tiles(codes, tile_refs, chosen, picked, slots, height, dummy)

    def body(step, carry):
        products = []
        for sub in range(group):
            code = picked[step * group + sub]
            block = jnp.minimum(code & 63, blocks - 1)
            top = pl.multiple_of((block % halves) * height, height)
            product = lax.dot_general(
                chosen[step * group + sub],
                spreads[block // halves, pl.ds(top, height), :],
                (((0,), (0,)), ((), ())),
                preferred_element_type=jnp.float32,
            )
            products.append((code >> 6, product))
        for slab, product in products:
            totals[slab] += product
        return carry

    lax.fori_loop(0, (total + group - 1) // group, body, 0)
    near = slab_count // far
    ahead = outs[0].shape[0] // near
    rest = nodes - ahead
    for shift in range(far):
        for index in range(near):
            total = totals[shift * near + index].astype(jnp.bfloat16)
            outs[shift][pl.ds(index * ahead, ahead), :] = total[:ahead]
            columns[index, pl.ds(shift * rest, rest), :] = total[ahead:]
    weight_sum = sum_rows(spreads, nodes, 2 * share) + sum_rows(spreads, nodes + 2 * share, 2 * share)
    weight_sum = weight_sum.astype(jnp.bfloat16)
    bias_block = pack_bias(sum_bias(spreads, nodes + 4 * share))
    for index in range(near):
        columns[index, pl.ds(far * rest, 2 * share), :] = weight_sum
        columns[index, pl.ds(far * rest + 2 * share, 16), :] = bias_block


def middle_kernel(arrived, *refs, share, far):
    lines, outs, line = refs[:far], refs[far : 2 * far], refs[2 * far]
    near, ahead = line.shape[:2]
    rest = outs[0].shape[0] - 4 * share - 16
    for index in range(near):
        total = lines[0][pl.ds(index * ahead, ahead), :].astype(jnp.float32)
        for other in lines[1:]:
            total = total + other[pl.ds(index * ahead, ahead), :].astype(jnp.float32)
        line[index] = total.astype(jnp.bfloat16)
    high, low = split_wide(sum_rows(arrived, far * rest, 2 * share))
    bias_block = pack_bias(sum_bias(arrived, far * rest + 2 * share))
    for shift, out in enumerate(outs):
        out[pl.ds(0, rest), :] = sum_rows(arrived, shift * rest, rest).astype(jnp.bfloat16)
        out[pl.ds(rest, 2 * share), :] = high.astype(jnp.bfloat16)
        out[pl.ds(rest + 2 * share, 2 * share), :] = low.astype(jnp.bfloat16)
        out[pl.ds(rest + 4 * share, 16), :] = bias_block


def last_kernel(place, arrived, *refs, share, far, factor):
    pieces = refs[:far]
    grad, weight_share, bias_grad, stack = refs[far:]
    ahead = arrived.shape[1]
    rest = grad.shape[0] - ahead
    grad[pl.ds(0, ahead), :] = sum_rows(arrived, 0, ahead)
    for shift, piece in enumerate(pieces):
        stack[lax.rem(place[0] + shift, far)] = piece[...]
    grad[pl.ds(ahead, rest), :] = sum_rows(stack, 0, rest)
    weight_sum = sum_rows(stack, rest, 2 * share) + sum_rows(stack, rest + 2 * share, 2 * share)
    weight_share[...] = weight_sum * factor
    low, high = sum_bias(stack, rest + 4 * share)
    bias_grad[:, pl.ds(0, lanes)] = low * factor
    bias_grad[:, pl.ds(lanes, lanes)] = high * factor


def copies_kernel(*refs, count):
    out = refs[-1]
    rows = refs[0].shape[0]
    for index in range(out.shape[0]):
        for shift in range(count):
            out[index, pl.ds(shift * rows, rows), :] = refs[shift][...]


def in_vmem():
    return pl.BlockSpec(memory_space=pltpu.VMEM)


def in_smem():
    return pl.BlockSpec(memory_space=pltpu.SMEM)


def local(features, tile_rows, tile_cols, tile_counts, tile_values, weight, bias, cotangent):
    nodes, width = features.shape
    slots, height, tile_width = tile_values.shape[2:]
    hidden = weight.shape[1]
    far = lax.axis_size("yhi")
    across = lax.axis_size("x")
    near = lax.axis_size("z")
    members = lax.axis_size(team_axes)
    group_rows = lax.axis_size(row_axes)
    here = lax.axis_index("x")
    params = pltpu.CompilerParams(vmem_limit_bytes=vmem_bytes)
    halves = nodes // height
    blocks = members * halves

    def any_place():
        return pl.BlockSpec(memory_space=pl.ANY)

    live = jnp.arange(slots, dtype=jnp.int32) < tile_counts[0, 0]
    columns, rows = tile_cols[0, 0], tile_rows[0, 0]
    owner = jnp.where(live, (columns // near) % across, 255)
    distance = (lax.axis_index("yhi") - columns // (across * near)) % far
    slab = distance * near + columns % near
    block = ((rows // halves) * across + here) * halves + rows % halves
    places = jnp.stack([owner, slab, block])
    ends = jnp.stack([jnp.int32(254), jnp.int32(0), tile_counts[0, 0]])[:, None]
    places = jnp.concatenate([places, ends], axis=1)
    places = jnp.pad(places, ((0, 13), (0, lanes - slots - 1))).astype(jnp.bfloat16)
    own = jnp.concatenate([tile_values[0, 0].reshape(slots * height, tile_width), places], axis=0)

    def ring(size, shift):
        return [(start, (start + shift) % size) for start in range(size)]

    buffers = [own, lax.ppermute(own, "x", ring(across, 1))]
    if across > 2:
        buffers.append(lax.ppermute(own, "x", ring(across, -1)))
    early = buffers[1:]
    for shift in range(2, across - 1):
        buffers.append(lax.ppermute(buffers[1 if shift == 2 else -1], "x", ring(across, 1)))

    columns = [features[ahead_rows:]]
    for shift in range(1, far):
        columns.append(lax.ppermute(columns[0], "yhi", ring(far, shift)))
    lines = [spread_out(features[:ahead_rows], "z", near).reshape(near * ahead_rows, width)]
    copies = pl.pallas_call(
        lambda *refs: copies_kernel(*refs, count=far),
        out_shape=jax.ShapeDtypeStruct((near, far * (nodes - ahead_rows), width), jnp.bfloat16),
        in_specs=[in_vmem()] * far + [any_place()] * (1 + len(early)),
        out_specs=in_vmem(),
        compiler_params=params,
        name="column_copies",
    )(*columns, lines[0], *early)
    for shift in range(1, far):
        lines.append(lax.ppermute(lines[0], "yhi", ring(far, shift)))
    columns = lax.all_to_all(copies, "z", 0, 0, tiled=True)

    tables = []
    for buffer in buffers:
        top = buffer[slots * height :].astype(jnp.int32)
        mine = (top[0] == here) | (top[0] == 254)
        tables.append(jnp.where(mine, top[1] * 64 + top[2], -1))
    codes = jnp.stack(tables)

    scratch_tiles = pltpu.VMEM((across * slots + group, height, tile_width), jnp.bfloat16)
    scratch_list = pltpu.SMEM((across * slots + group,), jnp.int32)
    partial = pl.pallas_call(
        lambda *refs: forward_kernel(*refs, slots=slots, height=height, blocks=blocks, far=far, across=across),
        out_shape=jax.ShapeDtypeStruct((members, nodes, width), jnp.bfloat16),
        in_specs=[in_smem()] + [in_vmem()] * (far + 1 + across),
        out_specs=in_vmem(),
        scratch_shapes=[
            pltpu.VMEM((far * near, nodes, width), jnp.bfloat16),
            scratch_tiles,
            pltpu.VMEM((blocks + 1, height, width), jnp.float32),
            scratch_list,
        ],
        compiler_params=params,
        name="forward_tiles",
    )(codes, *lines, columns, *buffers)
    partials = lax.all_to_all(partial, team_axes, 0, 0, tiled=True)

    share = width // members
    hidden_out, message = pl.pallas_call(
        dense_kernel,
        out_shape=(
            jax.ShapeDtypeStruct((nodes, hidden), jnp.bfloat16),
            jax.ShapeDtypeStruct((members, nodes + 4 * share + 16, width), jnp.bfloat16),
        ),
        in_specs=[in_vmem()] * 4,
        out_specs=(in_vmem(), in_vmem()),
        compiler_params=params,
        name="dense_layer",
    )(partials, weight, bias.reshape(1, hidden), cotangent)
    spreads = lax.all_to_all(message, team_axes, 0, 0, tiled=True)

    rest = nodes - back_rows
    shared_rows = 2 * share + 16
    outs = pl.pallas_call(
        lambda *refs: backward_kernel(
            *refs,
            slots=slots,
            height=height,
            blocks=blocks,
            nodes=nodes,
            share=share,
            far=far,
            across=across,
        ),
        out_shape=(jax.ShapeDtypeStruct((near * back_rows, width), jnp.bfloat16),) * far
        + (jax.ShapeDtypeStruct((near, far * rest + shared_rows, width), jnp.bfloat16),),
        in_specs=[in_smem(), in_vmem()] + [in_vmem()] * across,
        out_specs=(in_vmem(),) * (far + 1),
        scratch_shapes=[
            scratch_tiles,
            pltpu.VMEM((far * near + 1, nodes, width), jnp.float32),
            scratch_list,
        ],
        compiler_params=params,
        name="backward_tiles",
    )(codes, spreads, *buffers)

    lines = [outs[0]]
    for shift in range(1, far):
        lines.append(lax.ppermute(outs[shift], "yhi", ring(far, -shift)))
    arrived = lax.all_to_all(outs[far], "z", 0, 0, tiled=True)
    outs = pl.pallas_call(
        lambda *refs: middle_kernel(*refs, share=share, far=far),
        out_shape=(jax.ShapeDtypeStruct((rest + 2 * share + shared_rows, width), jnp.bfloat16),) * far
        + (jax.ShapeDtypeStruct((near, back_rows, width), jnp.bfloat16),),
        in_specs=[in_vmem()] * (far + 1),
        out_specs=(in_vmem(),) * (far + 1),
        compiler_params=params,
        name="middle_sums",
    )(arrived, *lines)
    pieces = [outs[0]]
    for shift in range(1, far):
        pieces.append(lax.ppermute(outs[shift], "yhi", ring(far, -shift)))
    arrived = lax.all_to_all(outs[far], "z", 0, 0, tiled=True)
    factor = 1.0 / math.sqrt(nodes * group_rows * far * across * near)
    features_grad, weight_share, bias_grad = pl.pallas_call(
        lambda *refs: last_kernel(*refs, share=share, far=far, factor=factor),
        out_shape=(
            jax.ShapeDtypeStruct((nodes, width), jnp.float32),
            jax.ShapeDtypeStruct((2 * share, lanes), jnp.float32),
            jax.ShapeDtypeStruct((1, hidden), jnp.float32),
        ),
        in_specs=[in_smem()] + [in_vmem()] * (far + 1),
        out_specs=(in_vmem(), in_vmem(), in_vmem()),
        scratch_shapes=[pltpu.VMEM((far,) + pieces[0].shape, jnp.bfloat16)],
        compiler_params=params,
        name="last_sums",
    )(lax.axis_index("yhi").reshape(1), arrived, *pieces)
    shares = spread_out(weight_share, team_axes, members)
    weight_grad = shares.reshape(members, 2, share, lanes).transpose(0, 2, 1, 3)
    weight_grad = weight_grad.reshape(width, hidden)
    return (hidden_out, features_grad, weight_grad, bias_grad.reshape(hidden))


def solution(mesh):
    fine = Mesh(mesh.devices.reshape(row_split + col_split), axis_names)
    nodes_spec = P(row_axes + col_axes, None)
    in_specs = (
        nodes_spec,
        P(row_axes, col_axes, None),
        P(row_axes, col_axes, None),
        P(row_axes, col_axes),
        P(row_axes, col_axes, None, None, None),
        P(),
        P(),
        nodes_spec,
    )
    out_specs = (nodes_spec, nodes_spec, P(), P())
    return jax.shard_map(local, mesh=fine, in_specs=in_specs, out_specs=out_specs, check_vma=False)
```

```python
import math

import jax
import jax.numpy as jnp
from jax import lax
from jax.experimental import pallas as pl
from jax.experimental.pallas import tpu as pltpu
from jax.sharding import Mesh, PartitionSpec as P

row_split = (2, 2)
col_split = (4, 4, 12)
axis_names = ("ylo", "core", "yhi", "x", "z")
row_axes = ("ylo", "core")
col_axes = ("yhi", "x", "z")
team_axes = ("ylo", "core", "x")
group = 4
lanes = 128
vmem_bytes = 12 * 1024 * 1024
root_two_over_pi = math.sqrt(2.0 / math.pi)
cubic = 0.044715


def spread_out(value, axes, count):
    copies = jnp.broadcast_to(value[None], (count,) + value.shape)
    return lax.all_to_all(copies, axes, 0, 0, tiled=True)


def codes_kernel(here, *refs, across, top):
    out = refs[-1]
    for source in range(across):
        places = refs[source][pl.ds(top, 16), :].astype(jnp.float32).astype(jnp.int32)
        mine = (places[0:1] == here[0]) | (places[0:1] == 254)
        out[pl.ds(source, 1), :] = jnp.where(mine, places[1:2] * 64 + places[2:3], -1)


def pick_tiles(codes, tile_refs, chosen, picked, slots, height, dummy):
    total = jnp.int32(0)
    for source, tiles in enumerate(tile_refs):

        def body(step, total, source=source, tiles=tiles):
            for sub in range(group):
                slot = step * group + sub
                code = codes[source, slot]
                top = pl.multiple_of(slot * height, height)
                chosen[total] = tiles[pl.ds(top, height), :]
                picked[total] = code
                total = total + jnp.where(code >= 0, 1, 0)
            return total

        total = lax.fori_loop(0, (codes[source, slots] + group - 1) // group, body, total)
    for sub in range(group):
        picked[total + sub] = dummy
    return total


def forward_kernel(codes, *refs, slots, height, blocks, far, across):
    lines, tile_refs = refs[:far], refs[far : far + across]
    out, slabs, chosen, totals, picked = refs[far + across :]
    slab_count = slabs.shape[0]
    near = slab_count // far
    for shift, line in enumerate(lines):
        slabs[pl.ds(shift * near, near)] = line[...]
    dummy = slab_count * 64 + blocks
    totals[...] = jnp.zeros_like(totals)
    total = pick_tiles(codes, tile_refs, chosen, picked, slots, height, dummy)

    def body(step, carry):
        products = []
        for sub in range(group):
            code = picked[step * group + sub]
            slab = jnp.minimum(code >> 6, slab_count - 1)
            product = jnp.dot(
                chosen[step * group + sub], slabs[slab], preferred_element_type=jnp.float32
            )
            products.append((code & 63, product))
        for block, product in products:
            totals[block] += product
        return carry

    lax.fori_loop(0, (total + group - 1) // group, body, 0)
    halves = out.shape[1] // height
    for block in range(blocks):
        out[block // halves, pl.ds((block % halves) * height, height), :] = totals[block].astype(
            jnp.bfloat16
        )


def split_wide(value):
    high = value.astype(jnp.bfloat16).astype(jnp.float32)
    return high, value - high


def bias_rows(pieces):
    rows = lax.broadcasted_iota(jnp.int32, (16, lanes), 0)
    block = jnp.zeros((16, lanes), jnp.float32)
    for index, piece in enumerate(pieces):
        block = jnp.where(rows == index, jnp.broadcast_to(piece, (16, lanes)), block)
    return block


def sum_rows(ref, start, size):
    value = ref[0, pl.ds(start, size), :].astype(jnp.float32)
    for index in range(1, ref.shape[0]):
        value = value + ref[index, pl.ds(start, size), :].astype(jnp.float32)
    return value


def dense_kernel(partials, weight, bias, cotangent, hidden, message):
    members = partials.shape[0]
    nodes = partials.shape[1]
    aggregate = sum_rows(partials, 0, nodes)
    weight_wide = weight[...].astype(jnp.float32)
    pre = (
        jnp.dot(
            aggregate,
            weight_wide,
            precision=lax.Precision.HIGHEST,
            preferred_element_type=jnp.float32,
        )
        + bias[...]
    )
    square = pre * pre
    angle = jnp.tanh(root_two_over_pi * (pre + cubic * (square * pre)))
    gate = 0.5 * (1.0 + angle)
    hidden[...] = (pre * gate).astype(jnp.bfloat16)
    inner = root_two_over_pi * (1.0 + 3.0 * cubic * square)
    gradient = gate + 0.5 * pre * (1.0 - angle * angle) * inner
    slope = (cotangent[...].astype(jnp.float32) * gradient).astype(jnp.bfloat16)
    slope_wide = slope.astype(jnp.float32)
    spread = lax.dot_general(
        slope, weight[...], (((1,), (1,)), ((), ())), preferred_element_type=jnp.float32
    ).astype(jnp.bfloat16)
    weight_part = lax.dot_general(
        aggregate,
        slope_wide,
        (((0,), (0,)), ((), ())),
        precision=lax.Precision.HIGHEST,
        preferred_element_type=jnp.float32,
    )
    bias_part = jnp.sum(slope_wide, axis=0, keepdims=True)
    high, low = split_wide(bias_part)
    bias_block = bias_rows([high[:, :lanes], high[:, lanes:], low[:, :lanes], low[:, lanes:]])
    bias_block = bias_block.astype(jnp.bfloat16)
    share = weight_part.shape[0] // members
    for member in range(members):
        message[member, pl.ds(0, nodes), :] = spread
        part = weight_part[member * share : (member + 1) * share]
        part = jnp.concatenate([part[:, :lanes], part[:, lanes:]], axis=0)
        high, low = split_wide(part)
        message[member, pl.ds(nodes, 2 * share), :] = high.astype(jnp.bfloat16)
        message[member, pl.ds(nodes + 2 * share, 2 * share), :] = low.astype(jnp.bfloat16)
        message[member, pl.ds(nodes + 4 * share, 16), :] = bias_block


def sum_bias(ref, start):
    block = sum_rows(ref, start, 16)
    return [block[0:1] + block[2:3], block[1:2] + block[3:4]]


def pack_bias(values):
    parts = [split_wide(value) for value in values]
    return bias_rows([parts[0][0], parts[1][0], parts[0][1], parts[1][1]]).astype(jnp.bfloat16)


def backward_kernel(codes, spreads, *refs, slots, height, blocks, nodes, share, far, across):
    tile_refs, outs = refs[:across], refs[across : across + far]
    shares, chosen, totals, picked = refs[across + far :]
    slab_count = totals.shape[0] - 1
    halves = nodes // height
    dummy = slab_count * 64 + blocks
    totals[...] = jnp.zeros_like(totals)
    total = pick_tiles(codes, tile_refs, chosen, picked, slots, height, dummy)

    def body(step, carry):
        products = []
        for sub in range(group):
            code = picked[step * group + sub]
            block = jnp.minimum(code & 63, blocks - 1)
            top = pl.multiple_of((block % halves) * height, height)
            product = lax.dot_general(
                chosen[step * group + sub],
                spreads[block // halves, pl.ds(top, height), :],
                (((0,), (0,)), ((), ())),
                preferred_element_type=jnp.float32,
            )
            products.append((code >> 6, product))
        for slab, product in products:
            totals[slab] += product
        return carry

    lax.fori_loop(0, (total + group - 1) // group, body, 0)
    near = slab_count // far
    for shift, out in enumerate(outs):
        for index in range(near):
            out[index] = totals[shift * near + index].astype(jnp.bfloat16)
    weight_sum = sum_rows(spreads, nodes, 2 * share) + sum_rows(spreads, nodes + 2 * share, 2 * share)
    high, low = split_wide(weight_sum)
    bias_block = pack_bias(sum_bias(spreads, nodes + 4 * share))
    for index in range(near):
        shares[index, pl.ds(0, 2 * share), :] = high.astype(jnp.bfloat16)
        shares[index, pl.ds(2 * share, 2 * share), :] = low.astype(jnp.bfloat16)
        shares[index, pl.ds(4 * share, 16), :] = bias_block


def share_kernel(arrived, out, bias_block, *, share):
    total = sum_rows(arrived, 0, 2 * share) + sum_rows(arrived, 2 * share, 2 * share)
    for index in range(out.shape[0]):
        out[index] = total
    bias_block[...] = pack_bias(sum_bias(arrived, 4 * share))


def gather_kernel(shares, bias_block, out, *, share):
    step = 16 // share if share < 16 else 1
    rows = shares.shape[0] * share
    for half in range(2):
        for first in range(0, shares.shape[0], step):
            parts = [shares[first + sub, pl.ds(half * share, share), :] for sub in range(step)]
            part = jnp.concatenate(parts, axis=0) if step > 1 else parts[0]
            out[pl.ds(half * rows + first * share, step * share), :] = part.astype(jnp.bfloat16)
    out[pl.ds(2 * rows, 16), :] = bias_block[...]


def middle_kernel(*refs, far):
    out = refs[-1]
    for index in range(out.shape[0]):
        total = refs[0][index].astype(jnp.float32)
        for line in refs[1:far]:
            total = total + line[index].astype(jnp.float32)
        out[index] = total.astype(jnp.bfloat16)


def last_kernel(place, arrived, *refs, far, factor):
    pieces = refs[:far]
    grad, weight_grad, bias_grad, stack = refs[far:]
    grad[...] = sum_rows(arrived, 0, grad.shape[0])
    for shift, piece in enumerate(pieces):
        stack[lax.rem(place[0] + shift, far)] = piece[...]
    rows = weight_grad.shape[0]
    weight_grad[:, pl.ds(0, lanes)] = sum_rows(stack, 0, rows) * factor
    weight_grad[:, pl.ds(lanes, lanes)] = sum_rows(stack, rows, rows) * factor
    low, high = sum_bias(stack, 2 * rows)
    bias_grad[:, pl.ds(0, lanes)] = low * factor
    bias_grad[:, pl.ds(lanes, lanes)] = high * factor


def in_vmem():
    return pl.BlockSpec(memory_space=pltpu.VMEM)


def in_smem():
    return pl.BlockSpec(memory_space=pltpu.SMEM)


def local(features, tile_rows, tile_cols, tile_counts, tile_values, weight, bias, cotangent):
    nodes, width = features.shape
    slots, height, tile_width = tile_values.shape[2:]
    hidden = weight.shape[1]
    far = lax.axis_size("yhi")
    across = lax.axis_size("x")
    near = lax.axis_size("z")
    members = lax.axis_size(team_axes)
    group_rows = lax.axis_size(row_axes)
    here = lax.axis_index("x")
    params = pltpu.CompilerParams(vmem_limit_bytes=vmem_bytes)
    halves = nodes // height
    blocks = members * halves

    def any_place():
        return pl.BlockSpec(memory_space=pl.ANY)

    live = jnp.arange(slots, dtype=jnp.int32) < tile_counts[0, 0]
    columns, rows = tile_cols[0, 0], tile_rows[0, 0]
    owner = jnp.where(live, (columns // near) % across, 255)
    distance = (lax.axis_index("yhi") - columns // (across * near)) % far
    slab = distance * near + columns % near
    block = ((rows // halves) * across + here) * halves + rows % halves
    places = jnp.stack([owner, slab, block])
    ends = jnp.stack([jnp.int32(254), jnp.int32(0), tile_counts[0, 0]])[:, None]
    places = jnp.concatenate([places, ends], axis=1)
    places = jnp.pad(places, ((0, 13), (0, lanes - slots - 1))).astype(jnp.bfloat16)
    own = jnp.concatenate([tile_values[0, 0].reshape(slots * height, tile_width), places], axis=0)

    def ring(size, shift):
        return [(start, (start + shift) % size) for start in range(size)]

    buffers = [own]
    for shift in range(1, across):
        buffers.append(lax.ppermute(own, "x", ring(across, shift)))

    lines = [spread_out(features, "z", near)]
    for shift in range(1, far):
        lines.append(lax.ppermute(lines[0], "yhi", ring(far, shift)))

    codes = pl.pallas_call(
        lambda *refs: codes_kernel(*refs, across=across, top=slots * height),
        out_shape=jax.ShapeDtypeStruct((across, lanes), jnp.int32),
        in_specs=[in_smem()] + [in_vmem()] * across + [any_place()] * (far - 1),
        out_specs=in_vmem(),
        compiler_params=params,
        name="tile_codes",
    )(here.reshape(1), *buffers, *lines[1:])

    scratch_tiles = pltpu.VMEM((across * slots + group, height, tile_width), jnp.bfloat16)
    scratch_list = pltpu.SMEM((across * slots + group,), jnp.int32)
    partial = pl.pallas_call(
        lambda *refs: forward_kernel(*refs, slots=slots, height=height, blocks=blocks, far=far, across=across),
        out_shape=jax.ShapeDtypeStruct((members, nodes, width), jnp.bfloat16),
        in_specs=[in_smem()] + [in_vmem()] * (far + across),
        out_specs=in_vmem(),
        scratch_shapes=[
            pltpu.VMEM((far * near, nodes, width), jnp.bfloat16),
            scratch_tiles,
            pltpu.VMEM((blocks + 1, height, width), jnp.float32),
            scratch_list,
        ],
        compiler_params=params,
        name="forward_tiles",
    )(codes, *lines, *buffers)
    partials = lax.all_to_all(partial, team_axes, 0, 0, tiled=True)

    share = width // members
    hidden_out, message = pl.pallas_call(
        dense_kernel,
        out_shape=(
            jax.ShapeDtypeStruct((nodes, hidden), jnp.bfloat16),
            jax.ShapeDtypeStruct((members, nodes + 4 * share + 16, width), jnp.bfloat16),
        ),
        in_specs=[in_vmem()] * 4,
        out_specs=(in_vmem(), in_vmem()),
        compiler_params=params,
        name="dense_layer",
    )(partials, weight, bias.reshape(1, hidden), cotangent)
    spreads = lax.all_to_all(message, team_axes, 0, 0, tiled=True)

    outs = pl.pallas_call(
        lambda *refs: backward_kernel(
            *refs,
            slots=slots,
            height=height,
            blocks=blocks,
            nodes=nodes,
            share=share,
            far=far,
            across=across,
        ),
        out_shape=(jax.ShapeDtypeStruct((near, nodes, width), jnp.bfloat16),) * far
        + (jax.ShapeDtypeStruct((near, 4 * share + 16, width), jnp.bfloat16),),
        in_specs=[in_smem(), in_vmem()] + [in_vmem()] * across,
        out_specs=(in_vmem(),) * (far + 1),
        scratch_shapes=[
            scratch_tiles,
            pltpu.VMEM((far * near + 1, nodes, width), jnp.float32),
            scratch_list,
        ],
        compiler_params=params,
        name="backward_tiles",
    )(codes, spreads, *buffers)

    lines = [outs[0]]
    for shift in range(1, far):
        lines.append(lax.ppermute(outs[shift], "yhi", ring(far, -shift)))
    arrived = lax.all_to_all(outs[far], "z", 0, 0, tiled=True)
    shares, bias_block = pl.pallas_call(
        lambda *refs: share_kernel(*refs, share=share),
        out_shape=(
            jax.ShapeDtypeStruct((members, 2 * share, lanes), jnp.float32),
            jax.ShapeDtypeStruct((16, lanes), jnp.bfloat16),
        ),
        in_specs=[in_vmem()],
        out_specs=(in_vmem(), in_vmem()),
        compiler_params=params,
        name="share_sum",
    )(arrived)
    shares = lax.all_to_all(shares, team_axes, 0, 0, tiled=True)
    gradients = pl.pallas_call(
        lambda *refs: gather_kernel(*refs, share=share),
        out_shape=jax.ShapeDtypeStruct((2 * width + 16, lanes), jnp.bfloat16),
        in_specs=[in_vmem(), in_vmem()],
        out_specs=in_vmem(),
        compiler_params=params,
        name="share_gather",
    )(shares, bias_block)
    line = pl.pallas_call(
        lambda *refs: middle_kernel(*refs, far=far),
        out_shape=jax.ShapeDtypeStruct((near, nodes, width), jnp.bfloat16),
        in_specs=[in_vmem()] * far + [any_place()],
        out_specs=in_vmem(),
        compiler_params=params,
        name="middle_sums",
    )(*lines, gradients)

    pieces = [gradients]
    for shift in range(1, far):
        pieces.append(lax.ppermute(gradients, "yhi", ring(far, -shift)))
    arrived = lax.all_to_all(line, "z", 0, 0, tiled=True)
    factor = 1.0 / math.sqrt(nodes * group_rows * far * across * near)
    features_grad, weight_grad, bias_grad = pl.pallas_call(
        lambda *refs: last_kernel(*refs, far=far, factor=factor),
        out_shape=(
            jax.ShapeDtypeStruct((nodes, width), jnp.float32),
            jax.ShapeDtypeStruct((width, hidden), jnp.float32),
            jax.ShapeDtypeStruct((1, hidden), jnp.float32),
        ),
        in_specs=[in_smem()] + [in_vmem()] * (far + 1),
        out_specs=(in_vmem(), in_vmem(), in_vmem()),
        scratch_shapes=[pltpu.VMEM((far,) + gradients.shape, jnp.bfloat16)],
        compiler_params=params,
        name="last_sums",
    )(lax.axis_index("yhi").reshape(1), arrived, *pieces)
    return (hidden_out, features_grad, weight_grad, bias_grad.reshape(hidden))


def solution(mesh):
    fine = Mesh(mesh.devices.reshape(row_split + col_split), axis_names)
    nodes_spec = P(row_axes + col_axes, None)
    in_specs = (
        nodes_spec,
        P(row_axes, col_axes, None),
        P(row_axes, col_axes, None),
        P(row_axes, col_axes),
        P(row_axes, col_axes, None, None, None),
        P(),
        P(),
        nodes_spec,
    )
    out_specs = (nodes_spec, nodes_spec, P(), P())
    return jax.shard_map(local, mesh=fine, in_specs=in_specs, out_specs=out_specs, check_vma=False)
```

```python
import math

import jax
import jax.numpy as jnp
from jax import lax
from jax.experimental import pallas as pl
from jax.experimental.pallas import tpu as pltpu
from jax.sharding import Mesh, PartitionSpec as P

row_split = (2, 2)
col_split = (4, 4, 12)
axis_names = ("ylo", "core", "yhi", "x", "z")
row_axes = ("ylo", "core")
col_axes = ("yhi", "x", "z")
team_axes = ("ylo", "core", "x")
group = 4
lanes = 128
vmem_bytes = 12 * 1024 * 1024
root_two_over_pi = math.sqrt(2.0 / math.pi)
cubic = 0.044715


def spread_out(value, axes, count):
    copies = jnp.broadcast_to(value[None], (count,) + value.shape)
    return lax.all_to_all(copies, axes, 0, 0, tiled=True)


def codes_kernel(here, *refs, across, top):
    out = refs[-1]
    for source in range(across):
        places = refs[source][pl.ds(top, 16), :].astype(jnp.float32).astype(jnp.int32)
        mine = (places[0:1] == here[0]) | (places[0:1] == 254)
        out[pl.ds(source, 1), :] = jnp.where(mine, places[1:2] * 64 + places[2:3], -1)


def pick_tiles(codes, tile_refs, chosen, picked, slots, height, dummy):
    total = jnp.int32(0)
    for source, tiles in enumerate(tile_refs):

        def body(step, total, source=source, tiles=tiles):
            for sub in range(group):
                slot = step * group + sub
                code = codes[source, slot]
                top = pl.multiple_of(slot * height, height)
                chosen[total] = tiles[pl.ds(top, height), :]
                picked[total] = code
                total = total + jnp.where(code >= 0, 1, 0)
            return total

        total = lax.fori_loop(0, (codes[source, slots] + group - 1) // group, body, total)
    for sub in range(group):
        picked[total + sub] = dummy
    return total


def forward_kernel(codes, *refs, slots, height, blocks, far, across):
    lines, tile_refs = refs[:far], refs[far : far + across]
    out, slabs, chosen, totals, picked = refs[far + across :]
    slab_count = slabs.shape[0]
    near = slab_count // far
    for shift, line in enumerate(lines):
        slabs[pl.ds(shift * near, near)] = line[...]
    dummy = slab_count * 64 + blocks
    totals[...] = jnp.zeros_like(totals)
    total = pick_tiles(codes, tile_refs, chosen, picked, slots, height, dummy)

    def body(step, carry):
        products = []
        for sub in range(group):
            code = picked[step * group + sub]
            slab = jnp.minimum(code >> 6, slab_count - 1)
            product = jnp.dot(
                chosen[step * group + sub], slabs[slab], preferred_element_type=jnp.float32
            )
            products.append((code & 63, product))
        for block, product in products:
            totals[block] += product
        return carry

    lax.fori_loop(0, (total + group - 1) // group, body, 0)
    halves = out.shape[1] // height
    for block in range(blocks):
        out[block // halves, pl.ds((block % halves) * height, height), :] = totals[block].astype(
            jnp.bfloat16
        )


def split_wide(value):
    high = value.astype(jnp.bfloat16).astype(jnp.float32)
    return high, value - high


def bias_rows(pieces):
    rows = lax.broadcasted_iota(jnp.int32, (16, lanes), 0)
    block = jnp.zeros((16, lanes), jnp.float32)
    for index, piece in enumerate(pieces):
        block = jnp.where(rows == index, jnp.broadcast_to(piece, (16, lanes)), block)
    return block


def sum_rows(ref, start, size):
    value = ref[0, pl.ds(start, size), :].astype(jnp.float32)
    for index in range(1, ref.shape[0]):
        value = value + ref[index, pl.ds(start, size), :].astype(jnp.float32)
    return value


def dense_kernel(partials, weight, bias, cotangent, hidden, message):
    members = partials.shape[0]
    nodes = partials.shape[1]
    aggregate = sum_rows(partials, 0, nodes)
    weight_wide = weight[...].astype(jnp.float32)
    pre = (
        jnp.dot(
            aggregate,
            weight_wide,
            precision=lax.Precision.HIGHEST,
            preferred_element_type=jnp.float32,
        )
        + bias[...]
    )
    square = pre * pre
    angle = jnp.tanh(root_two_over_pi * (pre + cubic * (square * pre)))
    gate = 0.5 * (1.0 + angle)
    hidden[...] = (pre * gate).astype(jnp.bfloat16)
    inner = root_two_over_pi * (1.0 + 3.0 * cubic * square)
    gradient = gate + 0.5 * pre * (1.0 - angle * angle) * inner
    slope = (cotangent[...].astype(jnp.float32) * gradient).astype(jnp.bfloat16)
    slope_wide = slope.astype(jnp.float32)
    spread = lax.dot_general(
        slope, weight[...], (((1,), (1,)), ((), ())), preferred_element_type=jnp.float32
    ).astype(jnp.bfloat16)
    weight_part = lax.dot_general(
        aggregate,
        slope_wide,
        (((0,), (0,)), ((), ())),
        precision=lax.Precision.HIGHEST,
        preferred_element_type=jnp.float32,
    )
    bias_part = jnp.sum(slope_wide, axis=0, keepdims=True)
    high, low = split_wide(bias_part)
    bias_block = bias_rows([high[:, :lanes], high[:, lanes:], low[:, :lanes], low[:, lanes:]])
    bias_block = bias_block.astype(jnp.bfloat16)
    share = weight_part.shape[0] // members
    for member in range(members):
        message[member, pl.ds(0, nodes), :] = spread
        part = weight_part[member * share : (member + 1) * share]
        part = jnp.concatenate([part[:, :lanes], part[:, lanes:]], axis=0)
        high, low = split_wide(part)
        message[member, pl.ds(nodes, 2 * share), :] = high.astype(jnp.bfloat16)
        message[member, pl.ds(nodes + 2 * share, 2 * share), :] = low.astype(jnp.bfloat16)
        message[member, pl.ds(nodes + 4 * share, 16), :] = bias_block


def sum_bias(ref, start):
    block = sum_rows(ref, start, 16)
    return [block[0:1] + block[2:3], block[1:2] + block[3:4]]


def pack_bias(values):
    parts = [split_wide(value) for value in values]
    return bias_rows([parts[0][0], parts[1][0], parts[0][1], parts[1][1]]).astype(jnp.bfloat16)


def backward_kernel(codes, spreads, *refs, slots, height, blocks, nodes, share, far, across):
    tile_refs, outs = refs[:across], refs[across : across + far]
    shares, chosen, totals, picked = refs[across + far :]
    slab_count = totals.shape[0] - 1
    halves = nodes // height
    dummy = slab_count * 64 + blocks
    totals[...] = jnp.zeros_like(totals)
    total = pick_tiles(codes, tile_refs, chosen, picked, slots, height, dummy)

    def body(step, carry):
        products = []
        for sub in range(group):
            code = picked[step * group + sub]
            block = jnp.minimum(code & 63, blocks - 1)
            top = pl.multiple_of((block % halves) * height, height)
            product = lax.dot_general(
                chosen[step * group + sub],
                spreads[block // halves, pl.ds(top, height), :],
                (((0,), (0,)), ((), ())),
                preferred_element_type=jnp.float32,
            )
            products.append((code >> 6, product))
        for slab, product in products:
            totals[slab] += product
        return carry

    lax.fori_loop(0, (total + group - 1) // group, body, 0)
    near = slab_count // far
    for shift, out in enumerate(outs):
        for index in range(near):
            out[index] = totals[shift * near + index].astype(jnp.bfloat16)
    weight_sum = sum_rows(spreads, nodes, 2 * share) + sum_rows(spreads, nodes + 2 * share, 2 * share)
    high, low = split_wide(weight_sum)
    bias_block = pack_bias(sum_bias(spreads, nodes + 4 * share))
    for index in range(near):
        shares[index, pl.ds(0, 2 * share), :] = high.astype(jnp.bfloat16)
        shares[index, pl.ds(2 * share, 2 * share), :] = low.astype(jnp.bfloat16)
        shares[index, pl.ds(4 * share, 16), :] = bias_block


def share_kernel(arrived, out, bias_block, *, share):
    total = sum_rows(arrived, 0, 2 * share) + sum_rows(arrived, 2 * share, 2 * share)
    for index in range(out.shape[0]):
        out[index] = total
    bias_block[...] = pack_bias(sum_bias(arrived, 4 * share))


def gather_kernel(shares, bias_block, out, *, share):
    step = 16 // share if share < 16 else 1
    rows = shares.shape[0] * share
    for half in range(2):
        for first in range(0, shares.shape[0], step):
            parts = [shares[first + sub, pl.ds(half * share, share), :] for sub in range(step)]
            part = jnp.concatenate(parts, axis=0) if step > 1 else parts[0]
            out[pl.ds(half * rows + first * share, step * share), :] = part.astype(jnp.bfloat16)
    out[pl.ds(2 * rows, 16), :] = bias_block[...]


def middle_kernel(*refs, far):
    out = refs[-1]
    for index in range(out.shape[0]):
        total = refs[0][index].astype(jnp.float32)
        for line in refs[1:far]:
            total = total + line[index].astype(jnp.float32)
        out[index] = total.astype(jnp.bfloat16)


def last_kernel(place, arrived, *refs, far, factor):
    pieces = refs[:far]
    grad, weight_grad, bias_grad, stack = refs[far:]
    grad[...] = sum_rows(arrived, 0, grad.shape[0])
    for shift, piece in enumerate(pieces):
        stack[lax.rem(place[0] + shift, far)] = piece[...]
    rows = weight_grad.shape[0]
    weight_grad[:, pl.ds(0, lanes)] = sum_rows(stack, 0, rows) * factor
    weight_grad[:, pl.ds(lanes, lanes)] = sum_rows(stack, rows, rows) * factor
    low, high = sum_bias(stack, 2 * rows)
    bias_grad[:, pl.ds(0, lanes)] = low * factor
    bias_grad[:, pl.ds(lanes, lanes)] = high * factor


def in_vmem():
    return pl.BlockSpec(memory_space=pltpu.VMEM)


def in_smem():
    return pl.BlockSpec(memory_space=pltpu.SMEM)


def local(features, tile_rows, tile_cols, tile_counts, tile_values, weight, bias, cotangent):
    nodes, width = features.shape
    slots, height, tile_width = tile_values.shape[2:]
    hidden = weight.shape[1]
    far = lax.axis_size("yhi")
    across = lax.axis_size("x")
    near = lax.axis_size("z")
    members = lax.axis_size(team_axes)
    group_rows = lax.axis_size(row_axes)
    here = lax.axis_index("x")
    params = pltpu.CompilerParams(vmem_limit_bytes=vmem_bytes)
    halves = nodes // height
    blocks = members * halves

    def any_place():
        return pl.BlockSpec(memory_space=pl.ANY)

    live = jnp.arange(slots, dtype=jnp.int32) < tile_counts[0, 0]
    columns, rows = tile_cols[0, 0], tile_rows[0, 0]
    owner = jnp.where(live, (columns // near) % across, 255)
    distance = (lax.axis_index("yhi") - columns // (across * near)) % far
    slab = distance * near + columns % near
    block = ((rows // halves) * across + here) * halves + rows % halves
    places = jnp.stack([owner, slab, block])
    ends = jnp.stack([jnp.int32(254), jnp.int32(0), tile_counts[0, 0]])[:, None]
    places = jnp.concatenate([places, ends], axis=1)
    places = jnp.pad(places, ((0, 13), (0, lanes - slots - 1))).astype(jnp.bfloat16)
    own = jnp.concatenate([tile_values[0, 0].reshape(slots * height, tile_width), places], axis=0)

    def ring(size, shift):
        return [(start, (start + shift) % size) for start in range(size)]

    buffers = [own]
    for shift in range(1, across):
        buffers.append(lax.ppermute(own, "x", ring(across, shift)))

    lines = [spread_out(features, "z", near)]
    for shift in range(1, far):
        lines.append(lax.ppermute(lines[0], "yhi", ring(far, shift)))

    codes = pl.pallas_call(
        lambda *refs: codes_kernel(*refs, across=across, top=slots * height),
        out_shape=jax.ShapeDtypeStruct((across, lanes), jnp.int32),
        in_specs=[in_smem()] + [in_vmem()] * across + [any_place()] * (far - 1),
        out_specs=in_vmem(),
        compiler_params=params,
        name="tile_codes",
    )(here.reshape(1), *buffers, *lines[1:])

    scratch_tiles = pltpu.VMEM((across * slots + group, height, tile_width), jnp.bfloat16)
    scratch_list = pltpu.SMEM((across * slots + group,), jnp.int32)
    partial = pl.pallas_call(
        lambda *refs: forward_kernel(*refs, slots=slots, height=height, blocks=blocks, far=far, across=across),
        out_shape=jax.ShapeDtypeStruct((members, nodes, width), jnp.bfloat16),
        in_specs=[in_smem()] + [in_vmem()] * (far + across),
        out_specs=in_vmem(),
        scratch_shapes=[
            pltpu.VMEM((far * near, nodes, width), jnp.bfloat16),
            scratch_tiles,
            pltpu.VMEM((blocks + 1, height, width), jnp.float32),
            scratch_list,
        ],
        compiler_params=params,
        name="forward_tiles",
    )(codes, *lines, *buffers)
    partials = lax.all_to_all(partial, team_axes, 0, 0, tiled=True)

    share = width // members
    hidden_out, message = pl.pallas_call(
        dense_kernel,
        out_shape=(
            jax.ShapeDtypeStruct((nodes, hidden), jnp.bfloat16),
            jax.ShapeDtypeStruct((members, nodes + 4 * share + 16, width), jnp.bfloat16),
        ),
        in_specs=[in_vmem()] * 4,
        out_specs=(in_vmem(), in_vmem()),
        compiler_params=params,
        name="dense_layer",
    )(partials, weight, bias.reshape(1, hidden), cotangent)
    spreads = lax.all_to_all(message, team_axes, 0, 0, tiled=True)

    outs = pl.pallas_call(
        lambda *refs: backward_kernel(
            *refs,
            slots=slots,
            height=height,
            blocks=blocks,
            nodes=nodes,
            share=share,
            far=far,
            across=across,
        ),
        out_shape=(jax.ShapeDtypeStruct((near, nodes, width), jnp.bfloat16),) * far
        + (jax.ShapeDtypeStruct((near, 4 * share + 16, width), jnp.bfloat16),),
        in_specs=[in_smem(), in_vmem()] + [in_vmem()] * across,
        out_specs=(in_vmem(),) * (far + 1),
        scratch_shapes=[
            scratch_tiles,
            pltpu.VMEM((far * near + 1, nodes, width), jnp.float32),
            scratch_list,
        ],
        compiler_params=params,
        name="backward_tiles",
    )(codes, spreads, *buffers)

    lines = [outs[0]]
    for shift in range(1, far):
        lines.append(lax.ppermute(outs[shift], "yhi", ring(far, -shift)))

    def gather_gradients(value):
        arrived = lax.all_to_all(value, "z", 0, 0, tiled=True)
        shares, bias_block = pl.pallas_call(
            lambda *refs: share_kernel(*refs, share=share),
            out_shape=(
                jax.ShapeDtypeStruct((members, 2 * share, lanes), jnp.float32),
                jax.ShapeDtypeStruct((16, lanes), jnp.bfloat16),
            ),
            in_specs=[in_vmem()],
            out_specs=(in_vmem(), in_vmem()),
            compiler_params=params,
            name="share_sum",
        )(arrived)
        shares = lax.all_to_all(shares, team_axes, 0, 0, tiled=True)
        return pl.pallas_call(
            lambda *refs: gather_kernel(*refs, share=share),
            out_shape=jax.ShapeDtypeStruct((2 * width + 16, lanes), jnp.bfloat16),
            in_specs=[in_vmem(), in_vmem()],
            out_specs=in_vmem(),
            compiler_params=params,
            name="share_gather",
        )(shares, bias_block)

    gradients = lax.cond(
        tile_counts[0, 0] > 0,
        gather_gradients,
        lambda value: jnp.zeros((2 * width + 16, lanes), jnp.bfloat16),
        outs[far],
    )
    line = pl.pallas_call(
        lambda *refs: middle_kernel(*refs, far=far),
        out_shape=jax.ShapeDtypeStruct((near, nodes, width), jnp.bfloat16),
        in_specs=[in_vmem()] * far + [any_place()],
        out_specs=in_vmem(),
        compiler_params=params,
        name="middle_sums",
    )(*lines, gradients)

    pieces = [gradients]
    for shift in range(1, far):
        pieces.append(lax.ppermute(gradients, "yhi", ring(far, -shift)))
    arrived = lax.all_to_all(line, "z", 0, 0, tiled=True)
    factor = 1.0 / math.sqrt(nodes * group_rows * far * across * near)
    features_grad, weight_grad, bias_grad = pl.pallas_call(
        lambda *refs: last_kernel(*refs, far=far, factor=factor),
        out_shape=(
            jax.ShapeDtypeStruct((nodes, width), jnp.float32),
            jax.ShapeDtypeStruct((width, hidden), jnp.float32),
            jax.ShapeDtypeStruct((1, hidden), jnp.float32),
        ),
        in_specs=[in_smem()] + [in_vmem()] * (far + 1),
        out_specs=(in_vmem(), in_vmem(), in_vmem()),
        scratch_shapes=[pltpu.VMEM((far,) + gradients.shape, jnp.bfloat16)],
        compiler_params=params,
        name="last_sums",
    )(lax.axis_index("yhi").reshape(1), arrived, *pieces)
    return (hidden_out, features_grad, weight_grad, bias_grad.reshape(hidden))


def solution(mesh):
    fine = Mesh(mesh.devices.reshape(row_split + col_split), axis_names)
    nodes_spec = P(row_axes + col_axes, None)
    in_specs = (
        nodes_spec,
        P(row_axes, col_axes, None),
        P(row_axes, col_axes, None),
        P(row_axes, col_axes),
        P(row_axes, col_axes, None, None, None),
        P(),
        P(),
        nodes_spec,
    )
    out_specs = (nodes_spec, nodes_spec, P(), P())
    return jax.shard_map(local, mesh=fine, in_specs=in_specs, out_specs=out_specs, check_vma=False)
```

```python
import math

import jax
import jax.numpy as jnp
from jax import lax
from jax.experimental import pallas as pl
from jax.experimental.pallas import tpu as pltpu
from jax.sharding import Mesh, PartitionSpec as P

row_split = (2, 2)
col_split = (4, 4, 12)
axis_names = ("ylo", "core", "yhi", "x", "z")
row_axes = ("ylo", "core")
col_axes = ("yhi", "x", "z")
team_axes = ("ylo", "core", "x")
group = 4
lanes = 128
vmem_bytes = 12 * 1024 * 1024
root_two_over_pi = math.sqrt(2.0 / math.pi)
cubic = 0.044715


def spread_out(value, axes, count):
    copies = jnp.broadcast_to(value[None], (count,) + value.shape)
    return lax.all_to_all(copies, axes, 0, 0, tiled=True)


def codes_kernel(here, places, *refs):
    out = refs[-1]
    across = places.shape[0]
    for source in range(across):
        place = places[lax.rem(here[0] - source + across, across)].astype(jnp.float32)
        place = place.astype(jnp.int32)
        mine = (place[0:1] == here[0]) | (place[0:1] == 254)
        out[pl.ds(source, 1), :] = jnp.where(mine, place[1:2] * 64 + place[2:3], -1)


def pick_tiles(codes, tile_refs, chosen, picked, slots, height, dummy):
    total = jnp.int32(0)
    for source, tiles in enumerate(tile_refs):

        def body(step, total, source=source, tiles=tiles):
            for sub in range(group):
                slot = step * group + sub
                code = codes[source, slot]
                top = pl.multiple_of(slot * height, height)
                chosen[total] = tiles[pl.ds(top, height), :]
                picked[total] = code
                total = total + jnp.where(code >= 0, 1, 0)
            return total

        total = lax.fori_loop(0, (codes[source, slots] + group - 1) // group, body, total)
    for sub in range(group):
        picked[total + sub] = dummy
    return total


def forward_kernel(codes, *refs, slots, height, blocks, far, across):
    lines, tile_refs = refs[:far], refs[far : far + across]
    out, slabs, chosen, totals, picked = refs[far + across :]
    slab_count = slabs.shape[0]
    near = slab_count // far
    for shift, line in enumerate(lines):
        slabs[pl.ds(shift * near, near)] = line[...]
    dummy = slab_count * 64 + blocks
    totals[...] = jnp.zeros_like(totals)
    total = pick_tiles(codes, tile_refs, chosen, picked, slots, height, dummy)

    def body(step, carry):
        products = []
        for sub in range(group):
            code = picked[step * group + sub]
            slab = jnp.minimum(code >> 6, slab_count - 1)
            product = jnp.dot(
                chosen[step * group + sub], slabs[slab], preferred_element_type=jnp.float32
            )
            products.append((code & 63, product))
        for block, product in products:
            totals[block] += product
        return carry

    lax.fori_loop(0, (total + group - 1) // group, body, 0)
    halves = out.shape[1] // height
    for block in range(blocks):
        out[block // halves, pl.ds((block % halves) * height, height), :] = totals[block].astype(
            jnp.bfloat16
        )


def split_wide(value):
    high = value.astype(jnp.bfloat16).astype(jnp.float32)
    return high, value - high


def bias_rows(pieces):
    rows = lax.broadcasted_iota(jnp.int32, (16, lanes), 0)
    block = jnp.zeros((16, lanes), jnp.float32)
    for index, piece in enumerate(pieces):
        block = jnp.where(rows == index, jnp.broadcast_to(piece, (16, lanes)), block)
    return block


def sum_rows(ref, start, size):
    value = ref[0, pl.ds(start, size), :].astype(jnp.float32)
    for index in range(1, ref.shape[0]):
        value = value + ref[index, pl.ds(start, size), :].astype(jnp.float32)
    return value


def dense_kernel(partials, weight, bias, cotangent, hidden, message):
    members = partials.shape[0]
    nodes = partials.shape[1]
    aggregate = sum_rows(partials, 0, nodes)
    weight_wide = weight[...].astype(jnp.float32)
    pre = (
        jnp.dot(
            aggregate,
            weight_wide,
            precision=lax.Precision.HIGHEST,
            preferred_element_type=jnp.float32,
        )
        + bias[...]
    )
    square = pre * pre
    angle = jnp.tanh(root_two_over_pi * (pre + cubic * (square * pre)))
    gate = 0.5 * (1.0 + angle)
    hidden[...] = (pre * gate).astype(jnp.bfloat16)
    inner = root_two_over_pi * (1.0 + 3.0 * cubic * square)
    gradient = gate + 0.5 * pre * (1.0 - angle * angle) * inner
    slope = (cotangent[...].astype(jnp.float32) * gradient).astype(jnp.bfloat16)
    slope_wide = slope.astype(jnp.float32)
    spread = lax.dot_general(
        slope, weight[...], (((1,), (1,)), ((), ())), preferred_element_type=jnp.float32
    ).astype(jnp.bfloat16)
    weight_part = lax.dot_general(
        aggregate,
        slope_wide,
        (((0,), (0,)), ((), ())),
        precision=lax.Precision.HIGHEST,
        preferred_element_type=jnp.float32,
    )
    bias_part = jnp.sum(slope_wide, axis=0, keepdims=True)
    high, low = split_wide(bias_part)
    bias_block = bias_rows([high[:, :lanes], high[:, lanes:], low[:, :lanes], low[:, lanes:]])
    bias_block = bias_block.astype(jnp.bfloat16)
    share = weight_part.shape[0] // members
    for member in range(members):
        message[member, pl.ds(0, nodes), :] = spread
        part = weight_part[member * share : (member + 1) * share]
        part = jnp.concatenate([part[:, :lanes], part[:, lanes:]], axis=0)
        high, low = split_wide(part)
        message[member, pl.ds(nodes, 2 * share), :] = high.astype(jnp.bfloat16)
        message[member, pl.ds(nodes + 2 * share, 2 * share), :] = low.astype(jnp.bfloat16)
        message[member, pl.ds(nodes + 4 * share, 16), :] = bias_block


def sum_bias(ref, start):
    block = sum_rows(ref, start, 16)
    return [block[0:1] + block[2:3], block[1:2] + block[3:4]]


def pack_bias(values):
    parts = [split_wide(value) for value in values]
    return bias_rows([parts[0][0], parts[1][0], parts[0][1], parts[1][1]]).astype(jnp.bfloat16)


def backward_kernel(codes, spreads, *refs, slots, height, blocks, nodes, share, far, across):
    tile_refs, outs = refs[:across], refs[across : across + far]
    shares, chosen, totals, picked = refs[across + far :]
    slab_count = totals.shape[0] - 1
    halves = nodes // height
    dummy = slab_count * 64 + blocks
    totals[...] = jnp.zeros_like(totals)
    total = pick_tiles(codes, tile_refs, chosen, picked, slots, height, dummy)

    def body(step, carry):
        products = []
        for sub in range(group):
            code = picked[step * group + sub]
            block = jnp.minimum(code & 63, blocks - 1)
            top = pl.multiple_of((block % halves) * height, height)
            product = lax.dot_general(
                chosen[step * group + sub],
                spreads[block // halves, pl.ds(top, height), :],
                (((0,), (0,)), ((), ())),
                preferred_element_type=jnp.float32,
            )
            products.append((code >> 6, product))
        for slab, product in products:
            totals[slab] += product
        return carry

    lax.fori_loop(0, (total + group - 1) // group, body, 0)
    near = slab_count // far
    for shift, out in enumerate(outs):
        for index in range(near):
            out[index] = totals[shift * near + index].astype(jnp.bfloat16)
    weight_sum = sum_rows(spreads, nodes, 2 * share) + sum_rows(spreads, nodes + 2 * share, 2 * share)
    high, low = split_wide(weight_sum)
    bias_block = pack_bias(sum_bias(spreads, nodes + 4 * share))
    for index in range(near):
        shares[index, pl.ds(0, 2 * share), :] = high.astype(jnp.bfloat16)
        shares[index, pl.ds(2 * share, 2 * share), :] = low.astype(jnp.bfloat16)
        shares[index, pl.ds(4 * share, 16), :] = bias_block


def share_kernel(arrived, out, bias_block, *, share):
    total = sum_rows(arrived, 0, 2 * share) + sum_rows(arrived, 2 * share, 2 * share)
    for index in range(out.shape[0]):
        out[index] = total
    bias_block[...] = pack_bias(sum_bias(arrived, 4 * share))


def gather_kernel(shares, bias_block, out, *, share):
    step = 16 // share if share < 16 else 1
    rows = shares.shape[0] * share
    for half in range(2):
        for first in range(0, shares.shape[0], step):
            parts = [shares[first + sub, pl.ds(half * share, share), :] for sub in range(step)]
            part = jnp.concatenate(parts, axis=0) if step > 1 else parts[0]
            out[pl.ds(half * rows + first * share, step * share), :] = part.astype(jnp.bfloat16)
    out[pl.ds(2 * rows, 16), :] = bias_block[...]


def middle_kernel(*refs, far):
    out = refs[-1]
    for index in range(out.shape[0]):
        total = refs[0][index].astype(jnp.float32)
        for line in refs[1:far]:
            total = total + line[index].astype(jnp.float32)
        out[index] = total.astype(jnp.bfloat16)


def last_kernel(arrived, pieces, grad, weight_grad, bias_grad, *, factor):
    grad[...] = sum_rows(arrived, 0, grad.shape[0])
    rows = weight_grad.shape[0]
    weight_grad[:, pl.ds(0, lanes)] = sum_rows(pieces, 0, rows) * factor
    weight_grad[:, pl.ds(lanes, lanes)] = sum_rows(pieces, rows, rows) * factor
    low, high = sum_bias(pieces, 2 * rows)
    bias_grad[:, pl.ds(0, lanes)] = low * factor
    bias_grad[:, pl.ds(lanes, lanes)] = high * factor


def in_vmem():
    return pl.BlockSpec(memory_space=pltpu.VMEM)


def in_smem():
    return pl.BlockSpec(memory_space=pltpu.SMEM)


def local(features, tile_rows, tile_cols, tile_counts, tile_values, weight, bias, cotangent):
    nodes, width = features.shape
    slots, height, tile_width = tile_values.shape[2:]
    hidden = weight.shape[1]
    far = lax.axis_size("yhi")
    across = lax.axis_size("x")
    near = lax.axis_size("z")
    members = lax.axis_size(team_axes)
    group_rows = lax.axis_size(row_axes)
    here = lax.axis_index("x")
    params = pltpu.CompilerParams(vmem_limit_bytes=vmem_bytes)
    halves = nodes // height
    blocks = members * halves

    def any_place():
        return pl.BlockSpec(memory_space=pl.ANY)

    live = jnp.arange(slots, dtype=jnp.int32) < tile_counts[0, 0]
    columns, rows = tile_cols[0, 0], tile_rows[0, 0]
    owner = jnp.where(live, (columns // near) % across, 255)
    distance = (lax.axis_index("yhi") - columns // (across * near)) % far
    slab = distance * near + columns % near
    block = ((rows // halves) * across + here) * halves + rows % halves
    places = jnp.stack([owner, slab, block])
    ends = jnp.stack([jnp.int32(254), jnp.int32(0), tile_counts[0, 0]])[:, None]
    places = jnp.concatenate([places, ends], axis=1)
    places = jnp.pad(places, ((0, 13), (0, lanes - slots - 1))).astype(jnp.bfloat16)
    places = lax.all_gather(places, "x", axis=0)

    def ring(size, shift):
        return [(start, (start + shift) % size) for start in range(size)]

    own = tile_values[0, 0].reshape(slots * height, tile_width)
    buffers = [own, lax.ppermute(own, "x", ring(across, 1))]
    for shift in range(2, across - 1):
        buffers.append(lax.ppermute(buffers[-1], "x", ring(across, 1)))
    if across > 2:
        buffers.append(lax.ppermute(own, "x", ring(across, -1)))

    lines = [spread_out(features, "z", near)]
    for shift in range(1, far):
        lines.append(lax.ppermute(lines[0], "yhi", ring(far, shift)))

    codes = pl.pallas_call(
        codes_kernel,
        out_shape=jax.ShapeDtypeStruct((across, lanes), jnp.int32),
        in_specs=[in_smem(), in_vmem()] + [any_place()] * (far - 1),
        out_specs=in_vmem(),
        compiler_params=params,
        name="tile_codes",
    )(here.reshape(1), places, *lines[1:])

    scratch_tiles = pltpu.VMEM((across * slots + group, height, tile_width), jnp.bfloat16)
    scratch_list = pltpu.SMEM((across * slots + group,), jnp.int32)
    partial = pl.pallas_call(
        lambda *refs: forward_kernel(*refs, slots=slots, height=height, blocks=blocks, far=far, across=across),
        out_shape=jax.ShapeDtypeStruct((members, nodes, width), jnp.bfloat16),
        in_specs=[in_smem()] + [in_vmem()] * (far + across),
        out_specs=in_vmem(),
        scratch_shapes=[
            pltpu.VMEM((far * near, nodes, width), jnp.bfloat16),
            scratch_tiles,
            pltpu.VMEM((blocks + 1, height, width), jnp.float32),
            scratch_list,
        ],
        compiler_params=params,
        name="forward_tiles",
    )(codes, *lines, *buffers)
    partials = lax.all_to_all(partial, team_axes, 0, 0, tiled=True)

    share = width // members
    hidden_out, message = pl.pallas_call(
        dense_kernel,
        out_shape=(
            jax.ShapeDtypeStruct((nodes, hidden), jnp.bfloat16),
            jax.ShapeDtypeStruct((members, nodes + 4 * share + 16, width), jnp.bfloat16),
        ),
        in_specs=[in_vmem()] * 4,
        out_specs=(in_vmem(), in_vmem()),
        compiler_params=params,
        name="dense_layer",
    )(partials, weight, bias.reshape(1, hidden), cotangent)
    spreads = lax.all_to_all(message, team_axes, 0, 0, tiled=True)

    outs = pl.pallas_call(
        lambda *refs: backward_kernel(
            *refs,
            slots=slots,
            height=height,
            blocks=blocks,
            nodes=nodes,
            share=share,
            far=far,
            across=across,
        ),
        out_shape=(jax.ShapeDtypeStruct((near, nodes, width), jnp.bfloat16),) * far
        + (jax.ShapeDtypeStruct((near, 4 * share + 16, width), jnp.bfloat16),),
        in_specs=[in_smem(), in_vmem()] + [in_vmem()] * across,
        out_specs=(in_vmem(),) * (far + 1),
        scratch_shapes=[
            scratch_tiles,
            pltpu.VMEM((far * near + 1, nodes, width), jnp.float32),
            scratch_list,
        ],
        compiler_params=params,
        name="backward_tiles",
    )(codes, spreads, *buffers)

    lines = [outs[0]]
    for shift in range(1, far):
        lines.append(lax.ppermute(outs[shift], "yhi", ring(far, -shift)))

    def gather_gradients(value):
        arrived = lax.all_to_all(value, "z", 0, 0, tiled=True)
        shares, bias_block = pl.pallas_call(
            lambda *refs: share_kernel(*refs, share=share),
            out_shape=(
                jax.ShapeDtypeStruct((members, 2 * share, lanes), jnp.float32),
                jax.ShapeDtypeStruct((16, lanes), jnp.bfloat16),
            ),
            in_specs=[in_vmem()],
            out_specs=(in_vmem(), in_vmem()),
            compiler_params=params,
            name="share_sum",
        )(arrived)
        shares = lax.all_to_all(shares, team_axes, 0, 0, tiled=True)
        return pl.pallas_call(
            lambda *refs: gather_kernel(*refs, share=share),
            out_shape=jax.ShapeDtypeStruct((2 * width + 16, lanes), jnp.bfloat16),
            in_specs=[in_vmem(), in_vmem()],
            out_specs=in_vmem(),
            compiler_params=params,
            name="share_gather",
        )(shares, bias_block)

    gradients = lax.cond(
        tile_counts[0, 0] > 0,
        gather_gradients,
        lambda value: jnp.zeros((2 * width + 16, lanes), jnp.bfloat16),
        outs[far],
    )
    line = pl.pallas_call(
        lambda *refs: middle_kernel(*refs, far=far),
        out_shape=jax.ShapeDtypeStruct((near, nodes, width), jnp.bfloat16),
        in_specs=[in_vmem()] * far + [any_place()],
        out_specs=in_vmem(),
        compiler_params=params,
        name="middle_sums",
    )(*lines, gradients)

    pieces = lax.all_gather(gradients, "yhi", axis=0)
    arrived = lax.all_to_all(line, "z", 0, 0, tiled=True)
    factor = 1.0 / math.sqrt(nodes * group_rows * far * across * near)
    features_grad, weight_grad, bias_grad = pl.pallas_call(
        lambda *refs: last_kernel(*refs, factor=factor),
        out_shape=(
            jax.ShapeDtypeStruct((nodes, width), jnp.float32),
            jax.ShapeDtypeStruct((width, hidden), jnp.float32),
            jax.ShapeDtypeStruct((1, hidden), jnp.float32),
        ),
        in_specs=[in_vmem(), in_vmem()],
        out_specs=(in_vmem(), in_vmem(), in_vmem()),
        compiler_params=params,
        name="last_sums",
    )(arrived, pieces)
    return (hidden_out, features_grad, weight_grad, bias_grad.reshape(hidden))


def solution(mesh):
    fine = Mesh(mesh.devices.reshape(row_split + col_split), axis_names)
    nodes_spec = P(row_axes + col_axes, None)
    in_specs = (
        nodes_spec,
        P(row_axes, col_axes, None),
        P(row_axes, col_axes, None),
        P(row_axes, col_axes),
        P(row_axes, col_axes, None, None, None),
        P(),
        P(),
        nodes_spec,
    )
    out_specs = (nodes_spec, nodes_spec, P(), P())
    return jax.shard_map(local, mesh=fine, in_specs=in_specs, out_specs=out_specs, check_vma=False)
```

```python
import math

import jax
import jax.numpy as jnp
from jax import lax
from jax.experimental import pallas as pl
from jax.experimental.pallas import tpu as pltpu
from jax.sharding import Mesh, PartitionSpec as P

row_split = (2, 2)
col_split = (4, 4, 12)
axis_names = ("ylo", "core", "yhi", "x", "z")
row_axes = ("ylo", "core")
col_axes = ("yhi", "x", "z")
team_axes = ("ylo", "core", "x")
back_rows = 112
group = 4
lanes = 128
vmem_bytes = 12 * 1024 * 1024
root_two_over_pi = math.sqrt(2.0 / math.pi)
cubic = 0.044715


def spread_out(value, axes, count):
    copies = jnp.broadcast_to(value[None], (count,) + value.shape)
    return lax.all_to_all(copies, axes, 0, 0, tiled=True)


def codes_kernel(here, places, *refs):
    out = refs[-1]
    across = places.shape[0]
    for source in range(across):
        place = places[lax.rem(here[0] - source + across, across)].astype(jnp.float32)
        place = place.astype(jnp.int32)
        mine = (place[0:1] == here[0]) | (place[0:1] == 254)
        out[pl.ds(source, 1), :] = jnp.where(mine, place[1:2] * 64 + place[2:3], -1)


def pick_tiles(codes, tile_refs, chosen, picked, slots, height, dummy):
    total = jnp.int32(0)
    for source, tiles in enumerate(tile_refs):

        def body(step, total, source=source, tiles=tiles):
            for sub in range(group):
                slot = step * group + sub
                code = codes[source, slot]
                top = pl.multiple_of(slot * height, height)
                chosen[total] = tiles[pl.ds(top, height), :]
                picked[total] = code
                total = total + jnp.where(code >= 0, 1, 0)
            return total

        total = lax.fori_loop(0, (codes[source, slots] + group - 1) // group, body, total)
    for sub in range(group):
        picked[total + sub] = dummy
    return total


def forward_kernel(codes, *refs, slots, height, blocks, line_order, across):
    far = len(line_order)
    lines, tile_refs = refs[:far], refs[far : far + across]
    out, slabs, chosen, totals, picked = refs[far + across :]
    slab_count = slabs.shape[0]
    near = slab_count // far
    for shift, line in zip(line_order, lines):
        slabs[pl.ds(shift * near, near)] = line[...]
    dummy = slab_count * 64 + blocks
    totals[...] = jnp.zeros_like(totals)
    total = pick_tiles(codes, tile_refs, chosen, picked, slots, height, dummy)

    def body(step, carry):
        products = []
        for sub in range(group):
            code = picked[step * group + sub]
            slab = jnp.minimum(code >> 6, slab_count - 1)
            product = jnp.dot(
                chosen[step * group + sub], slabs[slab], preferred_element_type=jnp.float32
            )
            products.append((code & 63, product))
        for block, product in products:
            totals[block] += product
        return carry

    lax.fori_loop(0, (total + group - 1) // group, body, 0)
    halves = out.shape[1] // height
    for block in range(blocks):
        out[block // halves, pl.ds((block % halves) * height, height), :] = totals[block].astype(
            jnp.bfloat16
        )


def split_wide(value):
    high = value.astype(jnp.bfloat16).astype(jnp.float32)
    return high, value - high


def bias_rows(pieces):
    rows = lax.broadcasted_iota(jnp.int32, (16, lanes), 0)
    block = jnp.zeros((16, lanes), jnp.float32)
    for index, piece in enumerate(pieces):
        block = jnp.where(rows == index, jnp.broadcast_to(piece, (16, lanes)), block)
    return block


def sum_rows(ref, start, size):
    value = ref[0, pl.ds(start, size), :].astype(jnp.float32)
    for index in range(1, ref.shape[0]):
        value = value + ref[index, pl.ds(start, size), :].astype(jnp.float32)
    return value


def dense_kernel(partials, weight, bias, cotangent, hidden, message):
    members = partials.shape[0]
    nodes = partials.shape[1]
    aggregate = sum_rows(partials, 0, nodes)
    weight_wide = weight[...].astype(jnp.float32)
    pre = (
        jnp.dot(
            aggregate,
            weight_wide,
            precision=lax.Precision.HIGHEST,
            preferred_element_type=jnp.float32,
        )
        + bias[...]
    )
    square = pre * pre
    angle = jnp.tanh(root_two_over_pi * (pre + cubic * (square * pre)))
    gate = 0.5 * (1.0 + angle)
    hidden[...] = (pre * gate).astype(jnp.bfloat16)
    inner = root_two_over_pi * (1.0 + 3.0 * cubic * square)
    gradient = gate + 0.5 * pre * (1.0 - angle * angle) * inner
    slope = (cotangent[...].astype(jnp.float32) * gradient).astype(jnp.bfloat16)
    slope_wide = slope.astype(jnp.float32)
    spread = lax.dot_general(
        slope, weight[...], (((1,), (1,)), ((), ())), preferred_element_type=jnp.float32
    ).astype(jnp.bfloat16)
    weight_part = lax.dot_general(
        aggregate,
        slope_wide,
        (((0,), (0,)), ((), ())),
        precision=lax.Precision.HIGHEST,
        preferred_element_type=jnp.float32,
    )
    bias_part = jnp.sum(slope_wide, axis=0, keepdims=True)
    high, low = split_wide(bias_part)
    bias_block = bias_rows([high[:, :lanes], high[:, lanes:], low[:, :lanes], low[:, lanes:]])
    bias_block = bias_block.astype(jnp.bfloat16)
    share = weight_part.shape[0] // members
    for member in range(members):
        message[member, pl.ds(0, nodes), :] = spread
        part = weight_part[member * share : (member + 1) * share]
        part = jnp.concatenate([part[:, :lanes], part[:, lanes:]], axis=0)
        high, low = split_wide(part)
        message[member, pl.ds(nodes, 2 * share), :] = high.astype(jnp.bfloat16)
        message[member, pl.ds(nodes + 2 * share, 2 * share), :] = low.astype(jnp.bfloat16)
        message[member, pl.ds(nodes + 4 * share, 16), :] = bias_block


def sum_bias(ref, start):
    block = sum_rows(ref, start, 16)
    return [block[0:1] + block[2:3], block[1:2] + block[3:4]]


def pack_bias(values):
    parts = [split_wide(value) for value in values]
    return bias_rows([parts[0][0], parts[1][0], parts[0][1], parts[1][1]]).astype(jnp.bfloat16)


def backward_kernel(codes, spreads, *refs, slots, height, blocks, nodes, share, far, across):
    tile_refs, outs = refs[:across], refs[across : across + far]
    shares, chosen, totals, picked = refs[across + far :]
    slab_count = totals.shape[0] - 1
    halves = nodes // height
    dummy = slab_count * 64 + blocks
    totals[...] = jnp.zeros_like(totals)
    total = pick_tiles(codes, tile_refs, chosen, picked, slots, height, dummy)

    def body(step, carry):
        products = []
        for sub in range(group):
            code = picked[step * group + sub]
            block = jnp.minimum(code & 63, blocks - 1)
            top = pl.multiple_of((block % halves) * height, height)
            product = lax.dot_general(
                chosen[step * group + sub],
                spreads[block // halves, pl.ds(top, height), :],
                (((0,), (0,)), ((), ())),
                preferred_element_type=jnp.float32,
            )
            products.append((code >> 6, product))
        for slab, product in products:
            totals[slab] += product
        return carry

    lax.fori_loop(0, (total + group - 1) // group, body, 0)
    near = slab_count // far
    ahead = outs[0].shape[1]
    rest = nodes - ahead
    for shift, out in enumerate(outs):
        for index in range(near):
            total = totals[shift * near + index].astype(jnp.bfloat16)
            out[index] = total[:ahead]
            shares[index, pl.ds(4 * share + 16 + shift * rest, rest), :] = total[ahead:]
    weight_sum = sum_rows(spreads, nodes, 2 * share) + sum_rows(spreads, nodes + 2 * share, 2 * share)
    high, low = split_wide(weight_sum)
    bias_block = pack_bias(sum_bias(spreads, nodes + 4 * share))
    for index in range(near):
        shares[index, pl.ds(0, 2 * share), :] = high.astype(jnp.bfloat16)
        shares[index, pl.ds(2 * share, 2 * share), :] = low.astype(jnp.bfloat16)
        shares[index, pl.ds(4 * share, 16), :] = bias_block


def share_kernel(arrived, out, bias_block, rest_sums, *, share):
    total = sum_rows(arrived, 0, 2 * share) + sum_rows(arrived, 2 * share, 2 * share)
    for index in range(out.shape[0]):
        out[index] = total
    bias_block[...] = pack_bias(sum_bias(arrived, 4 * share))
    rest_sums[...] = sum_rows(arrived, 4 * share + 16, rest_sums.shape[0]).astype(jnp.bfloat16)


def gather_kernel(shares, bias_block, rest_sums, *outs, share):
    step = 16 // share if share < 16 else 1
    rows = shares.shape[0] * share
    rest = rest_sums.shape[0] // len(outs)
    for half in range(2):
        for first in range(0, shares.shape[0], step):
            parts = [shares[first + sub, pl.ds(half * share, share), :] for sub in range(step)]
            part = jnp.concatenate(parts, axis=0) if step > 1 else parts[0]
            for out in outs:
                out[pl.ds(half * rows + first * share, step * share), :] = part.astype(jnp.bfloat16)
    for shift, out in enumerate(outs):
        out[pl.ds(2 * rows, 16), :] = bias_block[...]
        out[pl.ds(2 * rows + 16, rest), :] = rest_sums[pl.ds(shift * rest, rest), :]


def middle_kernel(*refs, far):
    out = refs[-1]
    for index in range(out.shape[0]):
        total = refs[0][index].astype(jnp.float32)
        for line in refs[1:far]:
            total = total + line[index].astype(jnp.float32)
        out[index] = total.astype(jnp.bfloat16)


def last_kernel(place, arrived, *refs, far, factor):
    grad, weight_grad, bias_grad, stack = refs[far:]
    ahead = arrived.shape[1]
    rest = grad.shape[0] - ahead
    for shift, piece in enumerate(refs[:far]):
        stack[lax.rem(place[0] + shift, far)] = piece[...]
    rows = weight_grad.shape[0]
    weight_grad[:, pl.ds(0, lanes)] = sum_rows(stack, 0, rows) * factor
    weight_grad[:, pl.ds(lanes, lanes)] = sum_rows(stack, rows, rows) * factor
    low, high = sum_bias(stack, 2 * rows)
    bias_grad[:, pl.ds(0, lanes)] = low * factor
    bias_grad[:, pl.ds(lanes, lanes)] = high * factor
    grad[pl.ds(0, ahead), :] = sum_rows(arrived, 0, ahead)
    grad[pl.ds(ahead, rest), :] = sum_rows(stack, 2 * rows + 16, rest)


def in_vmem():
    return pl.BlockSpec(memory_space=pltpu.VMEM)


def in_smem():
    return pl.BlockSpec(memory_space=pltpu.SMEM)


def local(features, tile_rows, tile_cols, tile_counts, tile_values, weight, bias, cotangent):
    nodes, width = features.shape
    slots, height, tile_width = tile_values.shape[2:]
    hidden = weight.shape[1]
    far = lax.axis_size("yhi")
    across = lax.axis_size("x")
    near = lax.axis_size("z")
    members = lax.axis_size(team_axes)
    group_rows = lax.axis_size(row_axes)
    here = lax.axis_index("x")
    params = pltpu.CompilerParams(vmem_limit_bytes=vmem_bytes)
    halves = nodes // height
    blocks = members * halves

    def any_place():
        return pl.BlockSpec(memory_space=pl.ANY)

    live = jnp.arange(slots, dtype=jnp.int32) < tile_counts[0, 0]
    columns, rows = tile_cols[0, 0], tile_rows[0, 0]
    owner = jnp.where(live, (columns // near) % across, 255)
    distance = (lax.axis_index("yhi") - columns // (across * near)) % far
    slab = distance * near + columns % near
    block = ((rows // halves) * across + here) * halves + rows % halves
    places = jnp.stack([owner, slab, block])
    ends = jnp.stack([jnp.int32(254), jnp.int32(0), tile_counts[0, 0]])[:, None]
    places = jnp.concatenate([places, ends], axis=1)
    places = jnp.pad(places, ((0, 13), (0, lanes - slots - 1))).astype(jnp.bfloat16)
    places = lax.all_gather(places, "x", axis=0)

    def ring(size, shift):
        return [(start, (start + shift) % size) for start in range(size)]

    longest_first = sorted(range(1, far), key=lambda shift: -min(shift, far - shift))

    own = tile_values[0, 0].reshape(slots * height, tile_width)
    buffers = [own, lax.ppermute(own, "x", ring(across, 1))]
    for shift in range(2, across - 1):
        buffers.append(lax.ppermute(buffers[-1], "x", ring(across, 1)))
    if across > 2:
        buffers.append(lax.ppermute(own, "x", ring(across, -1)))

    lines = [spread_out(features, "z", near)]
    line_order = [0] + longest_first[::-1]
    for shift in line_order[1:]:
        lines.append(lax.ppermute(lines[0], "yhi", ring(far, shift)))

    codes = pl.pallas_call(
        codes_kernel,
        out_shape=jax.ShapeDtypeStruct((across, lanes), jnp.int32),
        in_specs=[in_smem(), in_vmem()] + [any_place()] * (far - 1),
        out_specs=in_vmem(),
        compiler_params=params,
        name="tile_codes",
    )(here.reshape(1), places, *lines[1:])

    scratch_tiles = pltpu.VMEM((across * slots + group, height, tile_width), jnp.bfloat16)
    scratch_list = pltpu.SMEM((across * slots + group,), jnp.int32)
    partial = pl.pallas_call(
        lambda *refs: forward_kernel(
            *refs,
            slots=slots,
            height=height,
            blocks=blocks,
            line_order=line_order,
            across=across,
        ),
        out_shape=jax.ShapeDtypeStruct((members, nodes, width), jnp.bfloat16),
        in_specs=[in_smem()] + [in_vmem()] * (far + across),
        out_specs=in_vmem(),
        scratch_shapes=[
            pltpu.VMEM((far * near, nodes, width), jnp.bfloat16),
            scratch_tiles,
            pltpu.VMEM((blocks + 1, height, width), jnp.float32),
            scratch_list,
        ],
        compiler_params=params,
        name="forward_tiles",
    )(codes, *lines, *buffers)
    partials = lax.all_to_all(partial, team_axes, 0, 0, tiled=True)

    share = width // members
    hidden_out, message = pl.pallas_call(
        dense_kernel,
        out_shape=(
            jax.ShapeDtypeStruct((nodes, hidden), jnp.bfloat16),
            jax.ShapeDtypeStruct((members, nodes + 4 * share + 16, width), jnp.bfloat16),
        ),
        in_specs=[in_vmem()] * 4,
        out_specs=(in_vmem(), in_vmem()),
        compiler_params=params,
        name="dense_layer",
    )(partials, weight, bias.reshape(1, hidden), cotangent)
    spreads = lax.all_to_all(message, team_axes, 0, 0, tiled=True)

    rest = nodes - back_rows
    outs = pl.pallas_call(
        lambda *refs: backward_kernel(
            *refs,
            slots=slots,
            height=height,
            blocks=blocks,
            nodes=nodes,
            share=share,
            far=far,
            across=across,
        ),
        out_shape=(jax.ShapeDtypeStruct((near, back_rows, width), jnp.bfloat16),) * far
        + (jax.ShapeDtypeStruct((near, 4 * share + 16 + far * rest, width), jnp.bfloat16),),
        in_specs=[in_smem(), in_vmem()] + [in_vmem()] * across,
        out_specs=(in_vmem(),) * (far + 1),
        scratch_shapes=[
            scratch_tiles,
            pltpu.VMEM((far * near + 1, nodes, width), jnp.float32),
            scratch_list,
        ],
        compiler_params=params,
        name="backward_tiles",
    )(codes, spreads, *buffers)

    lines = [outs[0]]
    for shift in longest_first:
        lines.append(lax.ppermute(outs[shift], "yhi", ring(far, -shift)))

    gradients_shape = (2 * width + 16 + rest, lanes)

    def gather_gradients(value):
        arrived = lax.all_to_all(value, "z", 0, 0, tiled=True)
        shares, bias_block, rest_sums = pl.pallas_call(
            lambda *refs: share_kernel(*refs, share=share),
            out_shape=(
                jax.ShapeDtypeStruct((members, 2 * share, lanes), jnp.float32),
                jax.ShapeDtypeStruct((16, lanes), jnp.bfloat16),
                jax.ShapeDtypeStruct((far * rest, width), jnp.bfloat16),
            ),
            in_specs=[in_vmem()],
            out_specs=(in_vmem(), in_vmem(), in_vmem()),
            compiler_params=params,
            name="share_sum",
        )(arrived)
        shares = lax.all_to_all(shares, team_axes, 0, 0, tiled=True)
        return pl.pallas_call(
            lambda *refs: gather_kernel(*refs, share=share),
            out_shape=(jax.ShapeDtypeStruct(gradients_shape, jnp.bfloat16),) * far,
            in_specs=[in_vmem()] * 3,
            out_specs=(in_vmem(),) * far,
            compiler_params=params,
            name="share_gather",
        )(shares, bias_block, rest_sums)

    gradients = lax.cond(
        tile_counts[0, 0] > 0,
        gather_gradients,
        lambda value: (jnp.zeros(gradients_shape, jnp.bfloat16),) * far,
        outs[far],
    )
    line = pl.pallas_call(
        lambda *refs: middle_kernel(*refs, far=far),
        out_shape=jax.ShapeDtypeStruct((near, back_rows, width), jnp.bfloat16),
        in_specs=[in_vmem()] * far + [any_place()],
        out_specs=in_vmem(),
        compiler_params=params,
        name="middle_sums",
    )(*lines, gradients[0])

    pieces = [gradients[0]]
    for shift in range(1, far):
        pieces.append(lax.ppermute(gradients[shift], "yhi", ring(far, -shift)))
    arrived = lax.all_to_all(line, "z", 0, 0, tiled=True)
    factor = 1.0 / math.sqrt(nodes * group_rows * far * across * near)
    features_grad, weight_grad, bias_grad = pl.pallas_call(
        lambda *refs: last_kernel(*refs, far=far, factor=factor),
        out_shape=(
            jax.ShapeDtypeStruct((nodes, width), jnp.float32),
            jax.ShapeDtypeStruct((width, hidden), jnp.float32),
            jax.ShapeDtypeStruct((1, hidden), jnp.float32),
        ),
        in_specs=[in_smem()] + [in_vmem()] * (far + 1),
        out_specs=(in_vmem(), in_vmem(), in_vmem()),
        scratch_shapes=[pltpu.VMEM((far,) + gradients_shape, jnp.bfloat16)],
        compiler_params=params,
        name="last_sums",
    )(lax.axis_index("yhi").reshape(1), arrived, *pieces)
    return (hidden_out, features_grad, weight_grad, bias_grad.reshape(hidden))


def solution(mesh):
    fine = Mesh(mesh.devices.reshape(row_split + col_split), axis_names)
    nodes_spec = P(row_axes + col_axes, None)
    in_specs = (
        nodes_spec,
        P(row_axes, col_axes, None),
        P(row_axes, col_axes, None),
        P(row_axes, col_axes),
        P(row_axes, col_axes, None, None, None),
        P(),
        P(),
        nodes_spec,
    )
    out_specs = (nodes_spec, nodes_spec, P(), P())
    return jax.shard_map(local, mesh=fine, in_specs=in_specs, out_specs=out_specs, check_vma=False)
```

```python
import math

import jax
import jax.numpy as jnp
from jax import lax
from jax.experimental import pallas as pl
from jax.experimental.pallas import tpu as pltpu
from jax.sharding import Mesh, PartitionSpec as P

row_split = (2, 2)
col_split = (4, 4, 12)
axis_names = ("ylo", "core", "yhi", "x", "z")
row_axes = ("ylo", "core")
col_axes = ("yhi", "x", "z")
team_axes = ("ylo", "core", "x")
group = 4
lanes = 128
vmem_bytes = 12 * 1024 * 1024
root_two_over_pi = math.sqrt(2.0 / math.pi)
cubic = 0.044715


def spread_out(value, axes, count):
    copies = jnp.broadcast_to(value[None], (count,) + value.shape)
    return lax.all_to_all(copies, axes, 0, 0, tiled=True)


def codes_kernel(here, places, *refs):
    out = refs[-1]
    across = places.shape[0]
    for source in range(across):
        place = places[lax.rem(here[0] - source + across, across)].astype(jnp.float32)
        place = place.astype(jnp.int32)
        mine = (place[0:1] == here[0]) | (place[0:1] == 254)
        out[pl.ds(source, 1), :] = jnp.where(mine, place[1:2] * 64 + place[2:3], -1)


def pick_tiles(codes, tile_refs, chosen, picked, slots, height, dummy):
    total = jnp.int32(0)
    for source, tiles in enumerate(tile_refs):

        def body(step, total, source=source, tiles=tiles):
            for sub in range(group):
                slot = step * group + sub
                code = codes[source, slot]
                top = pl.multiple_of(slot * height, height)
                chosen[total] = tiles[pl.ds(top, height), :]
                picked[total] = code
                total = total + jnp.where(code >= 0, 1, 0)
            return total

        total = lax.fori_loop(0, (codes[source, slots] + group - 1) // group, body, total)
    for sub in range(group):
        picked[total + sub] = dummy
    return total


def forward_kernel(codes, *refs, slots, height, blocks, line_order, across):
    far = len(line_order)
    lines, tile_refs = refs[:far], refs[far : far + across]
    out, slabs, chosen, totals, picked = refs[far + across :]
    slab_count = slabs.shape[0]
    near = slab_count // far
    for shift, line in zip(line_order, lines):
        slabs[pl.ds(shift * near, near)] = line[...]
    dummy = slab_count * 64 + blocks
    totals[...] = jnp.zeros_like(totals)
    total = pick_tiles(codes, tile_refs, chosen, picked, slots, height, dummy)

    def body(step, carry):
        products = []
        for sub in range(group):
            code = picked[step * group + sub]
            slab = jnp.minimum(code >> 6, slab_count - 1)
            product = jnp.dot(
                chosen[step * group + sub], slabs[slab], preferred_element_type=jnp.float32
            )
            products.append((code & 63, product))
        for block, product in products:
            totals[block] += product
        return carry

    lax.fori_loop(0, (total + group - 1) // group, body, 0)
    halves = out.shape[1] // height
    for block in range(blocks):
        out[block // halves, pl.ds((block % halves) * height, height), :] = totals[block].astype(
            jnp.bfloat16
        )


def split_wide(value):
    high = value.astype(jnp.bfloat16).astype(jnp.float32)
    return high, value - high


def bias_rows(pieces):
    rows = lax.broadcasted_iota(jnp.int32, (16, lanes), 0)
    block = jnp.zeros((16, lanes), jnp.float32)
    for index, piece in enumerate(pieces):
        block = jnp.where(rows == index, jnp.broadcast_to(piece, (16, lanes)), block)
    return block


def sum_rows(ref, start, size):
    value = ref[0, pl.ds(start, size), :].astype(jnp.float32)
    for index in range(1, ref.shape[0]):
        value = value + ref[index, pl.ds(start, size), :].astype(jnp.float32)
    return value


def dense_kernel(partials, weight, bias, cotangent, hidden, message):
    members = partials.shape[0]
    nodes = partials.shape[1]
    aggregate = sum_rows(partials, 0, nodes)
    weight_wide = weight[...].astype(jnp.float32)
    pre = (
        jnp.dot(
            aggregate,
            weight_wide,
            precision=lax.Precision.HIGHEST,
            preferred_element_type=jnp.float32,
        )
        + bias[...]
    )
    square = pre * pre
    angle = jnp.tanh(root_two_over_pi * (pre + cubic * (square * pre)))
    gate = 0.5 * (1.0 + angle)
    hidden[...] = (pre * gate).astype(jnp.bfloat16)
    inner = root_two_over_pi * (1.0 + 3.0 * cubic * square)
    gradient = gate + 0.5 * pre * (1.0 - angle * angle) * inner
    slope = (cotangent[...].astype(jnp.float32) * gradient).astype(jnp.bfloat16)
    slope_wide = slope.astype(jnp.float32)
    spread = lax.dot_general(
        slope, weight[...], (((1,), (1,)), ((), ())), preferred_element_type=jnp.float32
    ).astype(jnp.bfloat16)
    weight_part = lax.dot_general(
        aggregate,
        slope_wide,
        (((0,), (0,)), ((), ())),
        precision=lax.Precision.HIGHEST,
        preferred_element_type=jnp.float32,
    )
    bias_part = jnp.sum(slope_wide, axis=0, keepdims=True)
    high, low = split_wide(bias_part)
    bias_block = bias_rows([high[:, :lanes], high[:, lanes:], low[:, :lanes], low[:, lanes:]])
    bias_block = bias_block.astype(jnp.bfloat16)
    share = weight_part.shape[0] // members
    for member in range(members):
        message[member, pl.ds(0, nodes), :] = spread
        part = weight_part[member * share : (member + 1) * share]
        part = jnp.concatenate([part[:, :lanes], part[:, lanes:]], axis=0)
        high, low = split_wide(part)
        message[member, pl.ds(nodes, 2 * share), :] = high.astype(jnp.bfloat16)
        message[member, pl.ds(nodes + 2 * share, 2 * share), :] = low.astype(jnp.bfloat16)
        message[member, pl.ds(nodes + 4 * share, 16), :] = bias_block


def sum_bias(ref, start):
    block = sum_rows(ref, start, 16)
    return [block[0:1] + block[2:3], block[1:2] + block[3:4]]


def pack_bias(values):
    parts = [split_wide(value) for value in values]
    return bias_rows([parts[0][0], parts[1][0], parts[0][1], parts[1][1]]).astype(jnp.bfloat16)


def backward_kernel(codes, spreads, *refs, slots, height, blocks, nodes, share, far, across):
    tile_refs, outs = refs[:across], refs[across : across + far]
    shares, chosen, totals, picked = refs[across + far :]
    slab_count = totals.shape[0] - 1
    halves = nodes // height
    dummy = slab_count * 64 + blocks
    totals[...] = jnp.zeros_like(totals)
    total = pick_tiles(codes, tile_refs, chosen, picked, slots, height, dummy)

    def body(step, carry):
        products = []
        for sub in range(group):
            code = picked[step * group + sub]
            block = jnp.minimum(code & 63, blocks - 1)
            top = pl.multiple_of((block % halves) * height, height)
            product = lax.dot_general(
                chosen[step * group + sub],
                spreads[block // halves, pl.ds(top, height), :],
                (((0,), (0,)), ((), ())),
                preferred_element_type=jnp.float32,
            )
            products.append((code >> 6, product))
        for slab, product in products:
            totals[slab] += product
        return carry

    lax.fori_loop(0, (total + group - 1) // group, body, 0)
    near = slab_count // far
    for shift, out in enumerate(outs):
        for index in range(near):
            out[index] = totals[shift * near + index].astype(jnp.bfloat16)
    weight_sum = sum_rows(spreads, nodes, 2 * share) + sum_rows(spreads, nodes + 2 * share, 2 * share)
    high, low = split_wide(weight_sum)
    bias_block = pack_bias(sum_bias(spreads, nodes + 4 * share))
    for index in range(near):
        shares[index, pl.ds(0, 2 * share), :] = high.astype(jnp.bfloat16)
        shares[index, pl.ds(2 * share, 2 * share), :] = low.astype(jnp.bfloat16)
        shares[index, pl.ds(4 * share, 16), :] = bias_block


def share_kernel(arrived, out, bias_block, *, share):
    total = sum_rows(arrived, 0, 2 * share) + sum_rows(arrived, 2 * share, 2 * share)
    for index in range(out.shape[0]):
        out[index] = total
    bias_block[...] = pack_bias(sum_bias(arrived, 4 * share))


def gather_kernel(shares, bias_block, out, *, share):
    step = 16 // share if share < 16 else 1
    rows = shares.shape[0] * share
    for half in range(2):
        for first in range(0, shares.shape[0], step):
            parts = [shares[first + sub, pl.ds(half * share, share), :] for sub in range(step)]
            part = jnp.concatenate(parts, axis=0) if step > 1 else parts[0]
            out[pl.ds(half * rows + first * share, step * share), :] = part.astype(jnp.bfloat16)
    out[pl.ds(2 * rows, 16), :] = bias_block[...]


def middle_kernel(*refs, far):
    out = refs[-1]
    for index in range(out.shape[0]):
        total = refs[0][index].astype(jnp.float32)
        for line in refs[1:far]:
            total = total + line[index].astype(jnp.float32)
        out[index] = total.astype(jnp.bfloat16)


def last_kernel(arrived, pieces, grad, weight_grad, bias_grad, *, factor):
    grad[...] = sum_rows(arrived, 0, grad.shape[0])
    rows = weight_grad.shape[0]
    weight_grad[:, pl.ds(0, lanes)] = sum_rows(pieces, 0, rows) * factor
    weight_grad[:, pl.ds(lanes, lanes)] = sum_rows(pieces, rows, rows) * factor
    low, high = sum_bias(pieces, 2 * rows)
    bias_grad[:, pl.ds(0, lanes)] = low * factor
    bias_grad[:, pl.ds(lanes, lanes)] = high * factor


def in_vmem():
    return pl.BlockSpec(memory_space=pltpu.VMEM)


def in_smem():
    return pl.BlockSpec(memory_space=pltpu.SMEM)


def local(features, tile_rows, tile_cols, tile_counts, tile_values, weight, bias, cotangent):
    nodes, width = features.shape
    slots, height, tile_width = tile_values.shape[2:]
    hidden = weight.shape[1]
    far = lax.axis_size("yhi")
    across = lax.axis_size("x")
    near = lax.axis_size("z")
    members = lax.axis_size(team_axes)
    group_rows = lax.axis_size(row_axes)
    here = lax.axis_index("x")
    params = pltpu.CompilerParams(vmem_limit_bytes=vmem_bytes)
    halves = nodes // height
    blocks = members * halves

    def any_place():
        return pl.BlockSpec(memory_space=pl.ANY)

    live = jnp.arange(slots, dtype=jnp.int32) < tile_counts[0, 0]
    columns, rows = tile_cols[0, 0], tile_rows[0, 0]
    owner = jnp.where(live, (columns // near) % across, 255)
    distance = (lax.axis_index("yhi") - columns // (across * near)) % far
    slab = distance * near + columns % near
    block = ((rows // halves) * across + here) * halves + rows % halves
    places = jnp.stack([owner, slab, block])
    ends = jnp.stack([jnp.int32(254), jnp.int32(0), tile_counts[0, 0]])[:, None]
    places = jnp.concatenate([places, ends], axis=1)
    places = jnp.pad(places, ((0, 13), (0, lanes - slots - 1))).astype(jnp.bfloat16)
    places = lax.all_gather(places, "x", axis=0)

    def ring(size, shift):
        return [(start, (start + shift) % size) for start in range(size)]

    longest_first = sorted(range(1, far), key=lambda shift: -min(shift, far - shift))

    own = tile_values[0, 0].reshape(slots * height, tile_width)
    buffers = [own, lax.ppermute(own, "x", ring(across, 1))]
    for shift in range(2, across - 1):
        buffers.append(lax.ppermute(buffers[-1], "x", ring(across, 1)))
    if across > 2:
        buffers.append(lax.ppermute(own, "x", ring(across, -1)))

    lines = [spread_out(features, "z", near)]
    line_order = [0] + longest_first[::-1]
    for shift in line_order[1:]:
        lines.append(lax.ppermute(lines[0], "yhi", ring(far, shift)))

    codes = pl.pallas_call(
        codes_kernel,
        out_shape=jax.ShapeDtypeStruct((across, lanes), jnp.int32),
        in_specs=[in_smem(), in_vmem()] + [any_place()] * (far - 1),
        out_specs=in_vmem(),
        compiler_params=params,
        name="tile_codes",
    )(here.reshape(1), places, *lines[1:])

    scratch_tiles = pltpu.VMEM((across * slots + group, height, tile_width), jnp.bfloat16)
    scratch_list = pltpu.SMEM((across * slots + group,), jnp.int32)
    partial = pl.pallas_call(
        lambda *refs: forward_kernel(
            *refs,
            slots=slots,
            height=height,
            blocks=blocks,
            line_order=line_order,
            across=across,
        ),
        out_shape=jax.ShapeDtypeStruct((members, nodes, width), jnp.bfloat16),
        in_specs=[in_smem()] + [in_vmem()] * (far + across),
        out_specs=in_vmem(),
        scratch_shapes=[
            pltpu.VMEM((far * near, nodes, width), jnp.bfloat16),
            scratch_tiles,
            pltpu.VMEM((blocks + 1, height, width), jnp.float32),
            scratch_list,
        ],
        compiler_params=params,
        name="forward_tiles",
    )(codes, *lines, *buffers)
    partials = lax.all_to_all(partial, team_axes, 0, 0, tiled=True)

    share = width // members
    hidden_out, message = pl.pallas_call(
        dense_kernel,
        out_shape=(
            jax.ShapeDtypeStruct((nodes, hidden), jnp.bfloat16),
            jax.ShapeDtypeStruct((members, nodes + 4 * share + 16, width), jnp.bfloat16),
        ),
        in_specs=[in_vmem()] * 4,
        out_specs=(in_vmem(), in_vmem()),
        compiler_params=params,
        name="dense_layer",
    )(partials, weight, bias.reshape(1, hidden), cotangent)
    spreads = lax.all_to_all(message, team_axes, 0, 0, tiled=True)

    outs = pl.pallas_call(
        lambda *refs: backward_kernel(
            *refs,
            slots=slots,
            height=height,
            blocks=blocks,
            nodes=nodes,
            share=share,
            far=far,
            across=across,
        ),
        out_shape=(jax.ShapeDtypeStruct((near, nodes, width), jnp.bfloat16),) * far
        + (jax.ShapeDtypeStruct((near, 4 * share + 16, width), jnp.bfloat16),),
        in_specs=[in_smem(), in_vmem()] + [in_vmem()] * across,
        out_specs=(in_vmem(),) * (far + 1),
        scratch_shapes=[
            scratch_tiles,
            pltpu.VMEM((far * near + 1, nodes, width), jnp.float32),
            scratch_list,
        ],
        compiler_params=params,
        name="backward_tiles",
    )(codes, spreads, *buffers)

    lines = [outs[0]]
    for shift in longest_first:
        lines.append(lax.ppermute(outs[shift], "yhi", ring(far, -shift)))

    def gather_gradients(value):
        arrived = lax.all_to_all(value, "z", 0, 0, tiled=True)
        shares, bias_block = pl.pallas_call(
            lambda *refs: share_kernel(*refs, share=share),
            out_shape=(
                jax.ShapeDtypeStruct((members, 2 * share, lanes), jnp.float32),
                jax.ShapeDtypeStruct((16, lanes), jnp.bfloat16),
            ),
            in_specs=[in_vmem()],
            out_specs=(in_vmem(), in_vmem()),
            compiler_params=params,
            name="share_sum",
        )(arrived)
        shares = lax.all_to_all(shares, team_axes, 0, 0, tiled=True)
        return pl.pallas_call(
            lambda *refs: gather_kernel(*refs, share=share),
            out_shape=jax.ShapeDtypeStruct((2 * width + 16, lanes), jnp.bfloat16),
            in_specs=[in_vmem(), in_vmem()],
            out_specs=in_vmem(),
            compiler_params=params,
            name="share_gather",
        )(shares, bias_block)

    gradients = lax.cond(
        tile_counts[0, 0] > 0,
        gather_gradients,
        lambda value: jnp.zeros((2 * width + 16, lanes), jnp.bfloat16),
        outs[far],
    )
    line = pl.pallas_call(
        lambda *refs: middle_kernel(*refs, far=far),
        out_shape=jax.ShapeDtypeStruct((near, nodes, width), jnp.bfloat16),
        in_specs=[in_vmem()] * far + [any_place()],
        out_specs=in_vmem(),
        compiler_params=params,
        name="middle_sums",
    )(*lines, gradients)

    pieces = lax.all_gather(gradients, "yhi", axis=0)
    arrived = lax.all_to_all(line, "z", 0, 0, tiled=True)
    factor = 1.0 / math.sqrt(nodes * group_rows * far * across * near)
    features_grad, weight_grad, bias_grad = pl.pallas_call(
        lambda *refs: last_kernel(*refs, factor=factor),
        out_shape=(
            jax.ShapeDtypeStruct((nodes, width), jnp.float32),
            jax.ShapeDtypeStruct((width, hidden), jnp.float32),
            jax.ShapeDtypeStruct((1, hidden), jnp.float32),
        ),
        in_specs=[in_vmem(), in_vmem()],
        out_specs=(in_vmem(), in_vmem(), in_vmem()),
        compiler_params=params,
        name="last_sums",
    )(arrived, pieces)
    return (hidden_out, features_grad, weight_grad, bias_grad.reshape(hidden))


def solution(mesh):
    fine = Mesh(mesh.devices.reshape(row_split + col_split), axis_names)
    nodes_spec = P(row_axes + col_axes, None)
    in_specs = (
        nodes_spec,
        P(row_axes, col_axes, None),
        P(row_axes, col_axes, None),
        P(row_axes, col_axes),
        P(row_axes, col_axes, None, None, None),
        P(),
        P(),
        nodes_spec,
    )
    out_specs = (nodes_spec, nodes_spec, P(), P())
    return jax.shard_map(local, mesh=fine, in_specs=in_specs, out_specs=out_specs, check_vma=False)
```

```python
import math

import jax
import jax.numpy as jnp
from jax import lax
from jax.experimental import pallas as pl
from jax.experimental.pallas import tpu as pltpu
from jax.sharding import Mesh, PartitionSpec as P

row_split = (2, 2)
col_split = (4, 4, 12)
axis_names = ("ylo", "core", "yhi", "x", "z")
row_axes = ("ylo", "core")
col_axes = ("yhi", "x", "z")
team_axes = ("ylo", "core", "x")
group = 4
lanes = 128
vmem_bytes = 12 * 1024 * 1024
root_two_over_pi = math.sqrt(2.0 / math.pi)
cubic = 0.044715


def spread_out(value, axes, count):
    copies = jnp.broadcast_to(value[None], (count,) + value.shape)
    return lax.all_to_all(copies, axes, 0, 0, tiled=True)


def codes_kernel(here, *refs, across, top):
    out = refs[-1]
    for source in range(across):
        places = refs[source][pl.ds(top, 16), :].astype(jnp.float32).astype(jnp.int32)
        mine = (places[0:1] == here[0]) | (places[0:1] == 254)
        out[pl.ds(source, 1), :] = jnp.where(mine, places[1:2] * 64 + places[2:3], -1)


def pick_tiles(codes, tile_refs, chosen, picked, slots, height, dummy):
    total = jnp.int32(0)
    for source, tiles in enumerate(tile_refs):

        def body(step, total, source=source, tiles=tiles):
            for sub in range(group):
                slot = step * group + sub
                code = codes[source, slot]
                top = pl.multiple_of(slot * height, height)
                chosen[total] = tiles[pl.ds(top, height), :]
                picked[total] = code
                total = total + jnp.where(code >= 0, 1, 0)
            return total

        total = lax.fori_loop(0, (codes[source, slots] + group - 1) // group, body, total)
    for sub in range(group):
        picked[total + sub] = dummy
    return total


def forward_kernel(codes, *refs, slots, height, blocks, line_order, across):
    far = len(line_order)
    lines, tile_refs = refs[:far], refs[far : far + across]
    out, slabs, chosen, totals, picked = refs[far + across :]
    slab_count = slabs.shape[0]
    near = slab_count // far
    for shift, line in zip(line_order, lines):
        slabs[pl.ds(shift * near, near)] = line[...]
    dummy = slab_count * 64 + blocks
    totals[...] = jnp.zeros_like(totals)
    total = pick_tiles(codes, tile_refs, chosen, picked, slots, height, dummy)

    def body(step, carry):
        products = []
        for sub in range(group):
            code = picked[step * group + sub]
            slab = jnp.minimum(code >> 6, slab_count - 1)
            product = jnp.dot(
                chosen[step * group + sub], slabs[slab], preferred_element_type=jnp.float32
            )
            products.append((code & 63, product))
        for block, product in products:
            totals[block] += product
        return carry

    lax.fori_loop(0, (total + group - 1) // group, body, 0)
    halves = out.shape[1] // height
    for block in range(blocks):
        out[block // halves, pl.ds((block % halves) * height, height), :] = totals[block].astype(
            jnp.bfloat16
        )


def split_wide(value):
    high = value.astype(jnp.bfloat16).astype(jnp.float32)
    return high, value - high


def bias_rows(pieces):
    rows = lax.broadcasted_iota(jnp.int32, (16, lanes), 0)
    block = jnp.zeros((16, lanes), jnp.float32)
    for index, piece in enumerate(pieces):
        block = jnp.where(rows == index, jnp.broadcast_to(piece, (16, lanes)), block)
    return block


def sum_rows(ref, start, size):
    value = ref[0, pl.ds(start, size), :].astype(jnp.float32)
    for index in range(1, ref.shape[0]):
        value = value + ref[index, pl.ds(start, size), :].astype(jnp.float32)
    return value


def dense_kernel(partials, weight, bias, cotangent, hidden, message):
    members = partials.shape[0]
    nodes = partials.shape[1]
    aggregate = sum_rows(partials, 0, nodes)
    weight_wide = weight[...].astype(jnp.float32)
    pre = (
        jnp.dot(
            aggregate,
            weight_wide,
            precision=lax.Precision.HIGHEST,
            preferred_element_type=jnp.float32,
        )
        + bias[...]
    )
    square = pre * pre
    angle = jnp.tanh(root_two_over_pi * (pre + cubic * (square * pre)))
    gate = 0.5 * (1.0 + angle)
    hidden[...] = (pre * gate).astype(jnp.bfloat16)
    inner = root_two_over_pi * (1.0 + 3.0 * cubic * square)
    gradient = gate + 0.5 * pre * (1.0 - angle * angle) * inner
    slope = (cotangent[...].astype(jnp.float32) * gradient).astype(jnp.bfloat16)
    slope_wide = slope.astype(jnp.float32)
    spread = lax.dot_general(
        slope, weight[...], (((1,), (1,)), ((), ())), preferred_element_type=jnp.float32
    ).astype(jnp.bfloat16)
    weight_part = lax.dot_general(
        aggregate,
        slope_wide,
        (((0,), (0,)), ((), ())),
        precision=lax.Precision.HIGHEST,
        preferred_element_type=jnp.float32,
    )
    bias_part = jnp.sum(slope_wide, axis=0, keepdims=True)
    high, low = split_wide(bias_part)
    bias_block = bias_rows([high[:, :lanes], high[:, lanes:], low[:, :lanes], low[:, lanes:]])
    bias_block = bias_block.astype(jnp.bfloat16)
    share = weight_part.shape[0] // members
    for member in range(members):
        message[member, pl.ds(0, nodes), :] = spread
        part = weight_part[member * share : (member + 1) * share]
        part = jnp.concatenate([part[:, :lanes], part[:, lanes:]], axis=0)
        high, low = split_wide(part)
        message[member, pl.ds(nodes, 2 * share), :] = high.astype(jnp.bfloat16)
        message[member, pl.ds(nodes + 2 * share, 2 * share), :] = low.astype(jnp.bfloat16)
        message[member, pl.ds(nodes + 4 * share, 16), :] = bias_block


def sum_bias(ref, start):
    block = sum_rows(ref, start, 16)
    return [block[0:1] + block[2:3], block[1:2] + block[3:4]]


def pack_bias(values):
    parts = [split_wide(value) for value in values]
    return bias_rows([parts[0][0], parts[1][0], parts[0][1], parts[1][1]]).astype(jnp.bfloat16)


def backward_kernel(codes, spreads, *refs, slots, height, blocks, nodes, share, far, across):
    tile_refs, outs = refs[:across], refs[across : across + far]
    shares, chosen, totals, picked = refs[across + far :]
    slab_count = totals.shape[0] - 1
    halves = nodes // height
    dummy = slab_count * 64 + blocks
    totals[...] = jnp.zeros_like(totals)
    total = pick_tiles(codes, tile_refs, chosen, picked, slots, height, dummy)

    def body(step, carry):
        products = []
        for sub in range(group):
            code = picked[step * group + sub]
            block = jnp.minimum(code & 63, blocks - 1)
            top = pl.multiple_of((block % halves) * height, height)
            product = lax.dot_general(
                chosen[step * group + sub],
                spreads[block // halves, pl.ds(top, height), :],
                (((0,), (0,)), ((), ())),
                preferred_element_type=jnp.float32,
            )
            products.append((code >> 6, product))
        for slab, product in products:
            totals[slab] += product
        return carry

    lax.fori_loop(0, (total + group - 1) // group, body, 0)
    near = slab_count // far
    for shift, out in enumerate(outs):
        for index in range(near):
            out[index] = totals[shift * near + index].astype(jnp.bfloat16)
    weight_sum = sum_rows(spreads, nodes, 2 * share) + sum_rows(spreads, nodes + 2 * share, 2 * share)
    high, low = split_wide(weight_sum)
    bias_block = pack_bias(sum_bias(spreads, nodes + 4 * share))
    for index in range(near):
        shares[index, pl.ds(0, 2 * share), :] = high.astype(jnp.bfloat16)
        shares[index, pl.ds(2 * share, 2 * share), :] = low.astype(jnp.bfloat16)
        shares[index, pl.ds(4 * share, 16), :] = bias_block


def share_kernel(arrived, out, bias_block, *, share):
    total = sum_rows(arrived, 0, 2 * share) + sum_rows(arrived, 2 * share, 2 * share)
    for index in range(out.shape[0]):
        out[index] = total
    bias_block[...] = pack_bias(sum_bias(arrived, 4 * share))


def gather_kernel(shares, bias_block, out, *, share):
    step = 16 // share if share < 16 else 1
    rows = shares.shape[0] * share
    for half in range(2):
        for first in range(0, shares.shape[0], step):
            parts = [shares[first + sub, pl.ds(half * share, share), :] for sub in range(step)]
            part = jnp.concatenate(parts, axis=0) if step > 1 else parts[0]
            out[pl.ds(half * rows + first * share, step * share), :] = part.astype(jnp.bfloat16)
    out[pl.ds(2 * rows, 16), :] = bias_block[...]


def middle_kernel(*refs, far):
    out = refs[-1]
    for index in range(out.shape[0]):
        total = refs[0][index].astype(jnp.float32)
        for line in refs[1:far]:
            total = total + line[index].astype(jnp.float32)
        out[index] = total.astype(jnp.bfloat16)


def last_kernel(arrived, pieces, grad, weight_grad, bias_grad, *, factor):
    grad[...] = sum_rows(arrived, 0, grad.shape[0])
    rows = weight_grad.shape[0]
    weight_grad[:, pl.ds(0, lanes)] = sum_rows(pieces, 0, rows) * factor
    weight_grad[:, pl.ds(lanes, lanes)] = sum_rows(pieces, rows, rows) * factor
    low, high = sum_bias(pieces, 2 * rows)
    bias_grad[:, pl.ds(0, lanes)] = low * factor
    bias_grad[:, pl.ds(lanes, lanes)] = high * factor


def in_vmem():
    return pl.BlockSpec(memory_space=pltpu.VMEM)


def in_smem():
    return pl.BlockSpec(memory_space=pltpu.SMEM)


def local(features, tile_rows, tile_cols, tile_counts, tile_values, weight, bias, cotangent):
    nodes, width = features.shape
    slots, height, tile_width = tile_values.shape[2:]
    hidden = weight.shape[1]
    far = lax.axis_size("yhi")
    across = lax.axis_size("x")
    near = lax.axis_size("z")
    members = lax.axis_size(team_axes)
    group_rows = lax.axis_size(row_axes)
    here = lax.axis_index("x")
    params = pltpu.CompilerParams(vmem_limit_bytes=vmem_bytes)
    halves = nodes // height
    blocks = members * halves

    def any_place():
        return pl.BlockSpec(memory_space=pl.ANY)

    live = jnp.arange(slots, dtype=jnp.int32) < tile_counts[0, 0]
    columns, rows = tile_cols[0, 0], tile_rows[0, 0]
    owner = jnp.where(live, (columns // near) % across, 255)
    distance = (lax.axis_index("yhi") - columns // (across * near)) % far
    slab = distance * near + columns % near
    block = ((rows // halves) * across + here) * halves + rows % halves
    places = jnp.stack([owner, slab, block])
    ends = jnp.stack([jnp.int32(254), jnp.int32(0), tile_counts[0, 0]])[:, None]
    places = jnp.concatenate([places, ends], axis=1)
    places = jnp.pad(places, ((0, 13), (0, lanes - slots - 1))).astype(jnp.bfloat16)
    own = jnp.concatenate([tile_values[0, 0].reshape(slots * height, tile_width), places], axis=0)

    def ring(size, shift):
        return [(start, (start + shift) % size) for start in range(size)]

    longest_first = sorted(range(1, far), key=lambda shift: -min(shift, far - shift))

    buffers = [own]
    for shift in sorted(range(1, across), key=lambda shift: -min(shift, across - shift)):
        buffers.append(lax.ppermute(own, "x", ring(across, shift)))

    lines = [spread_out(features, "z", near)]
    line_order = [0] + longest_first[::-1]
    for shift in line_order[1:]:
        lines.append(lax.ppermute(lines[0], "yhi", ring(far, shift)))

    codes = pl.pallas_call(
        lambda *refs: codes_kernel(*refs, across=across, top=slots * height),
        out_shape=jax.ShapeDtypeStruct((across, lanes), jnp.int32),
        in_specs=[in_smem()] + [in_vmem()] * across + [any_place()] * (far - 1),
        out_specs=in_vmem(),
        compiler_params=params,
        name="tile_codes",
    )(here.reshape(1), *buffers, *lines[1:])

    scratch_tiles = pltpu.VMEM((across * slots + group, height, tile_width), jnp.bfloat16)
    scratch_list = pltpu.SMEM((across * slots + group,), jnp.int32)
    partial = pl.pallas_call(
        lambda *refs: forward_kernel(
            *refs,
            slots=slots,
            height=height,
            blocks=blocks,
            line_order=line_order,
            across=across,
        ),
        out_shape=jax.ShapeDtypeStruct((members, nodes, width), jnp.bfloat16),
        in_specs=[in_smem()] + [in_vmem()] * (far + across),
        out_specs=in_vmem(),
        scratch_shapes=[
            pltpu.VMEM((far * near, nodes, width), jnp.bfloat16),
            scratch_tiles,
            pltpu.VMEM((blocks + 1, height, width), jnp.float32),
            scratch_list,
        ],
        compiler_params=params,
        name="forward_tiles",
    )(codes, *lines, *buffers)
    partials = lax.all_to_all(partial, team_axes, 0, 0, tiled=True)

    share = width // members
    hidden_out, message = pl.pallas_call(
        dense_kernel,
        out_shape=(
            jax.ShapeDtypeStruct((nodes, hidden), jnp.bfloat16),
            jax.ShapeDtypeStruct((members, nodes + 4 * share + 16, width), jnp.bfloat16),
        ),
        in_specs=[in_vmem()] * 4,
        out_specs=(in_vmem(), in_vmem()),
        compiler_params=params,
        name="dense_layer",
    )(partials, weight, bias.reshape(1, hidden), cotangent)
    spreads = lax.all_to_all(message, team_axes, 0, 0, tiled=True)

    outs = pl.pallas_call(
        lambda *refs: backward_kernel(
            *refs,
            slots=slots,
            height=height,
            blocks=blocks,
            nodes=nodes,
            share=share,
            far=far,
            across=across,
        ),
        out_shape=(jax.ShapeDtypeStruct((near, nodes, width), jnp.bfloat16),) * far
        + (jax.ShapeDtypeStruct((near, 4 * share + 16, width), jnp.bfloat16),),
        in_specs=[in_smem(), in_vmem()] + [in_vmem()] * across,
        out_specs=(in_vmem(),) * (far + 1),
        scratch_shapes=[
            scratch_tiles,
            pltpu.VMEM((far * near + 1, nodes, width), jnp.float32),
            scratch_list,
        ],
        compiler_params=params,
        name="backward_tiles",
    )(codes, spreads, *buffers)

    lines = [outs[0]]
    for shift in longest_first:
        lines.append(lax.ppermute(outs[shift], "yhi", ring(far, -shift)))

    def gather_gradients(value):
        arrived = lax.all_to_all(value, "z", 0, 0, tiled=True)
        shares, bias_block = pl.pallas_call(
            lambda *refs: share_kernel(*refs, share=share),
            out_shape=(
                jax.ShapeDtypeStruct((members, 2 * share, lanes), jnp.float32),
                jax.ShapeDtypeStruct((16, lanes), jnp.bfloat16),
            ),
            in_specs=[in_vmem()],
            out_specs=(in_vmem(), in_vmem()),
            compiler_params=params,
            name="share_sum",
        )(arrived)
        shares = lax.all_to_all(shares, team_axes, 0, 0, tiled=True)
        return pl.pallas_call(
            lambda *refs: gather_kernel(*refs, share=share),
            out_shape=jax.ShapeDtypeStruct((2 * width + 16, lanes), jnp.bfloat16),
            in_specs=[in_vmem(), in_vmem()],
            out_specs=in_vmem(),
            compiler_params=params,
            name="share_gather",
        )(shares, bias_block)

    gradients = lax.cond(
        tile_counts[0, 0] > 0,
        gather_gradients,
        lambda value: jnp.zeros((2 * width + 16, lanes), jnp.bfloat16),
        outs[far],
    )
    line = pl.pallas_call(
        lambda *refs: middle_kernel(*refs, far=far),
        out_shape=jax.ShapeDtypeStruct((near, nodes, width), jnp.bfloat16),
        in_specs=[in_vmem()] * far + [any_place()],
        out_specs=in_vmem(),
        compiler_params=params,
        name="middle_sums",
    )(*lines, gradients)

    pieces = lax.all_gather(gradients, "yhi", axis=0)
    arrived = lax.all_to_all(line, "z", 0, 0, tiled=True)
    factor = 1.0 / math.sqrt(nodes * group_rows * far * across * near)
    features_grad, weight_grad, bias_grad = pl.pallas_call(
        lambda *refs: last_kernel(*refs, factor=factor),
        out_shape=(
            jax.ShapeDtypeStruct((nodes, width), jnp.float32),
            jax.ShapeDtypeStruct((width, hidden), jnp.float32),
            jax.ShapeDtypeStruct((1, hidden), jnp.float32),
        ),
        in_specs=[in_vmem(), in_vmem()],
        out_specs=(in_vmem(), in_vmem(), in_vmem()),
        compiler_params=params,
        name="last_sums",
    )(arrived, pieces)
    return (hidden_out, features_grad, weight_grad, bias_grad.reshape(hidden))


def solution(mesh):
    fine = Mesh(mesh.devices.reshape(row_split + col_split), axis_names)
    nodes_spec = P(row_axes + col_axes, None)
    in_specs = (
        nodes_spec,
        P(row_axes, col_axes, None),
        P(row_axes, col_axes, None),
        P(row_axes, col_axes),
        P(row_axes, col_axes, None, None, None),
        P(),
        P(),
        nodes_spec,
    )
    out_specs = (nodes_spec, nodes_spec, P(), P())
    return jax.shard_map(local, mesh=fine, in_specs=in_specs, out_specs=out_specs, check_vma=False)
```

```python
import math

import jax
import jax.numpy as jnp
from jax import lax
from jax.experimental import pallas as pl
from jax.experimental.pallas import tpu as pltpu
from jax.sharding import Mesh, PartitionSpec as P

row_split = (2, 2)
col_split = (4, 4, 12)
axis_names = ("ylo", "core", "yhi", "x", "z")
row_axes = ("ylo", "core")
col_axes = ("yhi", "x", "z")
team_axes = ("ylo", "core", "x")
share_axes = ("core", "x")
group = 4
lanes = 128
vmem_bytes = 12 * 1024 * 1024
root_two_over_pi = math.sqrt(2.0 / math.pi)
cubic = 0.044715


def spread_out(value, axes, count):
    copies = jnp.broadcast_to(value[None], (count,) + value.shape)
    return lax.all_to_all(copies, axes, 0, 0, tiled=True)


def codes_kernel(here, *refs, across, top):
    out = refs[-1]
    for source in range(across):
        places = refs[source][pl.ds(top, 16), :].astype(jnp.float32).astype(jnp.int32)
        mine = (places[0:1] == here[0]) | (places[0:1] == 254)
        out[pl.ds(source, 1), :] = jnp.where(mine, places[1:2] * 64 + places[2:3], -1)


def pick_tiles(codes, tile_refs, chosen, picked, slots, height, dummy):
    total = jnp.int32(0)
    for source, tiles in enumerate(tile_refs):

        def body(step, total, source=source, tiles=tiles):
            for sub in range(group):
                slot = step * group + sub
                code = codes[source, slot]
                top = pl.multiple_of(slot * height, height)
                chosen[total] = tiles[pl.ds(top, height), :]
                picked[total] = code
                total = total + jnp.where(code >= 0, 1, 0)
            return total

        total = lax.fori_loop(0, (codes[source, slots] + group - 1) // group, body, total)
    for sub in range(group):
        picked[total + sub] = dummy
    return total


def forward_kernel(codes, *refs, slots, height, blocks, line_order, across):
    far = len(line_order)
    lines, tile_refs = refs[:far], refs[far : far + across]
    out, slabs, chosen, totals, picked = refs[far + across :]
    slab_count = slabs.shape[0]
    near = slab_count // far
    for shift, line in zip(line_order, lines):
        slabs[pl.ds(shift * near, near)] = line[...]
    dummy = slab_count * 64 + blocks
    totals[...] = jnp.zeros_like(totals)
    total = pick_tiles(codes, tile_refs, chosen, picked, slots, height, dummy)

    def body(step, carry):
        products = []
        for sub in range(group):
            code = picked[step * group + sub]
            slab = jnp.minimum(code >> 6, slab_count - 1)
            product = jnp.dot(
                chosen[step * group + sub], slabs[slab], preferred_element_type=jnp.float32
            )
            products.append((code & 63, product))
        for block, product in products:
            totals[block] += product
        return carry

    lax.fori_loop(0, (total + group - 1) // group, body, 0)
    halves = out.shape[1] // height
    for block in range(blocks):
        out[block // halves, pl.ds((block % halves) * height, height), :] = totals[block].astype(
            jnp.bfloat16
        )


def split_wide(value):
    high = value.astype(jnp.bfloat16).astype(jnp.float32)
    return high, value - high


def bias_rows(pieces):
    rows = lax.broadcasted_iota(jnp.int32, (16, lanes), 0)
    block = jnp.zeros((16, lanes), jnp.float32)
    for index, piece in enumerate(pieces):
        block = jnp.where(rows == index, jnp.broadcast_to(piece, (16, lanes)), block)
    return block


def sum_rows(ref, start, size):
    value = ref[0, pl.ds(start, size), :].astype(jnp.float32)
    for index in range(1, ref.shape[0]):
        value = value + ref[index, pl.ds(start, size), :].astype(jnp.float32)
    return value


def dense_kernel(partials, weight, bias, cotangent, hidden, message, *, share):
    members = partials.shape[0]
    nodes = partials.shape[1]
    aggregate = sum_rows(partials, 0, nodes)
    weight_wide = weight[...].astype(jnp.float32)
    pre = (
        jnp.dot(
            aggregate,
            weight_wide,
            precision=lax.Precision.HIGHEST,
            preferred_element_type=jnp.float32,
        )
        + bias[...]
    )
    square = pre * pre
    angle = jnp.tanh(root_two_over_pi * (pre + cubic * (square * pre)))
    gate = 0.5 * (1.0 + angle)
    hidden[...] = (pre * gate).astype(jnp.bfloat16)
    inner = root_two_over_pi * (1.0 + 3.0 * cubic * square)
    gradient = gate + 0.5 * pre * (1.0 - angle * angle) * inner
    slope = (cotangent[...].astype(jnp.float32) * gradient).astype(jnp.bfloat16)
    slope_wide = slope.astype(jnp.float32)
    spread = lax.dot_general(
        slope, weight[...], (((1,), (1,)), ((), ())), preferred_element_type=jnp.float32
    ).astype(jnp.bfloat16)
    weight_part = lax.dot_general(
        aggregate,
        slope_wide,
        (((0,), (0,)), ((), ())),
        precision=lax.Precision.HIGHEST,
        preferred_element_type=jnp.float32,
    )
    bias_part = jnp.sum(slope_wide, axis=0, keepdims=True)
    high, low = split_wide(bias_part)
    bias_block = bias_rows([high[:, :lanes], high[:, lanes:], low[:, :lanes], low[:, lanes:]])
    bias_block = bias_block.astype(jnp.bfloat16)
    for member in range(members):
        message[member, pl.ds(0, nodes), :] = spread
        first = member * share % weight_part.shape[0]
        part = weight_part[first : first + share]
        part = jnp.concatenate([part[:, :lanes], part[:, lanes:]], axis=0)
        message[member, pl.ds(nodes, 2 * share), :] = part.astype(jnp.bfloat16)
        message[member, pl.ds(nodes + 2 * share, 16), :] = bias_block


def sum_bias(ref, start):
    block = sum_rows(ref, start, 16)
    return [block[0:1] + block[2:3], block[1:2] + block[3:4]]


def pack_bias(values):
    parts = [split_wide(value) for value in values]
    return bias_rows([parts[0][0], parts[1][0], parts[0][1], parts[1][1]]).astype(jnp.bfloat16)


def backward_kernel(codes, spreads, *refs, slots, height, blocks, nodes, share, far, across):
    tile_refs, outs = refs[:across], refs[across : across + far]
    shares, chosen, totals, picked = refs[across + far :]
    slab_count = totals.shape[0] - 1
    halves = nodes // height
    dummy = slab_count * 64 + blocks
    totals[...] = jnp.zeros_like(totals)
    total = pick_tiles(codes, tile_refs, chosen, picked, slots, height, dummy)

    def body(step, carry):
        products = []
        for sub in range(group):
            code = picked[step * group + sub]
            block = jnp.minimum(code & 63, blocks - 1)
            top = pl.multiple_of((block % halves) * height, height)
            product = lax.dot_general(
                chosen[step * group + sub],
                spreads[block // halves, pl.ds(top, height), :],
                (((0,), (0,)), ((), ())),
                preferred_element_type=jnp.float32,
            )
            products.append((code >> 6, product))
        for slab, product in products:
            totals[slab] += product
        return carry

    lax.fori_loop(0, (total + group - 1) // group, body, 0)
    near = slab_count // far
    for shift, out in enumerate(outs):
        for index in range(near):
            out[index] = totals[shift * near + index].astype(jnp.bfloat16)
    weight_sum = sum_rows(spreads, nodes, 2 * share).astype(jnp.bfloat16)
    bias_block = pack_bias(sum_bias(spreads, nodes + 2 * share))
    for index in range(near):
        shares[index, pl.ds(0, 2 * share), :] = weight_sum
        shares[index, pl.ds(2 * share, 16), :] = bias_block


def share_kernel(arrived, out, bias_block, *, share):
    total = sum_rows(arrived, 0, 2 * share).astype(jnp.bfloat16)
    for index in range(out.shape[0]):
        out[index] = total
    bias_block[...] = pack_bias(sum_bias(arrived, 2 * share))


def gather_kernel(shares, bias_block, out, *, share):
    rows = shares.shape[0] * share
    for index in range(shares.shape[0]):
        for half in range(2):
            part = shares[index, pl.ds(half * share, share), :]
            out[pl.ds(half * rows + index * share, share), :] = part
    out[pl.ds(2 * rows, 16), :] = bias_block[...]


def middle_kernel(*refs, far):
    out = refs[-1]
    for index in range(out.shape[0]):
        total = refs[0][index].astype(jnp.float32)
        for line in refs[1:far]:
            total = total + line[index].astype(jnp.float32)
        out[index] = total.astype(jnp.bfloat16)


def last_kernel(arrived, pieces, grad, weight_grad, bias_grad, *, factor):
    grad[...] = sum_rows(arrived, 0, grad.shape[0])
    rows = weight_grad.shape[0]
    weight_grad[:, pl.ds(0, lanes)] = sum_rows(pieces, 0, rows) * factor
    weight_grad[:, pl.ds(lanes, lanes)] = sum_rows(pieces, rows, rows) * factor
    low, high = sum_bias(pieces, 2 * rows)
    bias_grad[:, pl.ds(0, lanes)] = low * factor
    bias_grad[:, pl.ds(lanes, lanes)] = high * factor


def in_vmem():
    return pl.BlockSpec(memory_space=pltpu.VMEM)


def in_smem():
    return pl.BlockSpec(memory_space=pltpu.SMEM)


def local(features, tile_rows, tile_cols, tile_counts, tile_values, weight, bias, cotangent):
    nodes, width = features.shape
    slots, height, tile_width = tile_values.shape[2:]
    hidden = weight.shape[1]
    far = lax.axis_size("yhi")
    across = lax.axis_size("x")
    near = lax.axis_size("z")
    members = lax.axis_size(team_axes)
    group_rows = lax.axis_size(row_axes)
    here = lax.axis_index("x")
    params = pltpu.CompilerParams(vmem_limit_bytes=vmem_bytes)
    halves = nodes // height
    blocks = members * halves

    def any_place():
        return pl.BlockSpec(memory_space=pl.ANY)

    live = jnp.arange(slots, dtype=jnp.int32) < tile_counts[0, 0]
    columns, rows = tile_cols[0, 0], tile_rows[0, 0]
    owner = jnp.where(live, (columns // near) % across, 255)
    distance = (lax.axis_index("yhi") - columns // (across * near)) % far
    slab = distance * near + columns % near
    block = ((rows // halves) * across + here) * halves + rows % halves
    places = jnp.stack([owner, slab, block])
    ends = jnp.stack([jnp.int32(254), jnp.int32(0), tile_counts[0, 0]])[:, None]
    places = jnp.concatenate([places, ends], axis=1)
    places = jnp.pad(places, ((0, 13), (0, lanes - slots - 1))).astype(jnp.bfloat16)
    own = jnp.concatenate([tile_values[0, 0].reshape(slots * height, tile_width), places], axis=0)

    def ring(size, shift):
        return [(start, (start + shift) % size) for start in range(size)]

    longest_first = sorted(range(1, far), key=lambda shift: -min(shift, far - shift))

    buffers = [own]
    for shift in sorted(range(1, across), key=lambda shift: -min(shift, across - shift)):
        buffers.append(lax.ppermute(own, "x", ring(across, shift)))

    lines = [spread_out(features, "z", near)]
    line_order = [0] + longest_first[::-1]
    for shift in line_order[1:]:
        lines.append(lax.ppermute(lines[0], "yhi", ring(far, shift)))

    codes = pl.pallas_call(
        lambda *refs: codes_kernel(*refs, across=across, top=slots * height),
        out_shape=jax.ShapeDtypeStruct((across, lanes), jnp.int32),
        in_specs=[in_smem()] + [in_vmem()] * across + [any_place()] * (far - 1),
        out_specs=in_vmem(),
        compiler_params=params,
        name="tile_codes",
    )(here.reshape(1), *buffers, *lines[1:])

    scratch_tiles = pltpu.VMEM((across * slots + group, height, tile_width), jnp.bfloat16)
    scratch_list = pltpu.SMEM((across * slots + group,), jnp.int32)
    partial = pl.pallas_call(
        lambda *refs: forward_kernel(
            *refs,
            slots=slots,
            height=height,
            blocks=blocks,
            line_order=line_order,
            across=across,
        ),
        out_shape=jax.ShapeDtypeStruct((members, nodes, width), jnp.bfloat16),
        in_specs=[in_smem()] + [in_vmem()] * (far + across),
        out_specs=in_vmem(),
        scratch_shapes=[
            pltpu.VMEM((far * near, nodes, width), jnp.bfloat16),
            scratch_tiles,
            pltpu.VMEM((blocks + 1, height, width), jnp.float32),
            scratch_list,
        ],
        compiler_params=params,
        name="forward_tiles",
    )(codes, *lines, *buffers)
    partials = lax.all_to_all(partial, team_axes, 0, 0, tiled=True)

    holders = lax.axis_size(share_axes)
    share = width // holders
    hidden_out, message = pl.pallas_call(
        lambda *refs: dense_kernel(*refs, share=share),
        out_shape=(
            jax.ShapeDtypeStruct((nodes, hidden), jnp.bfloat16),
            jax.ShapeDtypeStruct((members, nodes + 2 * share + 16, width), jnp.bfloat16),
        ),
        in_specs=[in_vmem()] * 4,
        out_specs=(in_vmem(), in_vmem()),
        compiler_params=params,
        name="dense_layer",
    )(partials, weight, bias.reshape(1, hidden), cotangent)
    spreads = lax.all_to_all(message, team_axes, 0, 0, tiled=True)

    outs = pl.pallas_call(
        lambda *refs: backward_kernel(
            *refs,
            slots=slots,
            height=height,
            blocks=blocks,
            nodes=nodes,
            share=share,
            far=far,
            across=across,
        ),
        out_shape=(jax.ShapeDtypeStruct((near, nodes, width), jnp.bfloat16),) * far
        + (jax.ShapeDtypeStruct((near, 2 * share + 16, width), jnp.bfloat16),),
        in_specs=[in_smem(), in_vmem()] + [in_vmem()] * across,
        out_specs=(in_vmem(),) * (far + 1),
        scratch_shapes=[
            scratch_tiles,
            pltpu.VMEM((far * near + 1, nodes, width), jnp.float32),
            scratch_list,
        ],
        compiler_params=params,
        name="backward_tiles",
    )(codes, spreads, *buffers)

    lines = [outs[0]]
    for shift in longest_first:
        lines.append(lax.ppermute(outs[shift], "yhi", ring(far, -shift)))

    def gather_gradients(value):
        arrived = lax.all_to_all(value, "z", 0, 0, tiled=True)
        shares, bias_block = pl.pallas_call(
            lambda *refs: share_kernel(*refs, share=share),
            out_shape=(
                jax.ShapeDtypeStruct((holders, 2 * share, lanes), jnp.bfloat16),
                jax.ShapeDtypeStruct((16, lanes), jnp.bfloat16),
            ),
            in_specs=[in_vmem()],
            out_specs=(in_vmem(), in_vmem()),
            compiler_params=params,
            name="share_sum",
        )(arrived)
        shares = lax.all_to_all(shares, share_axes, 0, 0, tiled=True)
        return pl.pallas_call(
            lambda *refs: gather_kernel(*refs, share=share),
            out_shape=jax.ShapeDtypeStruct((2 * width + 16, lanes), jnp.bfloat16),
            in_specs=[in_vmem(), in_vmem()],
            out_specs=in_vmem(),
            compiler_params=params,
            name="share_gather",
        )(shares, bias_block)

    gradients = lax.cond(
        tile_counts[0, 0] > 0,
        gather_gradients,
        lambda value: jnp.zeros((2 * width + 16, lanes), jnp.bfloat16),
        outs[far],
    )
    line = pl.pallas_call(
        lambda *refs: middle_kernel(*refs, far=far),
        out_shape=jax.ShapeDtypeStruct((near, nodes, width), jnp.bfloat16),
        in_specs=[in_vmem()] * far + [any_place()],
        out_specs=in_vmem(),
        compiler_params=params,
        name="middle_sums",
    )(*lines, gradients)

    pieces = lax.all_gather(gradients, "yhi", axis=0)
    arrived = lax.all_to_all(line, "z", 0, 0, tiled=True)
    factor = 1.0 / math.sqrt(nodes * group_rows * far * across * near)
    features_grad, weight_grad, bias_grad = pl.pallas_call(
        lambda *refs: last_kernel(*refs, factor=factor),
        out_shape=(
            jax.ShapeDtypeStruct((nodes, width), jnp.float32),
            jax.ShapeDtypeStruct((width, hidden), jnp.float32),
            jax.ShapeDtypeStruct((1, hidden), jnp.float32),
        ),
        in_specs=[in_vmem(), in_vmem()],
        out_specs=(in_vmem(), in_vmem(), in_vmem()),
        compiler_params=params,
        name="last_sums",
    )(arrived, pieces)
    return (hidden_out, features_grad, weight_grad, bias_grad.reshape(hidden))


def solution(mesh):
    fine = Mesh(mesh.devices.reshape(row_split + col_split), axis_names)
    nodes_spec = P(row_axes + col_axes, None)
    in_specs = (
        nodes_spec,
        P(row_axes, col_axes, None),
        P(row_axes, col_axes, None),
        P(row_axes, col_axes),
        P(row_axes, col_axes, None, None, None),
        P(),
        P(),
        nodes_spec,
    )
    out_specs = (nodes_spec, nodes_spec, P(), P())
    return jax.shard_map(local, mesh=fine, in_specs=in_specs, out_specs=out_specs, check_vma=False)
```

```python
import math

import jax
import jax.numpy as jnp
from jax import lax
from jax.experimental import pallas as pl
from jax.experimental.pallas import tpu as pltpu
from jax.sharding import Mesh, PartitionSpec as P

row_split = (2, 2)
col_split = (4, 4, 12)
axis_names = ("ylo", "core", "yhi", "x", "z")
row_axes = ("ylo", "core")
col_axes = ("yhi", "x", "z")
team_axes = ("ylo", "core", "x")
share_axes = ("core", "x")
tail_rows = 64
group = 4
lanes = 128
vmem_bytes = 12 * 1024 * 1024
root_two_over_pi = math.sqrt(2.0 / math.pi)
cubic = 0.044715


def spread_out(value, axes, count):
    copies = jnp.broadcast_to(value[None], (count,) + value.shape)
    return lax.all_to_all(copies, axes, 0, 0, tiled=True)


def codes_kernel(here, *refs, across, top):
    out = refs[-1]
    for source in range(across):
        places = refs[source][pl.ds(top, 16), :].astype(jnp.float32).astype(jnp.int32)
        mine = (places[0:1] == here[0]) | (places[0:1] == 254)
        out[pl.ds(source, 1), :] = jnp.where(mine, places[1:2] * 64 + places[2:3], -1)


def pick_tiles(codes, tile_refs, chosen, picked, slots, height, dummy):
    total = jnp.int32(0)
    for source, tiles in enumerate(tile_refs):

        def body(step, total, source=source, tiles=tiles):
            for sub in range(group):
                slot = step * group + sub
                code = codes[source, slot]
                top = pl.multiple_of(slot * height, height)
                chosen[total] = tiles[pl.ds(top, height), :]
                picked[total] = code
                total = total + jnp.where(code >= 0, 1, 0)
            return total

        total = lax.fori_loop(0, (codes[source, slots] + group - 1) // group, body, total)
    for sub in range(group):
        picked[total + sub] = dummy
    return total


def forward_kernel(codes, *refs, slots, height, blocks, line_order, across):
    far = len(line_order)
    lines, tails, tile_refs = refs[:far], refs[far], refs[far + 1 : far + 1 + across]
    out, slabs, chosen, totals, picked = refs[far + 1 + across :]
    slab_count = slabs.shape[0]
    near = slab_count // far
    for shift, line in zip(line_order, lines):
        lead = line.shape[1]
        slabs[pl.ds(shift * near, near), pl.ds(0, lead), :] = line[...]
        if lead < slabs.shape[1]:
            slabs[pl.ds(shift * near, near), pl.ds(lead, tails.shape[1]), :] = tails[...]
    dummy = slab_count * 64 + blocks
    totals[...] = jnp.zeros_like(totals)
    total = pick_tiles(codes, tile_refs, chosen, picked, slots, height, dummy)

    def body(step, carry):
        products = []
        for sub in range(group):
            code = picked[step * group + sub]
            slab = jnp.minimum(code >> 6, slab_count - 1)
            product = jnp.dot(
                chosen[step * group + sub], slabs[slab], preferred_element_type=jnp.float32
            )
            products.append((code & 63, product))
        for block, product in products:
            totals[block] += product
        return carry

    lax.fori_loop(0, (total + group - 1) // group, body, 0)
    halves = out.shape[1] // height
    for block in range(blocks):
        out[block // halves, pl.ds((block % halves) * height, height), :] = totals[block].astype(
            jnp.bfloat16
        )


def split_wide(value):
    high = value.astype(jnp.bfloat16).astype(jnp.float32)
    return high, value - high


def bias_rows(pieces):
    rows = lax.broadcasted_iota(jnp.int32, (16, lanes), 0)
    block = jnp.zeros((16, lanes), jnp.float32)
    for index, piece in enumerate(pieces):
        block = jnp.where(rows == index, jnp.broadcast_to(piece, (16, lanes)), block)
    return block


def sum_rows(ref, start, size):
    value = ref[0, pl.ds(start, size), :].astype(jnp.float32)
    for index in range(1, ref.shape[0]):
        value = value + ref[index, pl.ds(start, size), :].astype(jnp.float32)
    return value


def dense_kernel(partials, weight, bias, cotangent, hidden, message, *, share):
    members = partials.shape[0]
    nodes = partials.shape[1]
    aggregate = sum_rows(partials, 0, nodes)
    weight_wide = weight[...].astype(jnp.float32)
    pre = (
        jnp.dot(
            aggregate,
            weight_wide,
            precision=lax.Precision.HIGHEST,
            preferred_element_type=jnp.float32,
        )
        + bias[...]
    )
    square = pre * pre
    angle = jnp.tanh(root_two_over_pi * (pre + cubic * (square * pre)))
    gate = 0.5 * (1.0 + angle)
    hidden[...] = (pre * gate).astype(jnp.bfloat16)
    inner = root_two_over_pi * (1.0 + 3.0 * cubic * square)
    gradient = gate + 0.5 * pre * (1.0 - angle * angle) * inner
    slope = (cotangent[...].astype(jnp.float32) * gradient).astype(jnp.bfloat16)
    slope_wide = slope.astype(jnp.float32)
    spread = lax.dot_general(
        slope, weight[...], (((1,), (1,)), ((), ())), preferred_element_type=jnp.float32
    ).astype(jnp.bfloat16)
    weight_part = lax.dot_general(
        aggregate,
        slope_wide,
        (((0,), (0,)), ((), ())),
        precision=lax.Precision.HIGHEST,
        preferred_element_type=jnp.float32,
    )
    bias_part = jnp.sum(slope_wide, axis=0, keepdims=True)
    high, low = split_wide(bias_part)
    bias_block = bias_rows([high[:, :lanes], high[:, lanes:], low[:, :lanes], low[:, lanes:]])
    bias_block = bias_block.astype(jnp.bfloat16)
    for member in range(members):
        message[member, pl.ds(0, nodes), :] = spread
        first = member * share % weight_part.shape[0]
        part = weight_part[first : first + share]
        part = jnp.concatenate([part[:, :lanes], part[:, lanes:]], axis=0)
        message[member, pl.ds(nodes, 2 * share), :] = part.astype(jnp.bfloat16)
        message[member, pl.ds(nodes + 2 * share, 16), :] = bias_block


def sum_bias(ref, start):
    block = sum_rows(ref, start, 16)
    return [block[0:1] + block[2:3], block[1:2] + block[3:4]]


def pack_bias(values):
    parts = [split_wide(value) for value in values]
    return bias_rows([parts[0][0], parts[1][0], parts[0][1], parts[1][1]]).astype(jnp.bfloat16)


def backward_kernel(codes, spreads, *refs, slots, height, blocks, nodes, share, far, across):
    tile_refs, outs = refs[:across], refs[across : across + far]
    shares, chosen, totals, picked = refs[across + far :]
    slab_count = totals.shape[0] - 1
    halves = nodes // height
    dummy = slab_count * 64 + blocks
    totals[...] = jnp.zeros_like(totals)
    total = pick_tiles(codes, tile_refs, chosen, picked, slots, height, dummy)

    def body(step, carry):
        products = []
        for sub in range(group):
            code = picked[step * group + sub]
            block = jnp.minimum(code & 63, blocks - 1)
            top = pl.multiple_of((block % halves) * height, height)
            product = lax.dot_general(
                chosen[step * group + sub],
                spreads[block // halves, pl.ds(top, height), :],
                (((0,), (0,)), ((), ())),
                preferred_element_type=jnp.float32,
            )
            products.append((code >> 6, product))
        for slab, product in products:
            totals[slab] += product
        return carry

    lax.fori_loop(0, (total + group - 1) // group, body, 0)
    near = slab_count // far
    for shift, out in enumerate(outs):
        for index in range(near):
            out[index] = totals[shift * near + index].astype(jnp.bfloat16)
    weight_sum = sum_rows(spreads, nodes, 2 * share).astype(jnp.bfloat16)
    bias_block = pack_bias(sum_bias(spreads, nodes + 2 * share))
    for index in range(near):
        shares[index, pl.ds(0, 2 * share), :] = weight_sum
        shares[index, pl.ds(2 * share, 16), :] = bias_block


def share_kernel(arrived, out, bias_block, *, share):
    total = sum_rows(arrived, 0, 2 * share).astype(jnp.bfloat16)
    for index in range(out.shape[0]):
        out[index] = total
    bias_block[...] = pack_bias(sum_bias(arrived, 2 * share))


def gather_kernel(shares, bias_block, out, *, share):
    rows = shares.shape[0] * share
    for index in range(shares.shape[0]):
        for half in range(2):
            part = shares[index, pl.ds(half * share, share), :]
            out[pl.ds(half * rows + index * share, share), :] = part
    out[pl.ds(2 * rows, 16), :] = bias_block[...]


def middle_kernel(*refs, far):
    out = refs[-1]
    for index in range(out.shape[0]):
        total = refs[0][index].astype(jnp.float32)
        for line in refs[1:far]:
            total = total + line[index].astype(jnp.float32)
        out[index] = total.astype(jnp.bfloat16)


def last_kernel(arrived, pieces, grad, weight_grad, bias_grad, *, factor):
    grad[...] = sum_rows(arrived, 0, grad.shape[0])
    rows = weight_grad.shape[0]
    weight_grad[:, pl.ds(0, lanes)] = sum_rows(pieces, 0, rows) * factor
    weight_grad[:, pl.ds(lanes, lanes)] = sum_rows(pieces, rows, rows) * factor
    low, high = sum_bias(pieces, 2 * rows)
    bias_grad[:, pl.ds(0, lanes)] = low * factor
    bias_grad[:, pl.ds(lanes, lanes)] = high * factor


def in_vmem():
    return pl.BlockSpec(memory_space=pltpu.VMEM)


def in_smem():
    return pl.BlockSpec(memory_space=pltpu.SMEM)


def local(features, tile_rows, tile_cols, tile_counts, tile_values, weight, bias, cotangent):
    nodes, width = features.shape
    slots, height, tile_width = tile_values.shape[2:]
    hidden = weight.shape[1]
    far = lax.axis_size("yhi")
    across = lax.axis_size("x")
    near = lax.axis_size("z")
    members = lax.axis_size(team_axes)
    group_rows = lax.axis_size(row_axes)
    here = lax.axis_index("x")
    params = pltpu.CompilerParams(vmem_limit_bytes=vmem_bytes)
    halves = nodes // height
    blocks = members * halves

    def any_place():
        return pl.BlockSpec(memory_space=pl.ANY)

    live = jnp.arange(slots, dtype=jnp.int32) < tile_counts[0, 0]
    columns, rows = tile_cols[0, 0], tile_rows[0, 0]
    owner = jnp.where(live, (columns // near) % across, 255)
    distance = (lax.axis_index("yhi") - columns // (across * near)) % far
    slab = distance * near + columns % near
    block = ((rows // halves) * across + here) * halves + rows % halves
    places = jnp.stack([owner, slab, block])
    ends = jnp.stack([jnp.int32(254), jnp.int32(0), tile_counts[0, 0]])[:, None]
    places = jnp.concatenate([places, ends], axis=1)
    places = jnp.pad(places, ((0, 13), (0, lanes - slots - 1))).astype(jnp.bfloat16)
    own = jnp.concatenate([tile_values[0, 0].reshape(slots * height, tile_width), places], axis=0)

    def ring(size, shift):
        return [(start, (start + shift) % size) for start in range(size)]

    longest_first = sorted(range(1, far), key=lambda shift: -min(shift, far - shift))

    buffers = [own]
    for shift in sorted(range(1, across), key=lambda shift: -min(shift, across - shift)):
        buffers.append(lax.ppermute(own, "x", ring(across, shift)))

    opposite = far // 2
    tail = lax.ppermute(features[nodes - tail_rows :], "yhi", ring(far, opposite))
    lines = [spread_out(features, "z", near)]
    line_order = [0] + longest_first[::-1]
    for shift in line_order[1:]:
        line = lines[0][:, : nodes - tail_rows] if shift == opposite else lines[0]
        lines.append(lax.ppermute(line, "yhi", ring(far, shift)))
    some = tile_counts[0, 0] > 0
    tails = lax.cond(
        some,
        lambda value: spread_out(value, "z", near),
        lambda value: jnp.zeros((near,) + value.shape, value.dtype),
        tail,
    )

    codes = pl.pallas_call(
        lambda *refs: codes_kernel(*refs, across=across, top=slots * height),
        out_shape=jax.ShapeDtypeStruct((across, lanes), jnp.int32),
        in_specs=[in_smem()] + [in_vmem()] * across + [any_place()] * (far - 1),
        out_specs=in_vmem(),
        compiler_params=params,
        name="tile_codes",
    )(here.reshape(1), *buffers, *lines[1:])

    scratch_tiles = pltpu.VMEM((across * slots + group, height, tile_width), jnp.bfloat16)
    scratch_list = pltpu.SMEM((across * slots + group,), jnp.int32)
    partial = pl.pallas_call(
        lambda *refs: forward_kernel(
            *refs,
            slots=slots,
            height=height,
            blocks=blocks,
            line_order=line_order,
            across=across,
        ),
        out_shape=jax.ShapeDtypeStruct((members, nodes, width), jnp.bfloat16),
        in_specs=[in_smem()] + [in_vmem()] * (far + 1 + across),
        out_specs=in_vmem(),
        scratch_shapes=[
            pltpu.VMEM((far * near, nodes, width), jnp.bfloat16),
            scratch_tiles,
            pltpu.VMEM((blocks + 1, height, width), jnp.float32),
            scratch_list,
        ],
        compiler_params=params,
        name="forward_tiles",
    )(codes, *lines, tails, *buffers)
    partials = lax.all_to_all(partial, team_axes, 0, 0, tiled=True)

    holders = lax.axis_size(share_axes)
    share = width // holders
    hidden_out, message = pl.pallas_call(
        lambda *refs: dense_kernel(*refs, share=share),
        out_shape=(
            jax.ShapeDtypeStruct((nodes, hidden), jnp.bfloat16),
            jax.ShapeDtypeStruct((members, nodes + 2 * share + 16, width), jnp.bfloat16),
        ),
        in_specs=[in_vmem()] * 4,
        out_specs=(in_vmem(), in_vmem()),
        compiler_params=params,
        name="dense_layer",
    )(partials, weight, bias.reshape(1, hidden), cotangent)
    spreads = lax.all_to_all(message, team_axes, 0, 0, tiled=True)

    outs = pl.pallas_call(
        lambda *refs: backward_kernel(
            *refs,
            slots=slots,
            height=height,
            blocks=blocks,
            nodes=nodes,
            share=share,
            far=far,
            across=across,
        ),
        out_shape=(jax.ShapeDtypeStruct((near, nodes, width), jnp.bfloat16),) * far
        + (jax.ShapeDtypeStruct((near, 2 * share + 16, width), jnp.bfloat16),),
        in_specs=[in_smem(), in_vmem()] + [in_vmem()] * across,
        out_specs=(in_vmem(),) * (far + 1),
        scratch_shapes=[
            scratch_tiles,
            pltpu.VMEM((far * near + 1, nodes, width), jnp.float32),
            scratch_list,
        ],
        compiler_params=params,
        name="backward_tiles",
    )(codes, spreads, *buffers)

    lines = [outs[0]]
    for shift in longest_first:
        lines.append(lax.ppermute(outs[shift], "yhi", ring(far, -shift)))

    def gather_gradients(value):
        arrived = lax.all_to_all(value, "z", 0, 0, tiled=True)
        shares, bias_block = pl.pallas_call(
            lambda *refs: share_kernel(*refs, share=share),
            out_shape=(
                jax.ShapeDtypeStruct((holders, 2 * share, lanes), jnp.bfloat16),
                jax.ShapeDtypeStruct((16, lanes), jnp.bfloat16),
            ),
            in_specs=[in_vmem()],
            out_specs=(in_vmem(), in_vmem()),
            compiler_params=params,
            name="share_sum",
        )(arrived)
        shares = lax.all_to_all(shares, share_axes, 0, 0, tiled=True)
        return pl.pallas_call(
            lambda *refs: gather_kernel(*refs, share=share),
            out_shape=jax.ShapeDtypeStruct((2 * width + 16, lanes), jnp.bfloat16),
            in_specs=[in_vmem(), in_vmem()],
            out_specs=in_vmem(),
            compiler_params=params,
            name="share_gather",
        )(shares, bias_block)

    gradients = lax.cond(
        some,
        gather_gradients,
        lambda value: jnp.zeros((2 * width + 16, lanes), jnp.bfloat16),
        outs[far],
    )
    line = pl.pallas_call(
        lambda *refs: middle_kernel(*refs, far=far),
        out_shape=jax.ShapeDtypeStruct((near, nodes, width), jnp.bfloat16),
        in_specs=[in_vmem()] * far + [any_place()],
        out_specs=in_vmem(),
        compiler_params=params,
        name="middle_sums",
    )(*lines, gradients)

    pieces = lax.all_gather(gradients, "yhi", axis=0)
    arrived = lax.all_to_all(line, "z", 0, 0, tiled=True)
    factor = 1.0 / math.sqrt(nodes * group_rows * far * across * near)
    features_grad, weight_grad, bias_grad = pl.pallas_call(
        lambda *refs: last_kernel(*refs, factor=factor),
        out_shape=(
            jax.ShapeDtypeStruct((nodes, width), jnp.float32),
            jax.ShapeDtypeStruct((width, hidden), jnp.float32),
            jax.ShapeDtypeStruct((1, hidden), jnp.float32),
        ),
        in_specs=[in_vmem(), in_vmem()],
        out_specs=(in_vmem(), in_vmem(), in_vmem()),
        compiler_params=params,
        name="last_sums",
    )(arrived, pieces)
    return (hidden_out, features_grad, weight_grad, bias_grad.reshape(hidden))


def solution(mesh):
    fine = Mesh(mesh.devices.reshape(row_split + col_split), axis_names)
    nodes_spec = P(row_axes + col_axes, None)
    in_specs = (
        nodes_spec,
        P(row_axes, col_axes, None),
        P(row_axes, col_axes, None),
        P(row_axes, col_axes),
        P(row_axes, col_axes, None, None, None),
        P(),
        P(),
        nodes_spec,
    )
    out_specs = (nodes_spec, nodes_spec, P(), P())
    return jax.shard_map(local, mesh=fine, in_specs=in_specs, out_specs=out_specs, check_vma=False)
```

```python
import math

import jax
import jax.numpy as jnp
from jax import lax
from jax.experimental import pallas as pl
from jax.experimental.pallas import tpu as pltpu
from jax.sharding import Mesh, PartitionSpec as P

row_split = (2, 2)
col_split = (4, 4, 12)
axis_names = ("ylo", "core", "yhi", "x", "z")
row_axes = ("ylo", "core")
col_axes = ("yhi", "x", "z")
team_axes = ("ylo", "core", "x")
share_axes = ("core", "x")
group = 4
lanes = 128
vmem_bytes = 12 * 1024 * 1024
root_two_over_pi = math.sqrt(2.0 / math.pi)
cubic = 0.044715


def spread_out(value, axes, count):
    copies = jnp.broadcast_to(value[None], (count,) + value.shape)
    return lax.all_to_all(copies, axes, 0, 0, tiled=True)


def codes_kernel(here, *refs, across, top):
    out = refs[-1]
    for source in range(across):
        places = refs[source][pl.ds(top, 16), :].astype(jnp.float32).astype(jnp.int32)
        mine = (places[0:1] == here[0]) | (places[0:1] == 254)
        out[pl.ds(source, 1), :] = jnp.where(mine, places[1:2] * 64 + places[2:3], -1)


def pick_tiles(codes, tile_refs, chosen, picked, slots, height, dummy):
    total = jnp.int32(0)
    for source, tiles in enumerate(tile_refs):

        def body(step, total, source=source, tiles=tiles):
            for sub in range(group):
                slot = step * group + sub
                code = codes[source, slot]
                top = pl.multiple_of(slot * height, height)
                chosen[total] = tiles[pl.ds(top, height), :]
                picked[total] = code
                total = total + jnp.where(code >= 0, 1, 0)
            return total

        total = lax.fori_loop(0, (codes[source, slots] + group - 1) // group, body, total)
    for sub in range(group):
        picked[total + sub] = dummy
    return total


def forward_kernel(codes, *refs, slots, height, blocks, line_order, across):
    far = len(line_order)
    lines, tile_refs = refs[:far], refs[far : far + across]
    out, slabs, chosen, totals, picked = refs[far + across :]
    slab_count = slabs.shape[0]
    near = slab_count // far
    for shift, line in zip(line_order, lines):
        slabs[pl.ds(shift * near, near)] = line[...]
    dummy = slab_count * 64 + blocks
    totals[...] = jnp.zeros_like(totals)
    total = pick_tiles(codes, tile_refs, chosen, picked, slots, height, dummy)

    def body(step, carry):
        products = []
        for sub in range(group):
            code = picked[step * group + sub]
            slab = jnp.minimum(code >> 6, slab_count - 1)
            product = jnp.dot(
                chosen[step * group + sub], slabs[slab], preferred_element_type=jnp.float32
            )
            products.append((code & 63, product))
        for block, product in products:
            totals[block] += product
        return carry

    lax.fori_loop(0, (total + group - 1) // group, body, 0)
    halves = out.shape[1] // height
    for block in range(blocks):
        out[block // halves, pl.ds((block % halves) * height, height), :] = totals[block].astype(
            jnp.bfloat16
        )


def split_wide(value):
    high = value.astype(jnp.bfloat16).astype(jnp.float32)
    return high, value - high


def bias_rows(pieces):
    rows = lax.broadcasted_iota(jnp.int32, (16, lanes), 0)
    block = jnp.zeros((16, lanes), jnp.float32)
    for index, piece in enumerate(pieces):
        block = jnp.where(rows == index, jnp.broadcast_to(piece, (16, lanes)), block)
    return block


def sum_rows(ref, start, size):
    value = ref[0, pl.ds(start, size), :].astype(jnp.float32)
    for index in range(1, ref.shape[0]):
        value = value + ref[index, pl.ds(start, size), :].astype(jnp.float32)
    return value


def dense_kernel(partials, weight, bias, cotangent, hidden, message, *, share):
    members = partials.shape[0]
    nodes = partials.shape[1]
    aggregate = sum_rows(partials, 0, nodes)
    weight_wide = weight[...].astype(jnp.float32)
    pre = (
        jnp.dot(
            aggregate,
            weight_wide,
            precision=lax.Precision.HIGHEST,
            preferred_element_type=jnp.float32,
        )
        + bias[...]
    )
    square = pre * pre
    angle = jnp.tanh(root_two_over_pi * (pre + cubic * (square * pre)))
    gate = 0.5 * (1.0 + angle)
    hidden[...] = (pre * gate).astype(jnp.bfloat16)
    inner = root_two_over_pi * (1.0 + 3.0 * cubic * square)
    gradient = gate + 0.5 * pre * (1.0 - angle * angle) * inner
    slope = (cotangent[...].astype(jnp.float32) * gradient).astype(jnp.bfloat16)
    slope_wide = slope.astype(jnp.float32)
    spread = lax.dot_general(
        slope, weight[...], (((1,), (1,)), ((), ())), preferred_element_type=jnp.float32
    ).astype(jnp.bfloat16)
    weight_part = lax.dot_general(
        aggregate,
        slope_wide,
        (((0,), (0,)), ((), ())),
        precision=lax.Precision.HIGHEST,
        preferred_element_type=jnp.float32,
    )
    bias_part = jnp.sum(slope_wide, axis=0, keepdims=True)
    high, low = split_wide(bias_part)
    bias_block = bias_rows([high[:, :lanes], high[:, lanes:], low[:, :lanes], low[:, lanes:]])
    bias_block = bias_block.astype(jnp.bfloat16)
    for member in range(members):
        message[member, pl.ds(0, nodes), :] = spread
        first = member * share % weight_part.shape[0]
        part = weight_part[first : first + share]
        part = jnp.concatenate([part[:, :lanes], part[:, lanes:]], axis=0)
        message[member, pl.ds(nodes, 2 * share), :] = part.astype(jnp.bfloat16)
        message[member, pl.ds(nodes + 2 * share, 16), :] = bias_block


def sum_bias(ref, start):
    block = sum_rows(ref, start, 16)
    return [block[0:1] + block[2:3], block[1:2] + block[3:4]]


def pack_bias(values):
    parts = [split_wide(value) for value in values]
    return bias_rows([parts[0][0], parts[1][0], parts[0][1], parts[1][1]]).astype(jnp.bfloat16)


def backward_kernel(codes, spreads, *refs, slots, height, blocks, nodes, share, far, across):
    tile_refs, outs = refs[:across], refs[across : across + far]
    shares, chosen, totals, picked = refs[across + far :]
    slab_count = totals.shape[0] - 1
    halves = nodes // height
    dummy = slab_count * 64 + blocks
    totals[...] = jnp.zeros_like(totals)
    total = pick_tiles(codes, tile_refs, chosen, picked, slots, height, dummy)

    def body(step, carry):
        products = []
        for sub in range(group):
            code = picked[step * group + sub]
            block = jnp.minimum(code & 63, blocks - 1)
            top = pl.multiple_of((block % halves) * height, height)
            product = lax.dot_general(
                chosen[step * group + sub],
                spreads[block // halves, pl.ds(top, height), :],
                (((0,), (0,)), ((), ())),
                preferred_element_type=jnp.float32,
            )
            products.append((code >> 6, product))
        for slab, product in products:
            totals[slab] += product
        return carry

    lax.fori_loop(0, (total + group - 1) // group, body, 0)
    near = slab_count // far
    for shift, out in enumerate(outs):
        for index in range(near):
            out[index] = totals[shift * near + index].astype(jnp.bfloat16)
    weight_sum = sum_rows(spreads, nodes, 2 * share).astype(jnp.bfloat16)
    bias_block = pack_bias(sum_bias(spreads, nodes + 2 * share))
    for index in range(near):
        shares[index, pl.ds(0, 2 * share), :] = weight_sum
        shares[index, pl.ds(2 * share, 16), :] = bias_block


def share_kernel(arrived, out, bias_block, *, share):
    total = sum_rows(arrived, 0, 2 * share).astype(jnp.bfloat16)
    for index in range(out.shape[0]):
        out[index] = total
    bias_block[...] = pack_bias(sum_bias(arrived, 2 * share))


def gather_kernel(shares, bias_block, out, *, share):
    rows = shares.shape[0] * share
    for index in range(shares.shape[0]):
        for half in range(2):
            part = shares[index, pl.ds(half * share, share), :]
            out[pl.ds(half * rows + index * share, share), :] = part
    out[pl.ds(2 * rows, 16), :] = bias_block[...]


def middle_kernel(*refs, far):
    out = refs[-1]
    for index in range(out.shape[0]):
        total = refs[0][index].astype(jnp.float32)
        for line in refs[1:far]:
            total = total + line[index].astype(jnp.float32)
        out[index] = total.astype(jnp.bfloat16)


def last_kernel(arrived, pieces, grad, weight_grad, bias_grad, *, factor):
    grad[...] = sum_rows(arrived, 0, grad.shape[0])
    rows = weight_grad.shape[0]
    weight_grad[:, pl.ds(0, lanes)] = sum_rows(pieces, 0, rows) * factor
    weight_grad[:, pl.ds(lanes, lanes)] = sum_rows(pieces, rows, rows) * factor
    low, high = sum_bias(pieces, 2 * rows)
    bias_grad[:, pl.ds(0, lanes)] = low * factor
    bias_grad[:, pl.ds(lanes, lanes)] = high * factor


def in_vmem():
    return pl.BlockSpec(memory_space=pltpu.VMEM)


def in_smem():
    return pl.BlockSpec(memory_space=pltpu.SMEM)


def local(features, tile_rows, tile_cols, tile_counts, tile_values, weight, bias, cotangent):
    nodes, width = features.shape
    slots, height, tile_width = tile_values.shape[2:]
    hidden = weight.shape[1]
    far = lax.axis_size("yhi")
    across = lax.axis_size("x")
    near = lax.axis_size("z")
    members = lax.axis_size(team_axes)
    group_rows = lax.axis_size(row_axes)
    here = lax.axis_index("x")
    params = pltpu.CompilerParams(vmem_limit_bytes=vmem_bytes)
    halves = nodes // height
    blocks = members * halves

    def any_place():
        return pl.BlockSpec(memory_space=pl.ANY)

    live = jnp.arange(slots, dtype=jnp.int32) < tile_counts[0, 0]
    columns, rows = tile_cols[0, 0], tile_rows[0, 0]
    owner = jnp.where(live, (columns // near) % across, 255)
    distance = (lax.axis_index("yhi") - columns // (across * near)) % far
    slab = distance * near + columns % near
    block = ((rows // halves) * across + here) * halves + rows % halves
    places = jnp.stack([owner, slab, block])
    ends = jnp.stack([jnp.int32(254), jnp.int32(0), tile_counts[0, 0]])[:, None]
    places = jnp.concatenate([places, ends], axis=1)
    places = jnp.pad(places, ((0, 13), (0, lanes - slots - 1))).astype(jnp.bfloat16)
    own = jnp.concatenate([tile_values[0, 0].reshape(slots * height, tile_width), places], axis=0)

    def ring(size, shift):
        return [(start, (start + shift) % size) for start in range(size)]

    longest_first = sorted(range(1, far), key=lambda shift: -min(shift, far - shift))

    buffers = [own]
    for shift in range(1, across):
        if shift != across // 2:
            buffers.append(lax.ppermute(own, "x", ring(across, shift)))

    lines = [spread_out(features, "z", near)]
    own, lines[0] = lax.optimization_barrier((own, lines[0]))
    buffers.append(lax.ppermute(own, "x", ring(across, across // 2)))
    line_order = [0] + longest_first[::-1]
    for shift in line_order[1:]:
        lines.append(lax.ppermute(lines[0], "yhi", ring(far, shift)))

    codes = pl.pallas_call(
        lambda *refs: codes_kernel(*refs, across=across, top=slots * height),
        out_shape=jax.ShapeDtypeStruct((across, lanes), jnp.int32),
        in_specs=[in_smem()] + [in_vmem()] * across + [any_place()] * (far - 1),
        out_specs=in_vmem(),
        compiler_params=params,
        name="tile_codes",
    )(here.reshape(1), *buffers, *lines[1:])

    scratch_tiles = pltpu.VMEM((across * slots + group, height, tile_width), jnp.bfloat16)
    scratch_list = pltpu.SMEM((across * slots + group,), jnp.int32)
    partial = pl.pallas_call(
        lambda *refs: forward_kernel(
            *refs,
            slots=slots,
            height=height,
            blocks=blocks,
            line_order=line_order,
            across=across,
        ),
        out_shape=jax.ShapeDtypeStruct((members, nodes, width), jnp.bfloat16),
        in_specs=[in_smem()] + [in_vmem()] * (far + across),
        out_specs=in_vmem(),
        scratch_shapes=[
            pltpu.VMEM((far * near, nodes, width), jnp.bfloat16),
            scratch_tiles,
            pltpu.VMEM((blocks + 1, height, width), jnp.float32),
            scratch_list,
        ],
        compiler_params=params,
        name="forward_tiles",
    )(codes, *lines, *buffers)
    partials = lax.all_to_all(partial, team_axes, 0, 0, tiled=True)

    holders = lax.axis_size(share_axes)
    share = width // holders
    hidden_out, message = pl.pallas_call(
        lambda *refs: dense_kernel(*refs, share=share),
        out_shape=(
            jax.ShapeDtypeStruct((nodes, hidden), jnp.bfloat16),
            jax.ShapeDtypeStruct((members, nodes + 2 * share + 16, width), jnp.bfloat16),
        ),
        in_specs=[in_vmem()] * 4,
        out_specs=(in_vmem(), in_vmem()),
        compiler_params=params,
        name="dense_layer",
    )(partials, weight, bias.reshape(1, hidden), cotangent)
    spreads = lax.all_to_all(message, team_axes, 0, 0, tiled=True)

    outs = pl.pallas_call(
        lambda *refs: backward_kernel(
            *refs,
            slots=slots,
            height=height,
            blocks=blocks,
            nodes=nodes,
            share=share,
            far=far,
            across=across,
        ),
        out_shape=(jax.ShapeDtypeStruct((near, nodes, width), jnp.bfloat16),) * far
        + (jax.ShapeDtypeStruct((near, 2 * share + 16, width), jnp.bfloat16),),
        in_specs=[in_smem(), in_vmem()] + [in_vmem()] * across,
        out_specs=(in_vmem(),) * (far + 1),
        scratch_shapes=[
            scratch_tiles,
            pltpu.VMEM((far * near + 1, nodes, width), jnp.float32),
            scratch_list,
        ],
        compiler_params=params,
        name="backward_tiles",
    )(codes, spreads, *buffers)

    lines = [outs[0]]
    for shift in longest_first:
        lines.append(lax.ppermute(outs[shift], "yhi", ring(far, -shift)))

    def gather_gradients(value):
        arrived = lax.all_to_all(value, "z", 0, 0, tiled=True)
        shares, bias_block = pl.pallas_call(
            lambda *refs: share_kernel(*refs, share=share),
            out_shape=(
                jax.ShapeDtypeStruct((holders, 2 * share, lanes), jnp.bfloat16),
                jax.ShapeDtypeStruct((16, lanes), jnp.bfloat16),
            ),
            in_specs=[in_vmem()],
            out_specs=(in_vmem(), in_vmem()),
            compiler_params=params,
            name="share_sum",
        )(arrived)
        shares = lax.all_to_all(shares, share_axes, 0, 0, tiled=True)
        return pl.pallas_call(
            lambda *refs: gather_kernel(*refs, share=share),
            out_shape=jax.ShapeDtypeStruct((2 * width + 16, lanes), jnp.bfloat16),
            in_specs=[in_vmem(), in_vmem()],
            out_specs=in_vmem(),
            compiler_params=params,
            name="share_gather",
        )(shares, bias_block)

    gradients = lax.cond(
        tile_counts[0, 0] > 0,
        gather_gradients,
        lambda value: jnp.zeros((2 * width + 16, lanes), jnp.bfloat16),
        outs[far],
    )
    line = pl.pallas_call(
        lambda *refs: middle_kernel(*refs, far=far),
        out_shape=jax.ShapeDtypeStruct((near, nodes, width), jnp.bfloat16),
        in_specs=[in_vmem()] * far + [any_place()],
        out_specs=in_vmem(),
        compiler_params=params,
        name="middle_sums",
    )(*lines, gradients)

    pieces = lax.all_gather(gradients, "yhi", axis=0)
    arrived = lax.all_to_all(line, "z", 0, 0, tiled=True)
    factor = 1.0 / math.sqrt(nodes * group_rows * far * across * near)
    features_grad, weight_grad, bias_grad = pl.pallas_call(
        lambda *refs: last_kernel(*refs, factor=factor),
        out_shape=(
            jax.ShapeDtypeStruct((nodes, width), jnp.float32),
            jax.ShapeDtypeStruct((width, hidden), jnp.float32),
            jax.ShapeDtypeStruct((1, hidden), jnp.float32),
        ),
        in_specs=[in_vmem(), in_vmem()],
        out_specs=(in_vmem(), in_vmem(), in_vmem()),
        compiler_params=params,
        name="last_sums",
    )(arrived, pieces)
    return (hidden_out, features_grad, weight_grad, bias_grad.reshape(hidden))


def solution(mesh):
    fine = Mesh(mesh.devices.reshape(row_split + col_split), axis_names)
    nodes_spec = P(row_axes + col_axes, None)
    in_specs = (
        nodes_spec,
        P(row_axes, col_axes, None),
        P(row_axes, col_axes, None),
        P(row_axes, col_axes),
        P(row_axes, col_axes, None, None, None),
        P(),
        P(),
        nodes_spec,
    )
    out_specs = (nodes_spec, nodes_spec, P(), P())
    return jax.shard_map(local, mesh=fine, in_specs=in_specs, out_specs=out_specs, check_vma=False)
```

```python
import math

import jax
import jax.numpy as jnp
from jax import lax
from jax.experimental import pallas as pl
from jax.experimental.pallas import tpu as pltpu
from jax.sharding import Mesh, PartitionSpec as P

row_split = (2, 2)
col_split = (2, 2, 4, 12)
axis_names = ("ylo", "core", "yfar", "ynear", "x", "z")
row_axes = ("ylo", "core")
y_axes = ("yfar", "ynear")
col_axes = y_axes + ("x", "z")
team_axes = ("ylo", "core", "x")
share_axes = ("core", "x")
group = 4
lanes = 128
vmem_bytes = 12 * 1024 * 1024
root_two_over_pi = math.sqrt(2.0 / math.pi)
cubic = 0.044715


def spread_out(value, axes, count):
    copies = jnp.broadcast_to(value[None], (count,) + value.shape)
    return lax.all_to_all(copies, axes, 0, 0, tiled=True)


def codes_kernel(here, *refs, across, top):
    out = refs[-1]
    for source in range(across):
        places = refs[source][pl.ds(top, 16), :].astype(jnp.float32).astype(jnp.int32)
        mine = (places[0:1] == here[0]) | (places[0:1] == 254)
        out[pl.ds(source, 1), :] = jnp.where(mine, places[1:2] * 64 + places[2:3], -1)


def pick_tiles(codes, tile_refs, chosen, picked, slots, height, dummy):
    total = jnp.int32(0)
    for source, tiles in enumerate(tile_refs):

        def body(step, total, source=source, tiles=tiles):
            for sub in range(group):
                slot = step * group + sub
                code = codes[source, slot]
                top = pl.multiple_of(slot * height, height)
                chosen[total] = tiles[pl.ds(top, height), :]
                picked[total] = code
                total = total + jnp.where(code >= 0, 1, 0)
            return total

        total = lax.fori_loop(0, (codes[source, slots] + group - 1) // group, body, total)
    for sub in range(group):
        picked[total + sub] = dummy
    return total


def forward_kernel(codes, partner, *refs, slots, height, blocks, line_order, across):
    far = len(line_order)
    lines, pair, tile_refs = refs[:far], refs[far], refs[far + 1 : far + 1 + across]
    out, slabs, chosen, totals, picked = refs[far + 1 + across :]
    slab_count = slabs.shape[0]
    near = slab_count // (far + 1)
    for shift, line in zip(line_order, lines):
        slabs[pl.ds(shift * near, near)] = line[...]
    slabs[pl.ds((far + 1) // 2 * near, near)] = pair[partner[0]]
    dummy = slab_count * 64 + blocks
    totals[...] = jnp.zeros_like(totals)
    total = pick_tiles(codes, tile_refs, chosen, picked, slots, height, dummy)

    def body(step, carry):
        products = []
        for sub in range(group):
            code = picked[step * group + sub]
            slab = jnp.minimum(code >> 6, slab_count - 1)
            product = jnp.dot(
                chosen[step * group + sub], slabs[slab], preferred_element_type=jnp.float32
            )
            products.append((code & 63, product))
        for block, product in products:
            totals[block] += product
        return carry

    lax.fori_loop(0, (total + group - 1) // group, body, 0)
    halves = out.shape[1] // height
    for block in range(blocks):
        out[block // halves, pl.ds((block % halves) * height, height), :] = totals[block].astype(
            jnp.bfloat16
        )


def split_wide(value):
    high = value.astype(jnp.bfloat16).astype(jnp.float32)
    return high, value - high


def bias_rows(pieces):
    rows = lax.broadcasted_iota(jnp.int32, (16, lanes), 0)
    block = jnp.zeros((16, lanes), jnp.float32)
    for index, piece in enumerate(pieces):
        block = jnp.where(rows == index, jnp.broadcast_to(piece, (16, lanes)), block)
    return block


def sum_rows(ref, start, size):
    value = ref[0, pl.ds(start, size), :].astype(jnp.float32)
    for index in range(1, ref.shape[0]):
        value = value + ref[index, pl.ds(start, size), :].astype(jnp.float32)
    return value


def dense_kernel(partials, weight, bias, cotangent, hidden, message, *, share):
    members = partials.shape[0]
    nodes = partials.shape[1]
    aggregate = sum_rows(partials, 0, nodes)
    weight_wide = weight[...].astype(jnp.float32)
    pre = (
        jnp.dot(
            aggregate,
            weight_wide,
            precision=lax.Precision.HIGHEST,
            preferred_element_type=jnp.float32,
        )
        + bias[...]
    )
    square = pre * pre
    angle = jnp.tanh(root_two_over_pi * (pre + cubic * (square * pre)))
    gate = 0.5 * (1.0 + angle)
    hidden[...] = (pre * gate).astype(jnp.bfloat16)
    inner = root_two_over_pi * (1.0 + 3.0 * cubic * square)
    gradient = gate + 0.5 * pre * (1.0 - angle * angle) * inner
    slope = (cotangent[...].astype(jnp.float32) * gradient).astype(jnp.bfloat16)
    slope_wide = slope.astype(jnp.float32)
    spread = lax.dot_general(
        slope, weight[...], (((1,), (1,)), ((), ())), preferred_element_type=jnp.float32
    ).astype(jnp.bfloat16)
    weight_part = lax.dot_general(
        aggregate,
        slope_wide,
        (((0,), (0,)), ((), ())),
        precision=lax.Precision.HIGHEST,
        preferred_element_type=jnp.float32,
    )
    bias_part = jnp.sum(slope_wide, axis=0, keepdims=True)
    high, low = split_wide(bias_part)
    bias_block = bias_rows([high[:, :lanes], high[:, lanes:], low[:, :lanes], low[:, lanes:]])
    bias_block = bias_block.astype(jnp.bfloat16)
    for member in range(members):
        message[member, pl.ds(0, nodes), :] = spread
        first = member * share % weight_part.shape[0]
        part = weight_part[first : first + share]
        part = jnp.concatenate([part[:, :lanes], part[:, lanes:]], axis=0)
        message[member, pl.ds(nodes, 2 * share), :] = part.astype(jnp.bfloat16)
        message[member, pl.ds(nodes + 2 * share, 16), :] = bias_block


def sum_bias(ref, start):
    block = sum_rows(ref, start, 16)
    return [block[0:1] + block[2:3], block[1:2] + block[3:4]]


def pack_bias(values):
    parts = [split_wide(value) for value in values]
    return bias_rows([parts[0][0], parts[1][0], parts[0][1], parts[1][1]]).astype(jnp.bfloat16)


def backward_kernel(codes, spreads, *refs, slots, height, blocks, nodes, share, far, across):
    tile_refs, outs = refs[:across], refs[across : across + far]
    shares, chosen, totals, picked = refs[across + far :]
    slab_count = totals.shape[0] - 1
    halves = nodes // height
    dummy = slab_count * 64 + blocks
    totals[...] = jnp.zeros_like(totals)
    total = pick_tiles(codes, tile_refs, chosen, picked, slots, height, dummy)

    def body(step, carry):
        products = []
        for sub in range(group):
            code = picked[step * group + sub]
            block = jnp.minimum(code & 63, blocks - 1)
            top = pl.multiple_of((block % halves) * height, height)
            product = lax.dot_general(
                chosen[step * group + sub],
                spreads[block // halves, pl.ds(top, height), :],
                (((0,), (0,)), ((), ())),
                preferred_element_type=jnp.float32,
            )
            products.append((code >> 6, product))
        for slab, product in products:
            totals[slab] += product
        return carry

    lax.fori_loop(0, (total + group - 1) // group, body, 0)
    near = slab_count // far
    for shift, out in enumerate(outs):
        for index in range(near):
            out[index] = totals[shift * near + index].astype(jnp.bfloat16)
    weight_sum = sum_rows(spreads, nodes, 2 * share).astype(jnp.bfloat16)
    bias_block = pack_bias(sum_bias(spreads, nodes + 2 * share))
    for index in range(near):
        shares[index, pl.ds(0, 2 * share), :] = weight_sum
        shares[index, pl.ds(2 * share, 16), :] = bias_block


def share_kernel(arrived, out, bias_block, *, share):
    total = sum_rows(arrived, 0, 2 * share).astype(jnp.bfloat16)
    for index in range(out.shape[0]):
        out[index] = total
    bias_block[...] = pack_bias(sum_bias(arrived, 2 * share))


def gather_kernel(shares, bias_block, out, *, share):
    rows = shares.shape[0] * share
    for index in range(shares.shape[0]):
        for half in range(2):
            part = shares[index, pl.ds(half * share, share), :]
            out[pl.ds(half * rows + index * share, share), :] = part
    out[pl.ds(2 * rows, 16), :] = bias_block[...]


def middle_kernel(*refs, far):
    out = refs[-1]
    for index in range(out.shape[0]):
        total = refs[0][index].astype(jnp.float32)
        for line in refs[1:far]:
            total = total + line[index].astype(jnp.float32)
        out[index] = total.astype(jnp.bfloat16)


def last_kernel(arrived, pieces, grad, weight_grad, bias_grad, *, factor):
    grad[...] = sum_rows(arrived, 0, grad.shape[0])
    rows = weight_grad.shape[0]
    weight_grad[:, pl.ds(0, lanes)] = sum_rows(pieces, 0, rows) * factor
    weight_grad[:, pl.ds(lanes, lanes)] = sum_rows(pieces, rows, rows) * factor
    low, high = sum_bias(pieces, 2 * rows)
    bias_grad[:, pl.ds(0, lanes)] = low * factor
    bias_grad[:, pl.ds(lanes, lanes)] = high * factor


def in_vmem():
    return pl.BlockSpec(memory_space=pltpu.VMEM)


def in_smem():
    return pl.BlockSpec(memory_space=pltpu.SMEM)


def local(features, tile_rows, tile_cols, tile_counts, tile_values, weight, bias, cotangent):
    nodes, width = features.shape
    slots, height, tile_width = tile_values.shape[2:]
    hidden = weight.shape[1]
    far = lax.axis_size(y_axes)
    across = lax.axis_size("x")
    near = lax.axis_size("z")
    members = lax.axis_size(team_axes)
    group_rows = lax.axis_size(row_axes)
    here = lax.axis_index("x")
    params = pltpu.CompilerParams(vmem_limit_bytes=vmem_bytes)
    halves = nodes // height
    blocks = members * halves

    def any_place():
        return pl.BlockSpec(memory_space=pl.ANY)

    live = jnp.arange(slots, dtype=jnp.int32) < tile_counts[0, 0]
    columns, rows = tile_cols[0, 0], tile_rows[0, 0]
    owner = jnp.where(live, (columns // near) % across, 255)
    distance = (lax.axis_index(y_axes) - columns // (across * near)) % far
    slab = distance * near + columns % near
    block = ((rows // halves) * across + here) * halves + rows % halves
    places = jnp.stack([owner, slab, block])
    ends = jnp.stack([jnp.int32(254), jnp.int32(0), tile_counts[0, 0]])[:, None]
    places = jnp.concatenate([places, ends], axis=1)
    places = jnp.pad(places, ((0, 13), (0, lanes - slots - 1))).astype(jnp.bfloat16)
    own = jnp.concatenate([tile_values[0, 0].reshape(slots * height, tile_width), places], axis=0)

    def ring(size, shift):
        return [(start, (start + shift) % size) for start in range(size)]

    longest_first = sorted(range(1, far), key=lambda shift: -min(shift, far - shift))

    buffers = [own]
    for shift in sorted(range(1, across), key=lambda shift: -min(shift, across - shift)):
        buffers.append(lax.ppermute(own, "x", ring(across, shift)))

    lines = [spread_out(features, "z", near)]
    line_order = [0] + [shift for shift in range(1, far) if shift != far // 2]
    pair = spread_out(lines[0], "yfar", 2)
    for shift in line_order[1:]:
        lines.append(lax.ppermute(lines[0], y_axes, ring(far, shift)))
    partner = (1 - lax.axis_index("yfar")).reshape(1)

    codes = pl.pallas_call(
        lambda *refs: codes_kernel(*refs, across=across, top=slots * height),
        out_shape=jax.ShapeDtypeStruct((across, lanes), jnp.int32),
        in_specs=[in_smem()] + [in_vmem()] * across + [any_place()] * (far - 1),
        out_specs=in_vmem(),
        compiler_params=params,
        name="tile_codes",
    )(here.reshape(1), *buffers, *lines[1:], pair)

    scratch_tiles = pltpu.VMEM((across * slots + group, height, tile_width), jnp.bfloat16)
    scratch_list = pltpu.SMEM((across * slots + group,), jnp.int32)
    partial = pl.pallas_call(
        lambda *refs: forward_kernel(
            *refs,
            slots=slots,
            height=height,
            blocks=blocks,
            line_order=line_order,
            across=across,
        ),
        out_shape=jax.ShapeDtypeStruct((members, nodes, width), jnp.bfloat16),
        in_specs=[in_smem(), in_smem()] + [in_vmem()] * (far + across),
        out_specs=in_vmem(),
        scratch_shapes=[
            pltpu.VMEM((far * near, nodes, width), jnp.bfloat16),
            scratch_tiles,
            pltpu.VMEM((blocks + 1, height, width), jnp.float32),
            scratch_list,
        ],
        compiler_params=params,
        name="forward_tiles",
    )(codes, partner, *lines, pair, *buffers)
    partials = lax.all_to_all(partial, team_axes, 0, 0, tiled=True)

    holders = lax.axis_size(share_axes)
    share = width // holders
    hidden_out, message = pl.pallas_call(
        lambda *refs: dense_kernel(*refs, share=share),
        out_shape=(
            jax.ShapeDtypeStruct((nodes, hidden), jnp.bfloat16),
            jax.ShapeDtypeStruct((members, nodes + 2 * share + 16, width), jnp.bfloat16),
        ),
        in_specs=[in_vmem()] * 4,
        out_specs=(in_vmem(), in_vmem()),
        compiler_params=params,
        name="dense_layer",
    )(partials, weight, bias.reshape(1, hidden), cotangent)
    spreads = lax.all_to_all(message, team_axes, 0, 0, tiled=True)

    outs = pl.pallas_call(
        lambda *refs: backward_kernel(
            *refs,
            slots=slots,
            height=height,
            blocks=blocks,
            nodes=nodes,
            share=share,
            far=far,
            across=across,
        ),
        out_shape=(jax.ShapeDtypeStruct((near, nodes, width), jnp.bfloat16),) * far
        + (jax.ShapeDtypeStruct((near, 2 * share + 16, width), jnp.bfloat16),),
        in_specs=[in_smem(), in_vmem()] + [in_vmem()] * across,
        out_specs=(in_vmem(),) * (far + 1),
        scratch_shapes=[
            scratch_tiles,
            pltpu.VMEM((far * near + 1, nodes, width), jnp.float32),
            scratch_list,
        ],
        compiler_params=params,
        name="backward_tiles",
    )(codes, spreads, *buffers)

    lines = [outs[0]]
    for shift in longest_first:
        lines.append(lax.ppermute(outs[shift], y_axes, ring(far, -shift)))

    def gather_gradients(value):
        arrived = lax.all_to_all(value, "z", 0, 0, tiled=True)
        shares, bias_block = pl.pallas_call(
            lambda *refs: share_kernel(*refs, share=share),
            out_shape=(
                jax.ShapeDtypeStruct((holders, 2 * share, lanes), jnp.bfloat16),
                jax.ShapeDtypeStruct((16, lanes), jnp.bfloat16),
            ),
            in_specs=[in_vmem()],
            out_specs=(in_vmem(), in_vmem()),
            compiler_params=params,
            name="share_sum",
        )(arrived)
        shares = lax.all_to_all(shares, share_axes, 0, 0, tiled=True)
        return pl.pallas_call(
            lambda *refs: gather_kernel(*refs, share=share),
            out_shape=jax.ShapeDtypeStruct((2 * width + 16, lanes), jnp.bfloat16),
            in_specs=[in_vmem(), in_vmem()],
            out_specs=in_vmem(),
            compiler_params=params,
            name="share_gather",
        )(shares, bias_block)

    gradients = lax.cond(
        tile_counts[0, 0] > 0,
        gather_gradients,
        lambda value: jnp.zeros((2 * width + 16, lanes), jnp.bfloat16),
        outs[far],
    )
    line = pl.pallas_call(
        lambda *refs: middle_kernel(*refs, far=far),
        out_shape=jax.ShapeDtypeStruct((near, nodes, width), jnp.bfloat16),
        in_specs=[in_vmem()] * far + [any_place()],
        out_specs=in_vmem(),
        compiler_params=params,
        name="middle_sums",
    )(*lines, gradients)

    pieces = lax.all_gather(gradients, y_axes, axis=0)
    arrived = lax.all_to_all(line, "z", 0, 0, tiled=True)
    factor = 1.0 / math.sqrt(nodes * group_rows * far * across * near)
    features_grad, weight_grad, bias_grad = pl.pallas_call(
        lambda *refs: last_kernel(*refs, factor=factor),
        out_shape=(
            jax.ShapeDtypeStruct((nodes, width), jnp.float32),
            jax.ShapeDtypeStruct((width, hidden), jnp.float32),
            jax.ShapeDtypeStruct((1, hidden), jnp.float32),
        ),
        in_specs=[in_vmem(), in_vmem()],
        out_specs=(in_vmem(), in_vmem(), in_vmem()),
        compiler_params=params,
        name="last_sums",
    )(arrived, pieces)
    return (hidden_out, features_grad, weight_grad, bias_grad.reshape(hidden))


def solution(mesh):
    fine = Mesh(mesh.devices.reshape(row_split + col_split), axis_names)
    nodes_spec = P(row_axes + col_axes, None)
    in_specs = (
        nodes_spec,
        P(row_axes, col_axes, None),
        P(row_axes, col_axes, None),
        P(row_axes, col_axes),
        P(row_axes, col_axes, None, None, None),
        P(),
        P(),
        nodes_spec,
    )
    out_specs = (nodes_spec, nodes_spec, P(), P())
    return jax.shard_map(local, mesh=fine, in_specs=in_specs, out_specs=out_specs, check_vma=False)
```

```python
import math

import jax
import jax.numpy as jnp
from jax import lax
from jax.experimental import pallas as pl
from jax.experimental.pallas import tpu as pltpu
from jax.sharding import Mesh, PartitionSpec as P

row_split = (2, 2)
col_split = (4, 4, 12)
axis_names = ("ylo", "core", "yhi", "x", "z")
row_axes = ("ylo", "core")
col_axes = ("yhi", "x", "z")
team_axes = ("ylo", "core", "x")
share_axes = ("core", "x")
tail_rows = 64
group = 4
lanes = 128
vmem_bytes = 12 * 1024 * 1024
root_two_over_pi = math.sqrt(2.0 / math.pi)
cubic = 0.044715


def spread_out(value, axes, count):
    copies = jnp.broadcast_to(value[None], (count,) + value.shape)
    return lax.all_to_all(copies, axes, 0, 0, tiled=True)


def codes_kernel(here, *refs, across, top):
    out = refs[-1]
    for source in range(across):
        places = refs[source][pl.ds(top, 16), :].astype(jnp.float32).astype(jnp.int32)
        mine = (places[0:1] == here[0]) | (places[0:1] == 254)
        out[pl.ds(source, 1), :] = jnp.where(mine, places[1:2] * 64 + places[2:3], -1)


def pick_tiles(codes, tile_refs, chosen, picked, slots, height, dummy):
    total = jnp.int32(0)
    for source, tiles in enumerate(tile_refs):

        def body(step, total, source=source, tiles=tiles):
            for sub in range(group):
                slot = step * group + sub
                code = codes[source, slot]
                top = pl.multiple_of(slot * height, height)
                chosen[total] = tiles[pl.ds(top, height), :]
                picked[total] = code
                total = total + jnp.where(code >= 0, 1, 0)
            return total

        total = lax.fori_loop(0, (codes[source, slots] + group - 1) // group, body, total)
    for sub in range(group):
        picked[total + sub] = dummy
    return total


def forward_kernel(codes, *refs, slots, height, blocks, line_order, across):
    far = len(line_order)
    lines, tile_refs = refs[:far], refs[far : far + across]
    out, slabs, chosen, totals, picked = refs[far + across :]
    slab_count = slabs.shape[0]
    near = slab_count // far
    for shift, line in zip(line_order, lines):
        slabs[pl.ds(shift * near, near)] = line[...]
    dummy = slab_count * 64 + blocks
    totals[...] = jnp.zeros_like(totals)
    total = pick_tiles(codes, tile_refs, chosen, picked, slots, height, dummy)

    def body(step, carry):
        products = []
        for sub in range(group):
            code = picked[step * group + sub]
            slab = jnp.minimum(code >> 6, slab_count - 1)
            product = jnp.dot(
                chosen[step * group + sub], slabs[slab], preferred_element_type=jnp.float32
            )
            products.append((code & 63, product))
        for block, product in products:
            totals[block] += product
        return carry

    lax.fori_loop(0, (total + group - 1) // group, body, 0)
    halves = out.shape[1] // height
    for block in range(blocks):
        out[block // halves, pl.ds((block % halves) * height, height), :] = totals[block].astype(
            jnp.bfloat16
        )


def split_wide(value):
    high = value.astype(jnp.bfloat16).astype(jnp.float32)
    return high, value - high


def bias_rows(pieces):
    rows = lax.broadcasted_iota(jnp.int32, (16, lanes), 0)
    block = jnp.zeros((16, lanes), jnp.float32)
    for index, piece in enumerate(pieces):
        block = jnp.where(rows == index, jnp.broadcast_to(piece, (16, lanes)), block)
    return block


def sum_rows(ref, start, size):
    value = ref[0, pl.ds(start, size), :].astype(jnp.float32)
    for index in range(1, ref.shape[0]):
        value = value + ref[index, pl.ds(start, size), :].astype(jnp.float32)
    return value


def dense_kernel(partials, weight, bias, cotangent, hidden, message, *, share):
    members = partials.shape[0]
    nodes = partials.shape[1]
    aggregate = sum_rows(partials, 0, nodes)
    weight_wide = weight[...].astype(jnp.float32)
    pre = (
        jnp.dot(
            aggregate,
            weight_wide,
            precision=lax.Precision.HIGHEST,
            preferred_element_type=jnp.float32,
        )
        + bias[...]
    )
    square = pre * pre
    angle = jnp.tanh(root_two_over_pi * (pre + cubic * (square * pre)))
    gate = 0.5 * (1.0 + angle)
    hidden[...] = (pre * gate).astype(jnp.bfloat16)
    inner = root_two_over_pi * (1.0 + 3.0 * cubic * square)
    gradient = gate + 0.5 * pre * (1.0 - angle * angle) * inner
    slope = (cotangent[...].astype(jnp.float32) * gradient).astype(jnp.bfloat16)
    slope_wide = slope.astype(jnp.float32)
    spread = lax.dot_general(
        slope, weight[...], (((1,), (1,)), ((), ())), preferred_element_type=jnp.float32
    ).astype(jnp.bfloat16)
    weight_part = lax.dot_general(
        aggregate,
        slope_wide,
        (((0,), (0,)), ((), ())),
        precision=lax.Precision.HIGHEST,
        preferred_element_type=jnp.float32,
    )
    bias_part = jnp.sum(slope_wide, axis=0, keepdims=True)
    high, low = split_wide(bias_part)
    bias_block = bias_rows([high[:, :lanes], high[:, lanes:], low[:, :lanes], low[:, lanes:]])
    bias_block = bias_block.astype(jnp.bfloat16)
    for member in range(members):
        message[member, pl.ds(0, nodes), :] = spread
        first = member * share % weight_part.shape[0]
        part = weight_part[first : first + share]
        part = jnp.concatenate([part[:, :lanes], part[:, lanes:]], axis=0)
        message[member, pl.ds(nodes, 2 * share), :] = part.astype(jnp.bfloat16)
        message[member, pl.ds(nodes + 2 * share, 16), :] = bias_block


def sum_bias(ref, start):
    block = sum_rows(ref, start, 16)
    return [block[0:1] + block[2:3], block[1:2] + block[3:4]]


def pack_bias(values):
    parts = [split_wide(value) for value in values]
    return bias_rows([parts[0][0], parts[1][0], parts[0][1], parts[1][1]]).astype(jnp.bfloat16)


def backward_kernel(codes, spreads, *refs, slots, height, blocks, nodes, share, far, across):
    tile_refs, outs = refs[:across], refs[across : across + far]
    shares, chosen, totals, picked = refs[across + far :]
    slab_count = totals.shape[0] - 1
    halves = nodes // height
    dummy = slab_count * 64 + blocks
    totals[...] = jnp.zeros_like(totals)
    total = pick_tiles(codes, tile_refs, chosen, picked, slots, height, dummy)

    def body(step, carry):
        products = []
        for sub in range(group):
            code = picked[step * group + sub]
            block = jnp.minimum(code & 63, blocks - 1)
            top = pl.multiple_of((block % halves) * height, height)
            product = lax.dot_general(
                chosen[step * group + sub],
                spreads[block // halves, pl.ds(top, height), :],
                (((0,), (0,)), ((), ())),
                preferred_element_type=jnp.float32,
            )
            products.append((code >> 6, product))
        for slab, product in products:
            totals[slab] += product
        return carry

    lax.fori_loop(0, (total + group - 1) // group, body, 0)
    near = slab_count // far
    for shift, out in enumerate(outs):
        rows = out.shape[1]
        for index in range(near):
            total = totals[shift * near + index].astype(jnp.bfloat16)
            out[index] = total[:rows]
            if rows < nodes:
                shares[index, pl.ds(2 * share + 16, nodes - rows), :] = total[rows:]
    weight_sum = sum_rows(spreads, nodes, 2 * share).astype(jnp.bfloat16)
    bias_block = pack_bias(sum_bias(spreads, nodes + 2 * share))
    for index in range(near):
        shares[index, pl.ds(0, 2 * share), :] = weight_sum
        shares[index, pl.ds(2 * share, 16), :] = bias_block


def share_kernel(arrived, out):
    rows = out.shape[0]
    share_rows = rows - 16 - tail_rows
    out[pl.ds(0, share_rows), :] = sum_rows(arrived, 0, share_rows).astype(jnp.bfloat16)
    out[pl.ds(share_rows, 16), :] = pack_bias(sum_bias(arrived, share_rows))
    out[pl.ds(share_rows + 16, tail_rows), :] = sum_rows(
        arrived, share_rows + 16, tail_rows
    ).astype(jnp.bfloat16)


def share_sum_kernel(pieces, out):
    out[...] = sum_rows(pieces, 0, out.shape[0])


def middle_kernel(*refs, far):
    lines, out = refs[:far], refs[-1]
    nodes = out.shape[1]
    rows = min(line.shape[1] for line in lines)
    for index in range(out.shape[0]):
        for top, size in ((0, rows), (rows, nodes - rows)):
            total = jnp.zeros((size, lanes), jnp.float32)
            for line in lines:
                if top < line.shape[1]:
                    total = total + line[index, pl.ds(top, size), :].astype(jnp.float32)
            out[index, pl.ds(top, size), :] = total.astype(jnp.bfloat16)


def last_kernel(opposite, arrived, pieces, shares, grad, weight_grad, bias_grad, *, factor):
    share_rows = shares.shape[1]
    share = share_rows // 2
    lead = grad.shape[0] - tail_rows
    grad[pl.ds(0, lead), :] = sum_rows(arrived, 0, lead)
    late = pieces[opposite[0], pl.ds(share_rows + 16, tail_rows), :].astype(jnp.float32)
    grad[pl.ds(lead, tail_rows), :] = sum_rows(arrived, lead, tail_rows) + late
    for index in range(shares.shape[0]):
        for half in range(2):
            part = shares[index, pl.ds(half * share, share), :] * factor
            weight_grad[pl.ds(index * share, share), pl.ds(half * lanes, lanes)] = part
    low, high = sum_bias(pieces, share_rows)
    bias_grad[:, pl.ds(0, lanes)] = low * factor
    bias_grad[:, pl.ds(lanes, lanes)] = high * factor


def in_vmem():
    return pl.BlockSpec(memory_space=pltpu.VMEM)


def in_smem():
    return pl.BlockSpec(memory_space=pltpu.SMEM)


def local(features, tile_rows, tile_cols, tile_counts, tile_values, weight, bias, cotangent):
    nodes, width = features.shape
    slots, height, tile_width = tile_values.shape[2:]
    hidden = weight.shape[1]
    far = lax.axis_size("yhi")
    across = lax.axis_size("x")
    near = lax.axis_size("z")
    members = lax.axis_size(team_axes)
    group_rows = lax.axis_size(row_axes)
    here = lax.axis_index("x")
    params = pltpu.CompilerParams(vmem_limit_bytes=vmem_bytes)
    halves = nodes // height
    blocks = members * halves

    def any_place():
        return pl.BlockSpec(memory_space=pl.ANY)

    live = jnp.arange(slots, dtype=jnp.int32) < tile_counts[0, 0]
    columns, rows = tile_cols[0, 0], tile_rows[0, 0]
    owner = jnp.where(live, (columns // near) % across, 255)
    distance = (lax.axis_index("yhi") - columns // (across * near)) % far
    slab = distance * near + columns % near
    block = ((rows // halves) * across + here) * halves + rows % halves
    places = jnp.stack([owner, slab, block])
    ends = jnp.stack([jnp.int32(254), jnp.int32(0), tile_counts[0, 0]])[:, None]
    places = jnp.concatenate([places, ends], axis=1)
    places = jnp.pad(places, ((0, 13), (0, lanes - slots - 1))).astype(jnp.bfloat16)
    own = jnp.concatenate([tile_values[0, 0].reshape(slots * height, tile_width), places], axis=0)

    def ring(size, shift):
        return [(start, (start + shift) % size) for start in range(size)]

    longest_first = sorted(range(1, far), key=lambda shift: -min(shift, far - shift))

    buffers = [own]
    for shift in sorted(range(1, across), key=lambda shift: -min(shift, across - shift)):
        buffers.append(lax.ppermute(own, "x", ring(across, shift)))

    lines = [spread_out(features, "z", near)]
    line_order = [0] + longest_first[::-1]
    for shift in line_order[1:]:
        lines.append(lax.ppermute(lines[0], "yhi", ring(far, shift)))

    codes = pl.pallas_call(
        lambda *refs: codes_kernel(*refs, across=across, top=slots * height),
        out_shape=jax.ShapeDtypeStruct((across, lanes), jnp.int32),
        in_specs=[in_smem()] + [in_vmem()] * across + [any_place()] * (far - 1),
        out_specs=in_vmem(),
        compiler_params=params,
        name="tile_codes",
    )(here.reshape(1), *buffers, *lines[1:])

    scratch_tiles = pltpu.VMEM((across * slots + group, height, tile_width), jnp.bfloat16)
    scratch_list = pltpu.SMEM((across * slots + group,), jnp.int32)
    partial = pl.pallas_call(
        lambda *refs: forward_kernel(
            *refs,
            slots=slots,
            height=height,
            blocks=blocks,
            line_order=line_order,
            across=across,
        ),
        out_shape=jax.ShapeDtypeStruct((members, nodes, width), jnp.bfloat16),
        in_specs=[in_smem()] + [in_vmem()] * (far + across),
        out_specs=in_vmem(),
        scratch_shapes=[
            pltpu.VMEM((far * near, nodes, width), jnp.bfloat16),
            scratch_tiles,
            pltpu.VMEM((blocks + 1, height, width), jnp.float32),
            scratch_list,
        ],
        compiler_params=params,
        name="forward_tiles",
    )(codes, *lines, *buffers)
    partials = lax.all_to_all(partial, team_axes, 0, 0, tiled=True)

    holders = lax.axis_size(share_axes)
    share = width // holders
    hidden_out, message = pl.pallas_call(
        lambda *refs: dense_kernel(*refs, share=share),
        out_shape=(
            jax.ShapeDtypeStruct((nodes, hidden), jnp.bfloat16),
            jax.ShapeDtypeStruct((members, nodes + 2 * share + 16, width), jnp.bfloat16),
        ),
        in_specs=[in_vmem()] * 4,
        out_specs=(in_vmem(), in_vmem()),
        compiler_params=params,
        name="dense_layer",
    )(partials, weight, bias.reshape(1, hidden), cotangent)
    spreads = lax.all_to_all(message, team_axes, 0, 0, tiled=True)

    opposite = far // 2
    outs = pl.pallas_call(
        lambda *refs: backward_kernel(
            *refs,
            slots=slots,
            height=height,
            blocks=blocks,
            nodes=nodes,
            share=share,
            far=far,
            across=across,
        ),
        out_shape=tuple(
            jax.ShapeDtypeStruct(
                (near, nodes - (tail_rows if shift == opposite else 0), width), jnp.bfloat16
            )
            for shift in range(far)
        )
        + (jax.ShapeDtypeStruct((near, 2 * share + 16 + tail_rows, width), jnp.bfloat16),),
        in_specs=[in_smem(), in_vmem()] + [in_vmem()] * across,
        out_specs=(in_vmem(),) * (far + 1),
        scratch_shapes=[
            scratch_tiles,
            pltpu.VMEM((far * near + 1, nodes, width), jnp.float32),
            scratch_list,
        ],
        compiler_params=params,
        name="backward_tiles",
    )(codes, spreads, *buffers)

    lines = [outs[0]]
    for shift in longest_first:
        lines.append(lax.ppermute(outs[shift], "yhi", ring(far, -shift)))

    small_shape = (2 * share + 16 + tail_rows, lanes)

    def gather_gradients(value):
        arrived = lax.all_to_all(value, "z", 0, 0, tiled=True)
        return pl.pallas_call(
            share_kernel,
            out_shape=jax.ShapeDtypeStruct(small_shape, jnp.bfloat16),
            in_specs=[in_vmem()],
            out_specs=in_vmem(),
            compiler_params=params,
            name="share_sum",
        )(arrived)

    gradients = lax.cond(
        tile_counts[0, 0] > 0,
        gather_gradients,
        lambda value: jnp.zeros(small_shape, jnp.bfloat16),
        outs[far],
    )
    line = pl.pallas_call(
        lambda *refs: middle_kernel(*refs, far=far),
        out_shape=jax.ShapeDtypeStruct((near, nodes, width), jnp.bfloat16),
        in_specs=[in_vmem()] * far + [any_place()],
        out_specs=in_vmem(),
        compiler_params=params,
        name="middle_sums",
    )(*lines, gradients)

    pieces = lax.all_gather(gradients, "yhi", axis=0)
    shares = pl.pallas_call(
        share_sum_kernel,
        out_shape=jax.ShapeDtypeStruct((2 * share, lanes), jnp.float32),
        in_specs=[in_vmem()],
        out_specs=in_vmem(),
        compiler_params=params,
        name="share_sum_far",
    )(pieces)
    shares = lax.all_gather(shares, share_axes, axis=0)
    arrived = lax.all_to_all(line, "z", 0, 0, tiled=True)
    factor = 1.0 / math.sqrt(nodes * group_rows * far * across * near)
    features_grad, weight_grad, bias_grad = pl.pallas_call(
        lambda *refs: last_kernel(*refs, factor=factor),
        out_shape=(
            jax.ShapeDtypeStruct((nodes, width), jnp.float32),
            jax.ShapeDtypeStruct((width, hidden), jnp.float32),
            jax.ShapeDtypeStruct((1, hidden), jnp.float32),
        ),
        in_specs=[in_smem()] + [in_vmem()] * 3,
        out_specs=(in_vmem(), in_vmem(), in_vmem()),
        compiler_params=params,
        name="last_sums",
    )(((lax.axis_index("yhi") + opposite) % far).reshape(1), arrived, pieces, shares)
    return (hidden_out, features_grad, weight_grad, bias_grad.reshape(hidden))


def solution(mesh):
    fine = Mesh(mesh.devices.reshape(row_split + col_split), axis_names)
    nodes_spec = P(row_axes + col_axes, None)
    in_specs = (
        nodes_spec,
        P(row_axes, col_axes, None),
        P(row_axes, col_axes, None),
        P(row_axes, col_axes),
        P(row_axes, col_axes, None, None, None),
        P(),
        P(),
        nodes_spec,
    )
    out_specs = (nodes_spec, nodes_spec, P(), P())
    return jax.shard_map(local, mesh=fine, in_specs=in_specs, out_specs=out_specs, check_vma=False)
```

```python
import math

import jax
import jax.numpy as jnp
from jax import lax
from jax.experimental import pallas as pl
from jax.experimental.pallas import tpu as pltpu
from jax.sharding import Mesh, PartitionSpec as P

row_split = (2, 2)
col_split = (4, 4, 12)
axis_names = ("ylo", "core", "yhi", "x", "z")
row_axes = ("ylo", "core")
col_axes = ("yhi", "x", "z")
team_axes = ("ylo", "core", "x")
share_axes = ("core", "x")
tail_rows = 16
group = 4
lanes = 128
vmem_bytes = 12 * 1024 * 1024
root_two_over_pi = math.sqrt(2.0 / math.pi)
cubic = 0.044715


def spread_out(value, axes, count):
    copies = jnp.broadcast_to(value[None], (count,) + value.shape)
    return lax.all_to_all(copies, axes, 0, 0, tiled=True)


def codes_kernel(here, *refs, across, top):
    out = refs[-1]
    for source in range(across):
        places = refs[source][pl.ds(top, 16), :].astype(jnp.float32).astype(jnp.int32)
        mine = (places[0:1] == here[0]) | (places[0:1] == 254)
        out[pl.ds(source, 1), :] = jnp.where(mine, places[1:2] * 64 + places[2:3], -1)


def pick_tiles(codes, tile_refs, chosen, picked, slots, height, dummy):
    total = jnp.int32(0)
    for source, tiles in enumerate(tile_refs):

        def body(step, total, source=source, tiles=tiles):
            for sub in range(group):
                slot = step * group + sub
                code = codes[source, slot]
                top = pl.multiple_of(slot * height, height)
                chosen[total] = tiles[pl.ds(top, height), :]
                picked[total] = code
                total = total + jnp.where(code >= 0, 1, 0)
            return total

        total = lax.fori_loop(0, (codes[source, slots] + group - 1) // group, body, total)
    for sub in range(group):
        picked[total + sub] = dummy
    return total


def forward_kernel(codes, *refs, slots, height, blocks, line_order, across):
    far = len(line_order)
    lines, tile_refs = refs[:far], refs[far : far + across]
    out, slabs, chosen, totals, picked = refs[far + across :]
    slab_count = slabs.shape[0]
    near = slab_count // far
    for shift, line in zip(line_order, lines):
        slabs[pl.ds(shift * near, near)] = line[...]
    dummy = slab_count * 64 + blocks
    totals[...] = jnp.zeros_like(totals)
    total = pick_tiles(codes, tile_refs, chosen, picked, slots, height, dummy)

    def body(step, carry):
        products = []
        for sub in range(group):
            code = picked[step * group + sub]
            slab = jnp.minimum(code >> 6, slab_count - 1)
            product = jnp.dot(
                chosen[step * group + sub], slabs[slab], preferred_element_type=jnp.float32
            )
            products.append((code & 63, product))
        for block, product in products:
            totals[block] += product
        return carry

    lax.fori_loop(0, (total + group - 1) // group, body, 0)
    halves = out.shape[1] // height
    for block in range(blocks):
        out[block // halves, pl.ds((block % halves) * height, height), :] = totals[block].astype(
            jnp.bfloat16
        )


def split_wide(value):
    high = value.astype(jnp.bfloat16).astype(jnp.float32)
    return high, value - high


def bias_rows(pieces):
    rows = lax.broadcasted_iota(jnp.int32, (16, lanes), 0)
    block = jnp.zeros((16, lanes), jnp.float32)
    for index, piece in enumerate(pieces):
        block = jnp.where(rows == index, jnp.broadcast_to(piece, (16, lanes)), block)
    return block


def sum_rows(ref, start, size):
    value = ref[0, pl.ds(start, size), :].astype(jnp.float32)
    for index in range(1, ref.shape[0]):
        value = value + ref[index, pl.ds(start, size), :].astype(jnp.float32)
    return value


def dense_kernel(partials, weight, bias, cotangent, hidden, message, *, share):
    members = partials.shape[0]
    nodes = partials.shape[1]
    aggregate = sum_rows(partials, 0, nodes)
    weight_wide = weight[...].astype(jnp.float32)
    pre = (
        jnp.dot(
            aggregate,
            weight_wide,
            precision=lax.Precision.HIGHEST,
            preferred_element_type=jnp.float32,
        )
        + bias[...]
    )
    square = pre * pre
    angle = jnp.tanh(root_two_over_pi * (pre + cubic * (square * pre)))
    gate = 0.5 * (1.0 + angle)
    hidden[...] = (pre * gate).astype(jnp.bfloat16)
    inner = root_two_over_pi * (1.0 + 3.0 * cubic * square)
    gradient = gate + 0.5 * pre * (1.0 - angle * angle) * inner
    slope = (cotangent[...].astype(jnp.float32) * gradient).astype(jnp.bfloat16)
    slope_wide = slope.astype(jnp.float32)
    spread = lax.dot_general(
        slope, weight[...], (((1,), (1,)), ((), ())), preferred_element_type=jnp.float32
    ).astype(jnp.bfloat16)
    weight_part = lax.dot_general(
        aggregate,
        slope_wide,
        (((0,), (0,)), ((), ())),
        precision=lax.Precision.HIGHEST,
        preferred_element_type=jnp.float32,
    )
    bias_part = jnp.sum(slope_wide, axis=0, keepdims=True)
    high, low = split_wide(bias_part)
    bias_block = bias_rows([high[:, :lanes], high[:, lanes:], low[:, :lanes], low[:, lanes:]])
    bias_block = bias_block.astype(jnp.bfloat16)
    for member in range(members):
        message[member, pl.ds(0, nodes), :] = spread
        first = member * share % weight_part.shape[0]
        part = weight_part[first : first + share]
        part = jnp.concatenate([part[:, :lanes], part[:, lanes:]], axis=0)
        message[member, pl.ds(nodes, 2 * share), :] = part.astype(jnp.bfloat16)
        message[member, pl.ds(nodes + 2 * share, 16), :] = bias_block


def sum_bias(ref, start):
    block = sum_rows(ref, start, 16)
    return [block[0:1] + block[2:3], block[1:2] + block[3:4]]


def pack_bias(values):
    parts = [split_wide(value) for value in values]
    return bias_rows([parts[0][0], parts[1][0], parts[0][1], parts[1][1]]).astype(jnp.bfloat16)


def backward_kernel(codes, spreads, *refs, slots, height, blocks, nodes, share, far, across):
    tile_refs, outs = refs[:across], refs[across : across + far]
    shares, chosen, totals, picked = refs[across + far :]
    slab_count = totals.shape[0] - 1
    halves = nodes // height
    dummy = slab_count * 64 + blocks
    totals[...] = jnp.zeros_like(totals)
    total = pick_tiles(codes, tile_refs, chosen, picked, slots, height, dummy)

    def body(step, carry):
        products = []
        for sub in range(group):
            code = picked[step * group + sub]
            block = jnp.minimum(code & 63, blocks - 1)
            top = pl.multiple_of((block % halves) * height, height)
            product = lax.dot_general(
                chosen[step * group + sub],
                spreads[block // halves, pl.ds(top, height), :],
                (((0,), (0,)), ((), ())),
                preferred_element_type=jnp.float32,
            )
            products.append((code >> 6, product))
        for slab, product in products:
            totals[slab] += product
        return carry

    lax.fori_loop(0, (total + group - 1) // group, body, 0)
    near = slab_count // far
    for shift, out in enumerate(outs):
        rows = out.shape[1]
        for index in range(near):
            total = totals[shift * near + index].astype(jnp.bfloat16)
            out[index] = total[:rows]
            if rows < nodes:
                shares[index, pl.ds(2 * share + 16, nodes - rows), :] = total[rows:]
    weight_sum = sum_rows(spreads, nodes, 2 * share).astype(jnp.bfloat16)
    bias_block = pack_bias(sum_bias(spreads, nodes + 2 * share))
    for index in range(near):
        shares[index, pl.ds(0, 2 * share), :] = weight_sum
        shares[index, pl.ds(2 * share, 16), :] = bias_block


def share_kernel(arrived, out, bias_block, tail, *, share):
    total = sum_rows(arrived, 0, 2 * share).astype(jnp.bfloat16)
    for index in range(out.shape[0]):
        out[index] = total
    bias_block[...] = pack_bias(sum_bias(arrived, 2 * share))
    tail[...] = sum_rows(arrived, 2 * share + 16, tail.shape[0]).astype(jnp.bfloat16)


def gather_kernel(shares, bias_block, tail, out, *, share):
    rows = shares.shape[0] * share
    for index in range(shares.shape[0]):
        for half in range(2):
            part = shares[index, pl.ds(half * share, share), :]
            out[pl.ds(half * rows + index * share, share), :] = part
    out[pl.ds(2 * rows, 16), :] = bias_block[...]
    out[pl.ds(2 * rows + 16, tail.shape[0]), :] = tail[...]


def middle_kernel(*refs, far):
    lines, out = refs[:far], refs[-1]
    nodes = out.shape[1]
    rows = min(line.shape[1] for line in lines)
    for index in range(out.shape[0]):
        for top, size in ((0, rows), (rows, nodes - rows)):
            total = jnp.zeros((size, lanes), jnp.float32)
            for line in lines:
                if top < line.shape[1]:
                    total = total + line[index, pl.ds(top, size), :].astype(jnp.float32)
            out[index, pl.ds(top, size), :] = total.astype(jnp.bfloat16)


def last_kernel(opposite, arrived, pieces, grad, weight_grad, bias_grad, *, factor):
    rows = weight_grad.shape[0]
    tail = pieces.shape[1] - 2 * rows - 16
    lead = grad.shape[0] - tail
    grad[pl.ds(0, lead), :] = sum_rows(arrived, 0, lead)
    late = pieces[opposite[0], pl.ds(2 * rows + 16, tail), :].astype(jnp.float32)
    grad[pl.ds(lead, tail), :] = sum_rows(arrived, lead, tail) + late
    weight_grad[:, pl.ds(0, lanes)] = sum_rows(pieces, 0, rows) * factor
    weight_grad[:, pl.ds(lanes, lanes)] = sum_rows(pieces, rows, rows) * factor
    low, high = sum_bias(pieces, 2 * rows)
    bias_grad[:, pl.ds(0, lanes)] = low * factor
    bias_grad[:, pl.ds(lanes, lanes)] = high * factor


def in_vmem():
    return pl.BlockSpec(memory_space=pltpu.VMEM)


def in_smem():
    return pl.BlockSpec(memory_space=pltpu.SMEM)


def local(features, tile_rows, tile_cols, tile_counts, tile_values, weight, bias, cotangent):
    nodes, width = features.shape
    slots, height, tile_width = tile_values.shape[2:]
    hidden = weight.shape[1]
    far = lax.axis_size("yhi")
    across = lax.axis_size("x")
    near = lax.axis_size("z")
    members = lax.axis_size(team_axes)
    group_rows = lax.axis_size(row_axes)
    here = lax.axis_index("x")
    params = pltpu.CompilerParams(vmem_limit_bytes=vmem_bytes)
    halves = nodes // height
    blocks = members * halves

    def any_place():
        return pl.BlockSpec(memory_space=pl.ANY)

    live = jnp.arange(slots, dtype=jnp.int32) < tile_counts[0, 0]
    columns, rows = tile_cols[0, 0], tile_rows[0, 0]
    owner = jnp.where(live, (columns // near) % across, 255)
    distance = (lax.axis_index("yhi") - columns // (across * near)) % far
    slab = distance * near + columns % near
    block = ((rows // halves) * across + here) * halves + rows % halves
    places = jnp.stack([owner, slab, block])
    ends = jnp.stack([jnp.int32(254), jnp.int32(0), tile_counts[0, 0]])[:, None]
    places = jnp.concatenate([places, ends], axis=1)
    places = jnp.pad(places, ((0, 13), (0, lanes - slots - 1))).astype(jnp.bfloat16)
    own = jnp.concatenate([tile_values[0, 0].reshape(slots * height, tile_width), places], axis=0)

    def ring(size, shift):
        return [(start, (start + shift) % size) for start in range(size)]

    longest_first = sorted(range(1, far), key=lambda shift: -min(shift, far - shift))

    buffers = [own]
    for shift in sorted(range(1, across), key=lambda shift: -min(shift, across - shift)):
        buffers.append(lax.ppermute(own, "x", ring(across, shift)))

    lines = [spread_out(features, "z", near)]
    line_order = [0] + longest_first[::-1]
    for shift in line_order[1:]:
        lines.append(lax.ppermute(lines[0], "yhi", ring(far, shift)))

    codes = pl.pallas_call(
        lambda *refs: codes_kernel(*refs, across=across, top=slots * height),
        out_shape=jax.ShapeDtypeStruct((across, lanes), jnp.int32),
        in_specs=[in_smem()] + [in_vmem()] * across + [any_place()] * (far - 1),
        out_specs=in_vmem(),
        compiler_params=params,
        name="tile_codes",
    )(here.reshape(1), *buffers, *lines[1:])

    scratch_tiles = pltpu.VMEM((across * slots + group, height, tile_width), jnp.bfloat16)
    scratch_list = pltpu.SMEM((across * slots + group,), jnp.int32)
    partial = pl.pallas_call(
        lambda *refs: forward_kernel(
            *refs,
            slots=slots,
            height=height,
            blocks=blocks,
            line_order=line_order,
            across=across,
        ),
        out_shape=jax.ShapeDtypeStruct((members, nodes, width), jnp.bfloat16),
        in_specs=[in_smem()] + [in_vmem()] * (far + across),
        out_specs=in_vmem(),
        scratch_shapes=[
            pltpu.VMEM((far * near, nodes, width), jnp.bfloat16),
            scratch_tiles,
            pltpu.VMEM((blocks + 1, height, width), jnp.float32),
            scratch_list,
        ],
        compiler_params=params,
        name="forward_tiles",
    )(codes, *lines, *buffers)
    partials = lax.all_to_all(partial, team_axes, 0, 0, tiled=True)

    holders = lax.axis_size(share_axes)
    share = width // holders
    hidden_out, message = pl.pallas_call(
        lambda *refs: dense_kernel(*refs, share=share),
        out_shape=(
            jax.ShapeDtypeStruct((nodes, hidden), jnp.bfloat16),
            jax.ShapeDtypeStruct((members, nodes + 2 * share + 16, width), jnp.bfloat16),
        ),
        in_specs=[in_vmem()] * 4,
        out_specs=(in_vmem(), in_vmem()),
        compiler_params=params,
        name="dense_layer",
    )(partials, weight, bias.reshape(1, hidden), cotangent)
    spreads = lax.all_to_all(message, team_axes, 0, 0, tiled=True)

    opposite = far // 2
    outs = pl.pallas_call(
        lambda *refs: backward_kernel(
            *refs,
            slots=slots,
            height=height,
            blocks=blocks,
            nodes=nodes,
            share=share,
            far=far,
            across=across,
        ),
        out_shape=tuple(
            jax.ShapeDtypeStruct(
                (near, nodes - (tail_rows if shift == opposite else 0), width), jnp.bfloat16
            )
            for shift in range(far)
        )
        + (jax.ShapeDtypeStruct((near, 2 * share + 16 + tail_rows, width), jnp.bfloat16),),
        in_specs=[in_smem(), in_vmem()] + [in_vmem()] * across,
        out_specs=(in_vmem(),) * (far + 1),
        scratch_shapes=[
            scratch_tiles,
            pltpu.VMEM((far * near + 1, nodes, width), jnp.float32),
            scratch_list,
        ],
        compiler_params=params,
        name="backward_tiles",
    )(codes, spreads, *buffers)

    lines = [outs[0]]
    for shift in longest_first:
        lines.append(lax.ppermute(outs[shift], "yhi", ring(far, -shift)))

    def gather_gradients(value):
        arrived = lax.all_to_all(value, "z", 0, 0, tiled=True)
        shares, bias_block, tail = pl.pallas_call(
            lambda *refs: share_kernel(*refs, share=share),
            out_shape=(
                jax.ShapeDtypeStruct((holders, 2 * share, lanes), jnp.bfloat16),
                jax.ShapeDtypeStruct((16, lanes), jnp.bfloat16),
                jax.ShapeDtypeStruct((tail_rows, width), jnp.bfloat16),
            ),
            in_specs=[in_vmem()],
            out_specs=(in_vmem(), in_vmem(), in_vmem()),
            compiler_params=params,
            name="share_sum",
        )(arrived)
        shares = lax.all_to_all(shares, share_axes, 0, 0, tiled=True)
        return pl.pallas_call(
            lambda *refs: gather_kernel(*refs, share=share),
            out_shape=jax.ShapeDtypeStruct((2 * width + 16 + tail_rows, lanes), jnp.bfloat16),
            in_specs=[in_vmem()] * 3,
            out_specs=in_vmem(),
            compiler_params=params,
            name="share_gather",
        )(shares, bias_block, tail)

    gradients = lax.cond(
        tile_counts[0, 0] > 0,
        gather_gradients,
        lambda value: jnp.zeros((2 * width + 16 + tail_rows, lanes), jnp.bfloat16),
        outs[far],
    )
    line = pl.pallas_call(
        lambda *refs: middle_kernel(*refs, far=far),
        out_shape=jax.ShapeDtypeStruct((near, nodes, width), jnp.bfloat16),
        in_specs=[in_vmem()] * far + [any_place()],
        out_specs=in_vmem(),
        compiler_params=params,
        name="middle_sums",
    )(*lines, gradients)

    pieces = lax.all_gather(gradients, "yhi", axis=0)
    arrived = lax.all_to_all(line, "z", 0, 0, tiled=True)
    factor = 1.0 / math.sqrt(nodes * group_rows * far * across * near)
    features_grad, weight_grad, bias_grad = pl.pallas_call(
        lambda *refs: last_kernel(*refs, factor=factor),
        out_shape=(
            jax.ShapeDtypeStruct((nodes, width), jnp.float32),
            jax.ShapeDtypeStruct((width, hidden), jnp.float32),
            jax.ShapeDtypeStruct((1, hidden), jnp.float32),
        ),
        in_specs=[in_smem(), in_vmem(), in_vmem()],
        out_specs=(in_vmem(), in_vmem(), in_vmem()),
        compiler_params=params,
        name="last_sums",
    )(((lax.axis_index("yhi") + opposite) % far).reshape(1), arrived, pieces)
    return (hidden_out, features_grad, weight_grad, bias_grad.reshape(hidden))


def solution(mesh):
    fine = Mesh(mesh.devices.reshape(row_split + col_split), axis_names)
    nodes_spec = P(row_axes + col_axes, None)
    in_specs = (
        nodes_spec,
        P(row_axes, col_axes, None),
        P(row_axes, col_axes, None),
        P(row_axes, col_axes),
        P(row_axes, col_axes, None, None, None),
        P(),
        P(),
        nodes_spec,
    )
    out_specs = (nodes_spec, nodes_spec, P(), P())
    return jax.shard_map(local, mesh=fine, in_specs=in_specs, out_specs=out_specs, check_vma=False)
```

```python
import math

import jax
import jax.numpy as jnp
from jax import lax
from jax.experimental import pallas as pl
from jax.experimental.pallas import tpu as pltpu
from jax.sharding import Mesh, PartitionSpec as P

row_split = (2, 2)
col_split = (4, 4, 12)
axis_names = ("ylo", "core", "yhi", "x", "z")
row_axes = ("ylo", "core")
col_axes = ("yhi", "x", "z")
team_axes = ("ylo", "core", "x")
share_axes = ("core", "x")
tail_rows = 16
group = 4
lanes = 128
vmem_bytes = 12 * 1024 * 1024
root_two_over_pi = math.sqrt(2.0 / math.pi)
cubic = 0.044715


def spread_out(value, axes, count):
    copies = jnp.broadcast_to(value[None], (count,) + value.shape)
    return lax.all_to_all(copies, axes, 0, 0, tiled=True)


def codes_kernel(here, *refs, across, top):
    out = refs[-1]
    for source in range(across):
        places = refs[source][pl.ds(top, 16), :].astype(jnp.float32).astype(jnp.int32)
        mine = (places[0:1] == here[0]) | (places[0:1] == 254)
        out[pl.ds(source, 1), :] = jnp.where(mine, places[1:2] * 64 + places[2:3], -1)


def pick_tiles(codes, tile_refs, chosen, picked, slots, height, dummy):
    total = jnp.int32(0)
    for source, tiles in enumerate(tile_refs):

        def body(step, total, source=source, tiles=tiles):
            for sub in range(group):
                slot = step * group + sub
                code = codes[source, slot]
                top = pl.multiple_of(slot * height, height)
                chosen[total] = tiles[pl.ds(top, height), :]
                picked[total] = code
                total = total + jnp.where(code >= 0, 1, 0)
            return total

        total = lax.fori_loop(0, (codes[source, slots] + group - 1) // group, body, total)
    for sub in range(group):
        picked[total + sub] = dummy
    return total


def forward_kernel(codes, *refs, slots, height, blocks, line_order, across):
    far = len(line_order)
    lines, tile_refs = refs[:far], refs[far : far + across]
    out, slabs, chosen, totals, picked = refs[far + across :]
    slab_count = slabs.shape[0]
    near = slab_count // far
    for shift, line in zip(line_order, lines):
        slabs[pl.ds(shift * near, near)] = line[...]
    dummy = slab_count * 64 + blocks
    totals[...] = jnp.zeros_like(totals)
    total = pick_tiles(codes, tile_refs, chosen, picked, slots, height, dummy)

    def body(step, carry):
        products = []
        for sub in range(group):
            code = picked[step * group + sub]
            slab = jnp.minimum(code >> 6, slab_count - 1)
            product = jnp.dot(
                chosen[step * group + sub], slabs[slab], preferred_element_type=jnp.float32
            )
            products.append((code & 63, product))
        for block, product in products:
            totals[block] += product
        return carry

    lax.fori_loop(0, (total + group - 1) // group, body, 0)
    halves = out.shape[1] // height
    for block in range(blocks):
        out[block // halves, pl.ds((block % halves) * height, height), :] = totals[block].astype(
            jnp.bfloat16
        )


def split_wide(value):
    high = value.astype(jnp.bfloat16).astype(jnp.float32)
    return high, value - high


def bias_rows(pieces):
    rows = lax.broadcasted_iota(jnp.int32, (16, lanes), 0)
    block = jnp.zeros((16, lanes), jnp.float32)
    for index, piece in enumerate(pieces):
        block = jnp.where(rows == index, jnp.broadcast_to(piece, (16, lanes)), block)
    return block


def sum_rows(ref, start, size):
    value = ref[0, pl.ds(start, size), :].astype(jnp.float32)
    for index in range(1, ref.shape[0]):
        value = value + ref[index, pl.ds(start, size), :].astype(jnp.float32)
    return value


def dense_kernel(partials, weight, bias, cotangent, hidden, message, *, share):
    members = partials.shape[0]
    nodes = partials.shape[1]
    aggregate = sum_rows(partials, 0, nodes)
    weight_wide = weight[...].astype(jnp.float32)
    pre = (
        jnp.dot(
            aggregate,
            weight_wide,
            precision=lax.Precision.HIGHEST,
            preferred_element_type=jnp.float32,
        )
        + bias[...]
    )
    square = pre * pre
    angle = jnp.tanh(root_two_over_pi * (pre + cubic * (square * pre)))
    gate = 0.5 * (1.0 + angle)
    hidden[...] = (pre * gate).astype(jnp.bfloat16)
    inner = root_two_over_pi * (1.0 + 3.0 * cubic * square)
    gradient = gate + 0.5 * pre * (1.0 - angle * angle) * inner
    slope = (cotangent[...].astype(jnp.float32) * gradient).astype(jnp.bfloat16)
    slope_wide = slope.astype(jnp.float32)
    spread = lax.dot_general(
        slope, weight[...], (((1,), (1,)), ((), ())), preferred_element_type=jnp.float32
    ).astype(jnp.bfloat16)
    weight_part = lax.dot_general(
        aggregate,
        slope_wide,
        (((0,), (0,)), ((), ())),
        precision=lax.Precision.HIGHEST,
        preferred_element_type=jnp.float32,
    )
    bias_part = jnp.sum(slope_wide, axis=0, keepdims=True)
    high, low = split_wide(bias_part)
    bias_block = bias_rows([high[:, :lanes], high[:, lanes:], low[:, :lanes], low[:, lanes:]])
    bias_block = bias_block.astype(jnp.bfloat16)
    for member in range(members):
        message[member, pl.ds(0, nodes), :] = spread
        first = member * share % weight_part.shape[0]
        part = weight_part[first : first + share]
        part = jnp.concatenate([part[:, :lanes], part[:, lanes:]], axis=0)
        message[member, pl.ds(nodes, 2 * share), :] = part.astype(jnp.bfloat16)
        message[member, pl.ds(nodes + 2 * share, 16), :] = bias_block


def sum_bias(ref, start):
    block = sum_rows(ref, start, 16)
    return [block[0:1] + block[2:3], block[1:2] + block[3:4]]


def pack_bias(values):
    parts = [split_wide(value) for value in values]
    return bias_rows([parts[0][0], parts[1][0], parts[0][1], parts[1][1]]).astype(jnp.bfloat16)


def backward_kernel(codes, spreads, *refs, slots, height, blocks, nodes, share, far, across):
    tile_refs, outs = refs[:across], refs[across : across + far]
    shares, chosen, totals, picked = refs[across + far :]
    slab_count = totals.shape[0] - 1
    halves = nodes // height
    dummy = slab_count * 64 + blocks
    totals[...] = jnp.zeros_like(totals)
    total = pick_tiles(codes, tile_refs, chosen, picked, slots, height, dummy)

    def body(step, carry):
        products = []
        for sub in range(group):
            code = picked[step * group + sub]
            block = jnp.minimum(code & 63, blocks - 1)
            top = pl.multiple_of((block % halves) * height, height)
            product = lax.dot_general(
                chosen[step * group + sub],
                spreads[block // halves, pl.ds(top, height), :],
                (((0,), (0,)), ((), ())),
                preferred_element_type=jnp.float32,
            )
            products.append((code >> 6, product))
        for slab, product in products:
            totals[slab] += product
        return carry

    lax.fori_loop(0, (total + group - 1) // group, body, 0)
    near = slab_count // far
    for shift, out in enumerate(outs):
        rows = out.shape[1]
        for index in range(near):
            total = totals[shift * near + index].astype(jnp.bfloat16)
            out[index] = total[:rows]
            if rows < nodes:
                shares[index, pl.ds(2 * share + 16, nodes - rows), :] = total[rows:]
    weight_sum = sum_rows(spreads, nodes, 2 * share).astype(jnp.bfloat16)
    bias_block = pack_bias(sum_bias(spreads, nodes + 2 * share))
    for index in range(near):
        shares[index, pl.ds(0, 2 * share), :] = weight_sum
        shares[index, pl.ds(2 * share, 16), :] = bias_block


def share_kernel(arrived, out, bias_block, tail, *, share):
    total = sum_rows(arrived, 0, 2 * share).astype(jnp.bfloat16)
    for index in range(out.shape[0]):
        out[index] = total
    bias_block[...] = pack_bias(sum_bias(arrived, 2 * share))
    tail[...] = sum_rows(arrived, 2 * share + 16, tail.shape[0]).astype(jnp.bfloat16)


def gather_kernel(shares, bias_block, tail, out, *, share):
    rows = shares.shape[0] * share
    for index in range(shares.shape[0]):
        for half in range(2):
            part = shares[index, pl.ds(half * share, share), :]
            out[pl.ds(half * rows + index * share, share), :] = part
    out[pl.ds(2 * rows, 16), :] = bias_block[...]
    out[pl.ds(2 * rows + 16, tail.shape[0]), :] = tail[...]


def middle_kernel(*refs, far):
    lines, out = refs[:far], refs[-1]
    nodes = out.shape[1]
    rows = min(line.shape[1] for line in lines)
    for index in range(out.shape[0]):
        for top, size in ((0, rows), (rows, nodes - rows)):
            total = jnp.zeros((size, lanes), jnp.float32)
            for line in lines:
                if top < line.shape[1]:
                    total = total + line[index, pl.ds(top, size), :].astype(jnp.float32)
            out[index, pl.ds(top, size), :] = total.astype(jnp.bfloat16)


def last_kernel(opposite, arrived, pieces, grad, weight_grad, bias_grad, *, factor):
    rows = weight_grad.shape[0]
    tail = pieces.shape[1] - 2 * rows - 16
    lead = grad.shape[0] - tail
    grad[pl.ds(0, lead), :] = sum_rows(arrived, 0, lead)
    late = pieces[opposite[0], pl.ds(2 * rows + 16, tail), :].astype(jnp.float32)
    grad[pl.ds(lead, tail), :] = sum_rows(arrived, lead, tail) + late
    weight_grad[:, pl.ds(0, lanes)] = sum_rows(pieces, 0, rows) * factor
    weight_grad[:, pl.ds(lanes, lanes)] = sum_rows(pieces, rows, rows) * factor
    low, high = sum_bias(pieces, 2 * rows)
    bias_grad[:, pl.ds(0, lanes)] = low * factor
    bias_grad[:, pl.ds(lanes, lanes)] = high * factor


def in_vmem():
    return pl.BlockSpec(memory_space=pltpu.VMEM)


def in_smem():
    return pl.BlockSpec(memory_space=pltpu.SMEM)


def local(features, tile_rows, tile_cols, tile_counts, tile_values, weight, bias, cotangent):
    nodes, width = features.shape
    slots, height, tile_width = tile_values.shape[2:]
    hidden = weight.shape[1]
    far = lax.axis_size("yhi")
    across = lax.axis_size("x")
    near = lax.axis_size("z")
    members = lax.axis_size(team_axes)
    group_rows = lax.axis_size(row_axes)
    here = lax.axis_index("x")
    params = pltpu.CompilerParams(vmem_limit_bytes=vmem_bytes)
    halves = nodes // height
    blocks = members * halves

    def any_place():
        return pl.BlockSpec(memory_space=pl.ANY)

    live = jnp.arange(slots, dtype=jnp.int32) < tile_counts[0, 0]
    columns, rows = tile_cols[0, 0], tile_rows[0, 0]
    owner = jnp.where(live, (columns // near) % across, 255)
    distance = (lax.axis_index("yhi") - columns // (across * near)) % far
    slab = distance * near + columns % near
    block = ((rows // halves) * across + here) * halves + rows % halves
    places = jnp.stack([owner, slab, block])
    ends = jnp.stack([jnp.int32(254), jnp.int32(0), tile_counts[0, 0]])[:, None]
    places = jnp.concatenate([places, ends], axis=1)
    places = jnp.pad(places, ((0, 13), (0, lanes - slots - 1))).astype(jnp.bfloat16)
    own = jnp.concatenate([tile_values[0, 0].reshape(slots * height, tile_width), places], axis=0)

    def ring(size, shift):
        return [(start, (start + shift) % size) for start in range(size)]

    longest_first = sorted(range(1, far), key=lambda shift: -min(shift, far - shift))

    buffers = [own]
    for shift in sorted(range(1, across), key=lambda shift: -min(shift, across - shift)):
        buffers.append(lax.ppermute(own, "x", ring(across, shift)))

    lines = [spread_out(features, "z", near)]
    line_order = [0] + longest_first[::-1]
    for shift in line_order[1:]:
        lines.append(lax.ppermute(lines[0], "yhi", ring(far, shift)))

    codes = pl.pallas_call(
        lambda *refs: codes_kernel(*refs, across=across, top=slots * height),
        out_shape=jax.ShapeDtypeStruct((across, lanes), jnp.int32),
        in_specs=[in_smem()] + [in_vmem()] * across,
        out_specs=in_vmem(),
        compiler_params=params,
        name="tile_codes",
    )(here.reshape(1), *buffers)

    scratch_tiles = pltpu.VMEM((across * slots + group, height, tile_width), jnp.bfloat16)
    scratch_list = pltpu.SMEM((across * slots + group,), jnp.int32)
    partial = pl.pallas_call(
        lambda *refs: forward_kernel(
            *refs,
            slots=slots,
            height=height,
            blocks=blocks,
            line_order=line_order,
            across=across,
        ),
        out_shape=jax.ShapeDtypeStruct((members, nodes, width), jnp.bfloat16),
        in_specs=[in_smem()] + [in_vmem()] * (far + across),
        out_specs=in_vmem(),
        scratch_shapes=[
            pltpu.VMEM((far * near, nodes, width), jnp.bfloat16),
            scratch_tiles,
            pltpu.VMEM((blocks + 1, height, width), jnp.float32),
            scratch_list,
        ],
        compiler_params=params,
        name="forward_tiles",
    )(codes, *lines, *buffers)
    partials = lax.all_to_all(partial, team_axes, 0, 0, tiled=True)

    holders = lax.axis_size(share_axes)
    share = width // holders
    hidden_out, message = pl.pallas_call(
        lambda *refs: dense_kernel(*refs, share=share),
        out_shape=(
            jax.ShapeDtypeStruct((nodes, hidden), jnp.bfloat16),
            jax.ShapeDtypeStruct((members, nodes + 2 * share + 16, width), jnp.bfloat16),
        ),
        in_specs=[in_vmem()] * 4,
        out_specs=(in_vmem(), in_vmem()),
        compiler_params=params,
        name="dense_layer",
    )(partials, weight, bias.reshape(1, hidden), cotangent)
    spreads = lax.all_to_all(message, team_axes, 0, 0, tiled=True)

    opposite = far // 2
    outs = pl.pallas_call(
        lambda *refs: backward_kernel(
            *refs,
            slots=slots,
            height=height,
            blocks=blocks,
            nodes=nodes,
            share=share,
            far=far,
            across=across,
        ),
        out_shape=tuple(
            jax.ShapeDtypeStruct(
                (near, nodes - (tail_rows if shift == opposite else 0), width), jnp.bfloat16
            )
            for shift in range(far)
        )
        + (jax.ShapeDtypeStruct((near, 2 * share + 16 + tail_rows, width), jnp.bfloat16),),
        in_specs=[in_smem(), in_vmem()] + [in_vmem()] * across,
        out_specs=(in_vmem(),) * (far + 1),
        scratch_shapes=[
            scratch_tiles,
            pltpu.VMEM((far * near + 1, nodes, width), jnp.float32),
            scratch_list,
        ],
        compiler_params=params,
        name="backward_tiles",
    )(codes, spreads, *buffers)

    lines = [outs[0]]
    for shift in longest_first:
        lines.append(lax.ppermute(outs[shift], "yhi", ring(far, -shift)))

    def gather_gradients(value):
        arrived = lax.all_to_all(value, "z", 0, 0, tiled=True)
        shares, bias_block, tail = pl.pallas_call(
            lambda *refs: share_kernel(*refs, share=share),
            out_shape=(
                jax.ShapeDtypeStruct((holders, 2 * share, lanes), jnp.bfloat16),
                jax.ShapeDtypeStruct((16, lanes), jnp.bfloat16),
                jax.ShapeDtypeStruct((tail_rows, width), jnp.bfloat16),
            ),
            in_specs=[in_vmem()],
            out_specs=(in_vmem(), in_vmem(), in_vmem()),
            compiler_params=params,
            name="share_sum",
        )(arrived)
        shares = lax.all_to_all(shares, share_axes, 0, 0, tiled=True)
        return pl.pallas_call(
            lambda *refs: gather_kernel(*refs, share=share),
            out_shape=jax.ShapeDtypeStruct((2 * width + 16 + tail_rows, lanes), jnp.bfloat16),
            in_specs=[in_vmem()] * 3,
            out_specs=in_vmem(),
            compiler_params=params,
            name="share_gather",
        )(shares, bias_block, tail)

    gradients = lax.cond(
        tile_counts[0, 0] > 0,
        gather_gradients,
        lambda value: jnp.zeros((2 * width + 16 + tail_rows, lanes), jnp.bfloat16),
        outs[far],
    )
    line = pl.pallas_call(
        lambda *refs: middle_kernel(*refs, far=far),
        out_shape=jax.ShapeDtypeStruct((near, nodes, width), jnp.bfloat16),
        in_specs=[in_vmem()] * far + [any_place()],
        out_specs=in_vmem(),
        compiler_params=params,
        name="middle_sums",
    )(*lines, gradients)

    pieces = lax.all_gather(gradients, "yhi", axis=0)
    arrived = lax.all_to_all(line, "z", 0, 0, tiled=True)
    factor = 1.0 / math.sqrt(nodes * group_rows * far * across * near)
    features_grad, weight_grad, bias_grad = pl.pallas_call(
        lambda *refs: last_kernel(*refs, factor=factor),
        out_shape=(
            jax.ShapeDtypeStruct((nodes, width), jnp.float32),
            jax.ShapeDtypeStruct((width, hidden), jnp.float32),
            jax.ShapeDtypeStruct((1, hidden), jnp.float32),
        ),
        in_specs=[in_smem(), in_vmem(), in_vmem()],
        out_specs=(in_vmem(), in_vmem(), in_vmem()),
        compiler_params=params,
        name="last_sums",
    )(((lax.axis_index("yhi") + opposite) % far).reshape(1), arrived, pieces)
    return (hidden_out, features_grad, weight_grad, bias_grad.reshape(hidden))


def solution(mesh):
    fine = Mesh(mesh.devices.reshape(row_split + col_split), axis_names)
    nodes_spec = P(row_axes + col_axes, None)
    in_specs = (
        nodes_spec,
        P(row_axes, col_axes, None),
        P(row_axes, col_axes, None),
        P(row_axes, col_axes),
        P(row_axes, col_axes, None, None, None),
        P(),
        P(),
        nodes_spec,
    )
    out_specs = (nodes_spec, nodes_spec, P(), P())
    return jax.shard_map(local, mesh=fine, in_specs=in_specs, out_specs=out_specs, check_vma=False)
```
